32 devices in a mesh: tensor: 2 (over x), dp: 4 (over z), context: 4 (over y, core).
Axes of the slice: x: 2, y: 2, z: 4, core: 2. Of those that a mesh axis runs over, the one named last changes fastest.
Arguments:
- layer_input: bfloat16 [1024, 4, 2048], P('context', 'dp'), may hold values from -6 to 6
- cotangent: bfloat16 [1024, 4, 2048], P('context', 'dp'), may hold values from -6 to 6
- attn_gain: float32 [2048], replicated, may hold values from 0.1 to 1.9
- query_weight: bfloat16 [2048, 2048], P(None, 'tensor'), may hold values from -0.125 to 0.125
- key_matrix: bfloat16 [2048, 256], P(None, 'tensor'), may hold values from -0.125 to 0.125
- value_matrix: bfloat16 [2048, 256], P(None, 'tensor'), may hold values from -0.125 to 0.125
- output_matrix: bfloat16 [2048, 2048], P('tensor'), may hold values from -3 to 3
- feed_gain: float32 [2048], replicated, may hold values from 0.1 to 1.9
- gate_weight: bfloat16 [2048, 5632], P(None, 'tensor'), may hold values from -0.125 to 0.125
- up_weight: bfloat16 [2048, 5632], P(None, 'tensor'), may hold values from -0.125 to 0.125
- down_weight: bfloat16 [5632, 2048], P('tensor'), may hold values from -0.078125 to 0.078125
Outputs:
- layer_output: bfloat16 [1024, 4, 2048], P('context', 'dp')
- input_grad: bfloat16 [1024, 4, 2048], P('context', 'dp')
- attn_gain_grad: float32 [2048], P(('dp', 'context'))
- query_grad: float32 [2048, 2048], P(('dp', 'context'), 'tensor')
- key_grad: float32 [2048, 256], P(('dp', 'context'), 'tensor')
- value_grad: float32 [2048, 256], P(('dp', 'context'), 'tensor')
- out_grad: float32 [2048, 2048], P('tensor', ('dp', 'context'))
- feed_gain_grad: float32 [2048], P(('dp', 'context'))
- gate_grad: float32 [2048, 5632], P(('dp', 'context'), 'tensor')
- up_grad: float32 [2048, 5632], P(('dp', 'context'), 'tensor')
- down_grad: float32 [5632, 2048], P('tensor', ('dp', 'context'))
The draws below stay inside these ranges and needn't reach their ends.
All inputs are finite; a program needn't handle non-finite values.
Results may differ from the reference program's by a relative error of at most 0.019.
Values may be sent and summed in bfloat16 or wider, within the bound.
No kernel may reach another device: no remote copies, remote signals or barrier semaphores. Data moves between devices by JAX's collectives and lax.ppermute only.
A program may use at most 320 MiB of HBM per device.

```python
import math
import jax
import jax.numpy as jnp
from jax import lax

MODEL_WIDTH = 2048
QUERY_HEADS = 32
KEY_VALUE_HEADS = 4
HEAD_WIDTH = 64
FEED_UNITS = 5632
CTX_TOK = 256
LEN = 1024
SEQS = 4
N_CONTEXT = 4


def with_spikes(array, key, source, target, shards_of, factor):
    def block_of(dim):
        return (jnp.arange(array.shape[dim]) // (array.shape[dim] // shards_of)).reshape((-1,) + (1,) * (array.ndim - 1 - dim))

    near = jax.random.permutation(key, shards_of)[block_of(target)]
    second = (block_of(target) + shards_of // 2) % shards_of
    return jnp.where((block_of(source) == near) | (block_of(source) == second), factor * array, array)


def block_levels(rng, dims, shards, smallest, top_value):
    gain, own = 1.0, jax.random.fold_in(rng, 6)
    for position, blocks in shards:
        steps = jnp.exp(jax.random.uniform(jax.random.fold_in(own, position), (blocks,), jnp.float32, smallest / len(shards), top_value / len(shards)))
        gain = gain * jnp.repeat(steps, dims[position] // blocks).reshape([-1 if axis == position else 1 for axis in range(len(dims))])
    return gain


def noise(own_key, shape, deviation, bound, cuts=(), kind=jnp.bfloat16):
    drawn = deviation * jax.random.normal(own_key, shape, jnp.float32)
    if cuts:
        drawn = drawn * block_levels(own_key, shape, cuts, -0.22, 0.18)
    return jnp.clip(drawn, -bound, bound).astype(kind)


def bell_draw_with(key, shape, width, bound, split, heavy, held_as=jnp.bfloat16):
    values = width * jax.random.normal(key, shape, jnp.float32)
    if split:
        values = values * block_levels(key, shape, split, -0.22, 0.18)
    return jnp.clip(with_spikes(values, jax.random.fold_in(key, 3), *heavy), -bound, bound).astype(held_as)


def setup_inputs(seed: int = 0) -> dict:
    keys = jax.random.split(jax.random.key(seed), 12)
    return {
        "layer_input": bell_draw_with(keys[0], (LEN, SEQS, MODEL_WIDTH), 1.0, 6.0, ((0, 4), (1, 4)), (0, 2, 4, 2.0)),
        "cotangent": bell_draw_with(keys[1], (LEN, SEQS, MODEL_WIDTH), 1.0, 6.0, ((0, 4), (1, 4)), (0, 2, 4, 2.0)),
        "attn_gain": jnp.clip(1.0 + 0.18 * jax.random.normal(keys[2], (MODEL_WIDTH,), jnp.float32), 0.1, 1.9),
        "query_weight": noise(keys[3], (MODEL_WIDTH, QUERY_HEADS * HEAD_WIDTH), MODEL_WIDTH ** -0.5, 0.125, ((1, 2),)),
        "key_matrix": noise(keys[4], (MODEL_WIDTH, KEY_VALUE_HEADS * HEAD_WIDTH), MODEL_WIDTH ** -0.5, 0.125, ((1, 2),)),
        "value_matrix": noise(keys[5], (MODEL_WIDTH, KEY_VALUE_HEADS * HEAD_WIDTH), MODEL_WIDTH ** -0.5, 0.125, ((1, 2),)),
        "output_matrix": noise(keys[6], (QUERY_HEADS * HEAD_WIDTH, MODEL_WIDTH), (max(1, QUERY_HEADS * HEAD_WIDTH * 2 // (CTX_TOK * N_CONTEXT))) ** -0.5, 3.0, ((0, 2),)),
        "feed_gain": jnp.clip(1.0 + 0.18 * jax.random.normal(keys[7], (MODEL_WIDTH,), jnp.float32), 0.1, 1.9),
        "gate_weight": noise(keys[8], (MODEL_WIDTH, FEED_UNITS), MODEL_WIDTH ** -0.5, 0.125, ((1, 2),)),
        "up_weight": noise(keys[9], (MODEL_WIDTH, FEED_UNITS), MODEL_WIDTH ** -0.5, 0.125, ((1, 2),)),
        "down_weight": noise(keys[10], (FEED_UNITS, MODEL_WIDTH), FEED_UNITS ** -0.5, 0.078125, ((0, 2),)),
    }


EPS = 1e-05
ROPE_BASE = 10000.0
NEG_FILL = -1e+30
HIGH = lax.Precision.HIGHEST

def rope_angles(positions, head_size):
    half_size = head_size // 2
    frequencies = jnp.exp(jnp.arange(half_size, dtype=jnp.float32) * (-2.0 * math.log(ROPE_BASE) / head_size))
    return positions.astype(jnp.float32)[:, None] * frequencies[None, :]

def apply_rotary(heads_in, cosine_rows, sine_rows):
    half_size = heads_in.shape[-1] // 2
    first_half = heads_in[..., :half_size]
    second_half = heads_in[..., half_size:]
    return jnp.concatenate([first_half * cosine_rows - second_half * sine_rows, second_half * cosine_rows + first_half * sine_rows], axis=-1)

def inverse_rotary(heads_in, cosine_rows, sine_rows):
    half_size = heads_in.shape[-1] // 2
    first_half = heads_in[..., :half_size]
    second_half = heads_in[..., half_size:]
    return jnp.concatenate([first_half * cosine_rows + second_half * sine_rows, second_half * cosine_rows - first_half * sine_rows], axis=-1)

def rms_scale(values_in):
    return lax.rsqrt(lax.optimization_barrier(jnp.mean(values_in * values_in, axis=-1, keepdims=True)) + EPS)

def norm_backward(d_normed, inputs_f, inv_rms, gain_in):
    scaled = d_normed * gain_in
    return inv_rms * scaled - inputs_f * (inv_rms * inv_rms * inv_rms) * lax.optimization_barrier(jnp.mean(scaled * inputs_f, axis=-1, keepdims=True))

def round_keep(values_in):
    return lax.optimization_barrier(values_in.astype(jnp.bfloat16)).astype(jnp.float32)

def reference(layer_input, cotangent, attn_gain, query_weight, key_matrix, value_matrix, output_matrix, feed_gain, gate_weight, up_weight, down_weight):
    sequence_length = layer_input.shape[0]
    query_groups = QUERY_HEADS // KEY_VALUE_HEADS
    block_rows = min(512, sequence_length)
    block_count = sequence_length // block_rows
    score_scale = 1.0 / math.sqrt(HEAD_WIDTH)
    positions = jnp.arange(sequence_length, dtype=jnp.int32)
    angles = rope_angles(positions, HEAD_WIDTH)
    cosine_rows = jnp.cos(angles)[:, None, :]
    sine_rows = jnp.sin(angles)[:, None, :]
    block_ids = jnp.arange(block_count, dtype=jnp.int32)
    single_float = jnp.float32
    brain_float = jnp.bfloat16

    def per_sequence(totals, pair):
        tokens, upstream = pair
        inputs_f = tokens.astype(single_float)
        attn_rms = rms_scale(inputs_f)
        first_normed = (inputs_f * attn_rms * attn_gain).astype(brain_float)
        query_rows = apply_rotary(jnp.dot(first_normed, query_weight, preferred_element_type=single_float).reshape(sequence_length, QUERY_HEADS, HEAD_WIDTH), cosine_rows, sine_rows).astype(brain_float)
        rotated_keys = apply_rotary(jnp.dot(first_normed, key_matrix, preferred_element_type=single_float).reshape(sequence_length, KEY_VALUE_HEADS, HEAD_WIDTH), cosine_rows, sine_rows).astype(brain_float)
        value_rows = jnp.dot(first_normed, value_matrix, preferred_element_type=single_float).astype(brain_float)
        query_single = query_rows.astype(single_float).reshape(sequence_length, KEY_VALUE_HEADS, query_groups, HEAD_WIDTH)
        key_float = rotated_keys.astype(single_float)
        value_single = value_rows.astype(single_float).reshape(sequence_length, KEY_VALUE_HEADS, HEAD_WIDTH)

        def block_scores(block_index):
            offset = block_index * block_rows
            query_block = lax.dynamic_slice_in_dim(query_single, offset, block_rows, 0)
            scores = jnp.einsum('qngd,knd->qngk', query_block, key_float, precision=HIGH) * score_scale
            query_pos = offset + jnp.arange(block_rows, dtype=jnp.int32)
            allowed = (query_pos[:, None] >= positions[None, :])[:, None, None, :]
            return (query_block, scores, allowed)

        def forward_block(block_index):
            query_block, scores, allowed = block_scores(block_index)
            row_max = lax.optimization_barrier(jnp.max(jnp.where(allowed, scores, NEG_FILL), axis=-1))
            expo = jnp.where(allowed, jnp.exp(scores - row_max[..., None]), 0.0)
            row_total = lax.optimization_barrier(jnp.sum(expo, axis=-1))
            log_block = row_max + jnp.log(row_total)
            weighted = jnp.einsum('qngk,knd->qngd', round_keep(expo), value_single, precision=HIGH)
            return (weighted / row_total[..., None], log_block)
        attention_blocks, block_total = lax.map(forward_block, block_ids)
        attention_float = attention_blocks.reshape(sequence_length, KEY_VALUE_HEADS, query_groups, HEAD_WIDTH)
        logsum_total = block_total.reshape(sequence_length, KEY_VALUE_HEADS, query_groups)
        attn_b = attention_float.reshape(sequence_length, QUERY_HEADS * HEAD_WIDTH).astype(brain_float)
        resid = inputs_f + jnp.dot(attn_b, output_matrix, preferred_element_type=single_float)
        feed_rms = rms_scale(resid)
        normed_two = (resid * feed_rms * feed_gain).astype(brain_float)
        gate_values = jnp.dot(normed_two, gate_weight, preferred_element_type=single_float)
        up_values = jnp.dot(normed_two, up_weight, preferred_element_type=single_float)
        sigmoid_gate = jax.nn.sigmoid(gate_values)
        activated = gate_values * sigmoid_gate
        hidden = (activated * up_values).astype(brain_float)
        output = (resid + jnp.dot(hidden, down_weight, preferred_element_type=single_float)).astype(brain_float)
        d_hidden = jnp.dot(upstream, down_weight.T, preferred_element_type=single_float)
        down_sum = jnp.dot(hidden.T, upstream, preferred_element_type=single_float)
        d_gate = (d_hidden * up_values * (sigmoid_gate * (1.0 + gate_values * (1.0 - sigmoid_gate)))).astype(brain_float)
        d_up = (d_hidden * activated).astype(brain_float)
        gate_sum = jnp.dot(normed_two.T, d_gate, preferred_element_type=single_float)
        up_sum = jnp.dot(normed_two.T, d_up, preferred_element_type=single_float)
        d_normed_two = jnp.dot(d_gate, gate_weight.T, preferred_element_type=single_float) + jnp.dot(d_up, up_weight.T, preferred_element_type=single_float)
        feed_gain_sum = lax.optimization_barrier(jnp.sum(d_normed_two * resid * feed_rms, axis=0))
        d_resid = upstream.astype(single_float) + norm_backward(d_normed_two, resid, feed_rms, feed_gain)
        residual_grad_brain = d_resid.astype(brain_float)
        out_sum = jnp.dot(attn_b.T, residual_grad_brain, preferred_element_type=single_float)
        attention_grad = jnp.dot(residual_grad_brain, output_matrix.T, preferred_element_type=single_float).reshape(sequence_length, KEY_VALUE_HEADS, query_groups, HEAD_WIDTH)
        d_attn_r = round_keep(attention_grad)
        row_delta = lax.optimization_barrier(jnp.sum(attention_grad * attention_float, axis=-1))

        def backward_block(state_in, block_index):
            key_change, value_change = state_in
            query_block, scores, allowed = block_scores(block_index)
            offset = block_index * block_rows
            total_block = lax.dynamic_slice_in_dim(logsum_total, offset, block_rows, 0)
            attn_grad_block = lax.dynamic_slice_in_dim(d_attn_r, offset, block_rows, 0)
            delta_block = lax.dynamic_slice_in_dim(row_delta, offset, block_rows, 0)
            probs = jnp.where(allowed, jnp.exp(scores - total_block[..., None]), 0.0)
            d_probs = jnp.einsum('qngd,knd->qngk', attn_grad_block, value_single, precision=HIGH)
            d_scores = round_keep(probs * (d_probs - delta_block[..., None]) * score_scale)
            query_part = jnp.einsum('qngk,knd->qngd', d_scores, key_float, precision=HIGH)
            key_change = key_change + jnp.einsum('qngk,qngd->knd', d_scores, query_block, precision=HIGH)
            value_change = value_change + jnp.einsum('qngk,qngd->knd', round_keep(probs), attn_grad_block, precision=HIGH)
            return ((key_change, value_change), query_part)
        empty_keys = jnp.zeros((sequence_length, KEY_VALUE_HEADS, HEAD_WIDTH), single_float)
        (key_change, value_change), query_parts = lax.scan(backward_block, (empty_keys, empty_keys), block_ids)
        d_query_b = inverse_rotary(query_parts.reshape(sequence_length, QUERY_HEADS, HEAD_WIDTH), cosine_rows, sine_rows).reshape(sequence_length, QUERY_HEADS * HEAD_WIDTH).astype(brain_float)
        key_grad_brain = inverse_rotary(key_change, cosine_rows, sine_rows).reshape(sequence_length, KEY_VALUE_HEADS * HEAD_WIDTH).astype(brain_float)
        value_grad_brain = value_change.reshape(sequence_length, KEY_VALUE_HEADS * HEAD_WIDTH).astype(brain_float)
        query_sum = jnp.dot(first_normed.T, d_query_b, preferred_element_type=single_float)
        key_sum = jnp.dot(first_normed.T, key_grad_brain, preferred_element_type=single_float)
        value_sum = jnp.dot(first_normed.T, value_grad_brain, preferred_element_type=single_float)
        d_normed_one = jnp.dot(d_query_b, query_weight.T, preferred_element_type=single_float) + jnp.dot(key_grad_brain, key_matrix.T, preferred_element_type=single_float) + jnp.dot(value_grad_brain, value_matrix.T, preferred_element_type=single_float)
        attn_gain_sum = lax.optimization_barrier(jnp.sum(d_normed_one * inputs_f * attn_rms, axis=0))
        input_grad = (d_resid + norm_backward(d_normed_one, inputs_f, attn_rms, attn_gain)).astype(brain_float)
        new_totals = (totals[0] + attn_gain_sum, totals[1] + query_sum, totals[2] + key_sum, totals[3] + value_sum, totals[4] + out_sum, totals[5] + feed_gain_sum, totals[6] + gate_sum, totals[7] + up_sum, totals[8] + down_sum)
        return (new_totals, (output, input_grad))
    initial_state = (jnp.zeros((MODEL_WIDTH,), single_float), jnp.zeros((MODEL_WIDTH, QUERY_HEADS * HEAD_WIDTH), single_float), jnp.zeros((MODEL_WIDTH, KEY_VALUE_HEADS * HEAD_WIDTH), single_float), jnp.zeros((MODEL_WIDTH, KEY_VALUE_HEADS * HEAD_WIDTH), single_float), jnp.zeros((QUERY_HEADS * HEAD_WIDTH, MODEL_WIDTH), single_float), jnp.zeros((MODEL_WIDTH,), single_float), jnp.zeros((MODEL_WIDTH, FEED_UNITS), single_float), jnp.zeros((MODEL_WIDTH, FEED_UNITS), single_float), jnp.zeros((FEED_UNITS, MODEL_WIDTH), single_float))
    totals, (outputs, input_grads) = lax.scan(per_sequence, initial_state, (jnp.moveaxis(layer_input, 1, 0), jnp.moveaxis(cotangent, 1, 0)))
    return (jnp.moveaxis(outputs, 0, 1), jnp.moveaxis(input_grads, 0, 1), totals[0], totals[1], totals[2], totals[3], totals[4], totals[5], totals[6], totals[7], totals[8])
```

```python
import math
from functools import partial

import jax
import jax.numpy as jnp
from jax import lax
from jax.experimental import pallas as pl
from jax.experimental.pallas import tpu as pltpu
from jax.sharding import PartitionSpec as P

HEAD_WIDTH = 64
EPS = 1e-05
ROPE_BASE = 10000.0
NEG_FILL = -1e30
F32 = jnp.float32
BF16 = jnp.bfloat16


def rope_angles(positions, head_size):
    half_size = head_size // 2
    frequencies = jnp.exp(
        jnp.arange(half_size, dtype=jnp.float32) * (-2.0 * math.log(ROPE_BASE) / head_size)
    )
    return positions.astype(jnp.float32)[:, None] * frequencies[None, :]


def apply_rotary(heads_in, cosine_rows, sine_rows):
    half_size = heads_in.shape[-1] // 2
    first_half = heads_in[..., :half_size]
    second_half = heads_in[..., half_size:]
    return jnp.concatenate(
        [
            first_half * cosine_rows - second_half * sine_rows,
            second_half * cosine_rows + first_half * sine_rows,
        ],
        axis=-1,
    )


def inverse_rotary(heads_in, cosine_rows, sine_rows):
    return apply_rotary(heads_in, cosine_rows, -sine_rows)


def rms_scale(values_in):
    return lax.rsqrt(jnp.mean(values_in * values_in, axis=-1, keepdims=True) + EPS)


def norm_backward(d_normed, inputs_f, inv_rms, gain_in):
    scaled = d_normed * gain_in
    return inv_rms * scaled - inputs_f * (inv_rms * inv_rms * inv_rms) * jnp.mean(
        scaled * inputs_f, axis=-1, keepdims=True
    )


def dot_nn(a, b):
    return lax.dot_general(a, b, (((1,), (0,)), ((), ())), preferred_element_type=F32)


def dot_nt(a, b):
    return lax.dot_general(a, b, (((1,), (1,)), ((), ())), preferred_element_type=F32)


def dot_tn(a, b):
    return lax.dot_general(a, b, (((0,), (0,)), ((), ())), preferred_element_type=F32)


def swap(value, axis, flip):
    count = lax.axis_size(axis)
    return lax.ppermute(value, axis, [(i, i ^ flip) for i in range(count)])


def sum_pair(part):
    total = part.astype(BF16)
    flip = 1
    while flip < lax.axis_size("tensor"):
        other = swap(total, "tensor", flip)
        total = total.astype(F32) + other.astype(F32)
        flip *= 2
    return total


def gather_context(value):
    pieces = []
    for k in range(lax.axis_size("context")):
        if k == 0:
            pieces.append(value)
        elif k % 2 == 0:
            pieces.append(swap(value, "context", k))
        else:
            pieces.append(swap(pieces[k - 1], "context", 1))
    return pieces


def spread_columns(value):
    dp_count, ctx_count = lax.axis_size("dp"), lax.axis_size("context")
    here = lax.axis_index("context")
    tokens, width = value.shape
    blocks = value.reshape(tokens, dp_count, ctx_count, width // (dp_count * ctx_count))
    pieces = []
    for k in range(ctx_count):
        mine = lax.dynamic_index_in_dim(blocks, here ^ k, 2, keepdims=False)
        mine = mine.reshape(tokens, width // ctx_count)
        pieces.append(mine if k == 0 else swap(mine, "context", k))
    return pieces


def ring_sum(chunk_of):
    count = lax.axis_size("dp")
    here = lax.axis_index("dp")
    ring = [(i, (i + 1) % count) for i in range(count)]
    total = chunk_of((here - 1) % count).astype(BF16)
    for step in range(1, count):
        arrived = lax.ppermute(total, "dp", ring)
        total = arrived.astype(F32) + chunk_of((here - 1 - step) % count).astype(F32)
        if step < count - 1:
            total = total.astype(BF16)
    return total


def scatter_gain(value):
    dp_count, ctx_count = lax.axis_size("dp"), lax.axis_size("context")
    dp_here, ctx_here = lax.axis_index("dp"), lax.axis_index("context")
    blocks = value.reshape(dp_count, ctx_count, -1)
    total = lax.dynamic_index_in_dim(blocks, ctx_here, 1, keepdims=False)
    for k in range(1, ctx_count):
        total = total + swap(
            lax.dynamic_index_in_dim(blocks, ctx_here ^ k, 1, keepdims=False), "context", k
        )
    result = lax.dynamic_index_in_dim(total, dp_here, 0, keepdims=False)
    for k in range(1, dp_count):
        result = result + swap(
            lax.dynamic_index_in_dim(total, dp_here ^ k, 0, keepdims=False), "dp", k
        )
    return result


def grad_kernel(count, left_is_wide, *refs):
    narrow_refs, wide_refs, out_ref = refs[:count], refs[count : 2 * count], refs[-1]
    total = None
    for narrow_ref, wide_ref in zip(narrow_refs, wide_refs):
        if left_is_wide:
            term = dot_tn(wide_ref[...], narrow_ref[...])
        else:
            term = dot_tn(narrow_ref[...], wide_ref[...])
        total = term if total is None else total + term
    out_ref[...] = total.astype(out_ref.dtype)


def pick_block(size, largest):
    for block in range(largest, 0, -128):
        if size % block == 0:
            return block
    return size


def grad_product(narrow, wide, left_is_wide=False):
    count = len(narrow)
    tokens, rows = narrow[0].shape
    columns = wide[0].shape[1]
    block = pick_block(columns, 512)
    narrow_spec = pl.BlockSpec((tokens, rows), lambda j: (0, 0))
    wide_spec = pl.BlockSpec((tokens, block), lambda j: (0, j))
    if left_is_wide:
        out_shape, out_spec = (columns, rows), pl.BlockSpec((block, rows), lambda j: (j, 0))
    else:
        out_shape, out_spec = (rows, columns), pl.BlockSpec((rows, block), lambda j: (0, j))
    return pl.pallas_call(
        partial(grad_kernel, count, left_is_wide),
        grid=(columns // block,),
        in_specs=[narrow_spec] * count + [wide_spec] * count,
        out_specs=out_spec,
        out_shape=jax.ShapeDtypeStruct(out_shape, BF16),
        compiler_params=pltpu.CompilerParams(vmem_limit_bytes=32 * 1024 * 1024),
        cost_estimate=pl.CostEstimate(
            flops=2 * count * tokens * rows * columns,
            bytes_accessed=2 * (count * tokens * (rows + columns) + rows * columns),
            transcendentals=0,
        ),
    )(*narrow, *wide)


def row_share(narrow, wide):
    dp_count = lax.axis_size("dp")
    product = grad_product(narrow, wide)
    chunks = product.reshape(dp_count, product.shape[0] // dp_count, product.shape[1])
    return ring_sum(lambda d: lax.dynamic_index_in_dim(chunks, d, 0, keepdims=False))


def column_share(wide, narrow):
    dp_count = lax.axis_size("dp")
    product = grad_product(narrow, wide, left_is_wide=True)
    chunks = product.reshape(product.shape[0], dp_count, product.shape[1] // dp_count)
    return ring_sum(lambda d: lax.dynamic_index_in_dim(chunks, d, 1, keepdims=False))


def attend_piece(query_rows, query_pos, score_scale, state_in, kv_piece, offset):
    run_max, run_sum, accum = state_in
    key_heads, value_heads = kv_piece
    key_count = key_heads.shape[0]
    scores = (
        jnp.einsum("qngd,knd->qngk", query_rows, key_heads, preferred_element_type=F32)
        * score_scale
    )
    key_pos = offset + jnp.arange(key_count, dtype=jnp.int32)
    allowed = (query_pos[:, None] >= key_pos[None, :])[:, None, None, :]
    new_max = jnp.maximum(run_max, jnp.max(jnp.where(allowed, scores, NEG_FILL), axis=-1))
    factor = jnp.exp(run_max - new_max)
    weights = jnp.where(allowed, jnp.exp(scores - new_max[..., None]), 0.0)
    new_sum = run_sum * factor + jnp.sum(weights, axis=-1)
    new_accum = accum * factor[..., None] + jnp.einsum(
        "qngk,knd->qngd", weights.astype(BF16), value_heads, preferred_element_type=F32
    )
    return (new_max, new_sum, new_accum)


def on_device(
    layer_input,
    cotangent,
    attn_gain,
    query_weight,
    key_matrix,
    value_matrix,
    output_matrix,
    feed_gain,
    gate_weight,
    up_weight,
    down_weight,
):
    block_shape = layer_input.shape
    tok_here = block_shape[0] * block_shape[1]
    width = block_shape[2]
    layer_input = layer_input.reshape(tok_here, width)
    cotangent = cotangent.reshape(tok_here, width)
    head_size = HEAD_WIDTH
    q_local = query_weight.shape[1] // head_size
    kv_local = key_matrix.shape[1] // head_size
    group_size = q_local // kv_local
    score_scale = 1.0 / math.sqrt(head_size)
    ctx_count = lax.axis_size("context")
    first_pos = lax.axis_index("context") * tok_here
    query_pos = first_pos + jnp.arange(tok_here, dtype=jnp.int32)
    last_pos = first_pos + tok_here - 1
    angles = rope_angles(query_pos, head_size)
    cosine_rows = jnp.cos(angles)[:, None, :]
    sine_rows = jnp.sin(angles)[:, None, :]

    cot_cols = spread_columns(cotangent)
    inputs_f = layer_input.astype(F32)
    attn_rms = rms_scale(inputs_f)
    first_normed = (inputs_f * attn_rms * attn_gain).astype(BF16)
    query_rows = apply_rotary(
        dot_nn(first_normed, query_weight).reshape(tok_here, q_local, head_size),
        cosine_rows,
        sine_rows,
    ).astype(BF16)
    query_rows = query_rows.reshape(tok_here, kv_local, group_size, head_size)
    rotated_keys = (
        apply_rotary(
            dot_nn(first_normed, key_matrix).reshape(tok_here, kv_local, head_size),
            cosine_rows,
            sine_rows,
        )
        .astype(BF16)
        .reshape(tok_here, kv_local * head_size)
    )
    value_rows = dot_nn(first_normed, value_matrix).astype(BF16)
    kv_own = jnp.concatenate([rotated_keys, value_rows], axis=-1)
    kv_whole = lax.all_gather(kv_own, "context", axis=0, tiled=True)
    kv_stack = kv_whole.reshape(ctx_count, tok_here, 2, kv_local, head_size)
    first_cols = spread_columns(first_normed)

    stat_shape = (tok_here, kv_local, group_size)
    initial_state = (
        jnp.full(stat_shape, NEG_FILL, F32),
        jnp.zeros(stat_shape, F32),
        jnp.zeros(stat_shape + (head_size,), F32),
    )
    block_ids = jnp.arange(ctx_count, dtype=jnp.int32)

    def scan_piece(state_in, inputs):
        kv_block, block_index = inputs
        offset = block_index * tok_here
        state = lax.cond(
            offset <= last_pos,
            lambda s: attend_piece(
                query_rows, query_pos, score_scale, s, (kv_block[:, 0], kv_block[:, 1]), offset
            ),
            lambda s: s,
            state_in,
        )
        return (state, None)

    (run_max, run_sum, accum), _ = lax.scan(scan_piece, initial_state, (kv_stack, block_ids))
    logsum_total = run_max + jnp.log(run_sum)
    attention_float = accum / run_sum[..., None]
    attn_b = attention_float.reshape(tok_here, q_local * head_size).astype(BF16)
    resid = inputs_f + sum_pair(dot_nn(attn_b, output_matrix))
    feed_rms = rms_scale(resid)
    normed_two = (resid * feed_rms * feed_gain).astype(BF16)
    gate_values = dot_nn(normed_two, gate_weight)
    up_values = dot_nn(normed_two, up_weight)
    sigmoid_gate = jax.nn.sigmoid(gate_values)
    activated = gate_values * sigmoid_gate
    hidden = (activated * up_values).astype(BF16)
    hidden_all = gather_context(hidden)
    down_share = column_share(hidden_all, cot_cols)
    d_hidden = dot_nt(cotangent, down_weight)
    d_gate = (
        d_hidden * up_values * (sigmoid_gate * (1.0 + gate_values * (1.0 - sigmoid_gate)))
    ).astype(BF16)
    d_up = (d_hidden * activated).astype(BF16)
    two_cols = spread_columns(normed_two)
    gate_share = row_share(two_cols, gather_context(d_gate))
    up_share = row_share(two_cols, gather_context(d_up))
    d_normed_two = sum_pair(dot_nt(d_gate, gate_weight) + dot_nt(d_up, up_weight))
    layer_output = (resid + sum_pair(dot_nn(hidden, down_weight))).astype(BF16)
    feed_gain_sum = jnp.sum(d_normed_two * resid * feed_rms, axis=0)
    d_resid = cotangent.astype(F32) + norm_backward(d_normed_two, resid, feed_rms, feed_gain)
    d_resid_b = d_resid.astype(BF16)
    out_share = column_share(gather_context(attn_b), spread_columns(d_resid_b))
    attention_grad = dot_nt(d_resid_b, output_matrix).reshape(
        tok_here, kv_local, group_size, head_size
    )
    d_attn_b = attention_grad.astype(BF16)
    row_delta = jnp.sum(attention_grad * attention_float, axis=-1)

    def back_piece(query_delta, inputs):
        kv_block, block_index = inputs
        key_block, value_block = kv_block[:, 0], kv_block[:, 1]
        offset = block_index * tok_here

        def compute(delta_in):
            scores = (
                jnp.einsum("qngd,knd->qngk", query_rows, key_block, preferred_element_type=F32)
                * score_scale
            )
            key_pos = offset + jnp.arange(tok_here, dtype=jnp.int32)
            allowed = (query_pos[:, None] >= key_pos[None, :])[:, None, None, :]
            probs = jnp.where(allowed, jnp.exp(scores - logsum_total[..., None]), 0.0)
            d_probs = jnp.einsum(
                "qngd,knd->qngk", d_attn_b, value_block, preferred_element_type=F32
            )
            d_scores_b = (probs * (d_probs - row_delta[..., None]) * score_scale).astype(BF16)
            delta_out = delta_in + jnp.einsum(
                "qngk,knd->qngd", d_scores_b, key_block, preferred_element_type=F32
            )
            d_key = jnp.einsum(
                "qngk,qngd->knd", d_scores_b, query_rows, preferred_element_type=F32
            )
            d_value = jnp.einsum(
                "qngk,qngd->knd", probs.astype(BF16), d_attn_b, preferred_element_type=F32
            )
            return (delta_out, d_key, d_value)

        def skip_piece(delta_in):
            zero_block = jnp.zeros(key_block.shape, F32)
            return (delta_in, zero_block, zero_block)

        delta_next, d_key, d_value = lax.cond(offset <= last_pos, compute, skip_piece, query_delta)
        return (delta_next, jnp.concatenate([d_key, d_value], axis=1).astype(BF16))

    zero_query = jnp.zeros((tok_here, kv_local, group_size, head_size), F32)
    query_delta, kv_parts = lax.scan(back_piece, zero_query, (kv_stack, block_ids))
    kv_parts = kv_parts.reshape(ctx_count, tok_here, 2 * kv_local * head_size)
    ctx_here = lax.axis_index("context")
    kv_back = lax.dynamic_index_in_dim(kv_parts, ctx_here, 0, keepdims=False).astype(F32)
    for k in range(1, ctx_count):
        kv_back = kv_back + swap(
            lax.dynamic_index_in_dim(kv_parts, ctx_here ^ k, 0, keepdims=False), "context", k
        ).astype(F32)
    key_local = kv_back[:, : kv_local * head_size].reshape(tok_here, kv_local, head_size)
    d_query_b = (
        inverse_rotary(
            query_delta.reshape(tok_here, q_local, head_size), cosine_rows, sine_rows
        )
        .reshape(tok_here, q_local * head_size)
        .astype(BF16)
    )
    d_key_b = (
        inverse_rotary(key_local, cosine_rows, sine_rows)
        .reshape(tok_here, kv_local * head_size)
        .astype(BF16)
    )
    d_value_b = kv_back[:, kv_local * head_size :].astype(BF16)
    d_qkv = jnp.concatenate([d_query_b, d_key_b, d_value_b], axis=-1)
    qkv_share = row_share(first_cols, gather_context(d_qkv))
    d_normed_one = sum_pair(
        dot_nt(d_query_b, query_weight)
        + dot_nt(d_key_b, key_matrix)
        + dot_nt(d_value_b, value_matrix)
    )
    attn_gain_sum = jnp.sum(d_normed_one * inputs_f * attn_rms, axis=0)
    input_grad = (d_resid + norm_backward(d_normed_one, inputs_f, attn_rms, attn_gain)).astype(BF16)
    q_width, kv_width = q_local * head_size, kv_local * head_size
    return (
        layer_output.reshape(block_shape),
        input_grad.reshape(block_shape),
        scatter_gain(attn_gain_sum),
        qkv_share[:, :q_width],
        qkv_share[:, q_width : q_width + kv_width],
        qkv_share[:, q_width + kv_width :],
        out_share,
        scatter_gain(feed_gain_sum),
        gate_share,
        up_share,
        down_share,
    )


def solution(mesh):
    in_specs = (
        P("context", "dp", None),
        P("context", "dp", None),
        P(),
        P(None, "tensor"),
        P(None, "tensor"),
        P(None, "tensor"),
        P("tensor", None),
        P(),
        P(None, "tensor"),
        P(None, "tensor"),
        P("tensor", None),
    )
    out_specs = (
        P("context", "dp", None),
        P("context", "dp", None),
        P(("dp", "context")),
        P(("dp", "context"), "tensor"),
        P(("dp", "context"), "tensor"),
        P(("dp", "context"), "tensor"),
        P("tensor", ("dp", "context")),
        P(("dp", "context")),
        P(("dp", "context"), "tensor"),
        P(("dp", "context"), "tensor"),
        P("tensor", ("dp", "context")),
    )
    return jax.shard_map(
        on_device, mesh=mesh, in_specs=in_specs, out_specs=out_specs, check_vma=False
    )
```

```python
import math
from functools import partial

import jax
import jax.numpy as jnp
from jax import lax
from jax.experimental import pallas as pl
from jax.experimental.pallas import tpu as pltpu
from jax.sharding import PartitionSpec as P

CONTEXT = ("row", "core")
HEAD_WIDTH = 64
HALF = HEAD_WIDTH // 2
LANES = 128
EPS = 1e-05
ROPE_BASE = 10000.0
NEG_FILL = -1e30
F32 = jnp.float32
BF16 = jnp.bfloat16
MIB = 1024 * 1024
WEIGHT = 3.0


def dot_nn(a, b):
    return lax.dot_general(a, b, (((1,), (0,)), ((), ())), preferred_element_type=F32)


def dot_nt(a, b):
    return lax.dot_general(a, b, (((1,), (1,)), ((), ())), preferred_element_type=F32)


def dot_tn(a, b):
    return lax.dot_general(a, b, (((0,), (0,)), ((), ())), preferred_element_type=F32)


def whole(shape):
    return pl.BlockSpec(shape, lambda *index: (0,) * len(shape))


def shaped(shape, dtype):
    return jax.ShapeDtypeStruct(shape, dtype)


class Chain:
    def __init__(self):
        self.last = []

    def __call__(
        self,
        body,
        out_shape,
        *operands,
        in_specs,
        out_specs,
        grid=(1,),
        scratch=(),
        scalars=0,
        after=(),
        carry=(),
        vmem=40,
        us=1.0,
    ):
        waits = list(carry) + self.last + list(after)
        inputs = scalars + len(in_specs)
        out_shape = list(out_shape) if isinstance(out_shape, (list, tuple)) else [out_shape]
        out_specs = list(out_specs) if isinstance(out_specs, (list, tuple)) else [out_specs]
        outputs, unread = len(out_shape), pl.BlockSpec(memory_space=pl.ANY)

        def stripped(*refs):
            rest = refs[inputs + len(waits) :]
            body(*refs[:inputs], *rest[:outputs], *rest[outputs + len(carry) :])

        outs = pl.pallas_call(
            stripped,
            out_shape=out_shape + [shaped(c.shape, c.dtype) for c in carry],
            grid_spec=pltpu.PrefetchScalarGridSpec(
                num_scalar_prefetch=scalars,
                grid=grid,
                in_specs=list(in_specs) + [unread] * len(waits),
                out_specs=out_specs + [unread] * len(carry),
                scratch_shapes=list(scratch),
            ),
            input_output_aliases={inputs + i: outputs + i for i in range(len(carry))},
            compiler_params=pltpu.CompilerParams(vmem_limit_bytes=vmem * MIB),
            cost_estimate=pl.CostEstimate(
                flops=int(us * WEIGHT * 1.1e9), bytes_accessed=1000, transcendentals=0
            ),
        )(*operands, *waits)
        self.last = [outs[0]]
        return outs[0] if len(outs) == 1 else outs


def swap(value, axis, flip):
    count = lax.axis_size(axis)
    return lax.ppermute(value, axis, [(i, i ^ flip) for i in range(count)])


def exchange_context(pieces):
    return [p if k == 0 else swap(p, CONTEXT, k) for k, p in enumerate(pieces)]


def exchange_chips(pieces):
    return [p if m == 0 else swap(p, CONTEXT, 2 * m) for m, p in enumerate(pieces)]


def gather_chips(value):
    return exchange_chips([value] * (lax.axis_size(CONTEXT) // 2))


def scatter_gains(value):
    dp_count, ctx_count = lax.axis_size("dp"), lax.axis_size(CONTEXT)
    dp_here, ctx_here = lax.axis_index("dp"), lax.axis_index(CONTEXT)
    blocks = value.reshape(value.shape[0], dp_count, ctx_count, -1)
    total = lax.dynamic_index_in_dim(blocks, ctx_here, 2, keepdims=False)
    for k in range(1, ctx_count):
        total = total + swap(
            lax.dynamic_index_in_dim(blocks, ctx_here ^ k, 2, keepdims=False), CONTEXT, k
        )
    result = lax.dynamic_index_in_dim(total, dp_here, 1, keepdims=False)
    for k in range(1, dp_count):
        result = result + swap(
            lax.dynamic_index_in_dim(total, dp_here ^ k, 1, keepdims=False), "dp", k
        )
    return result


def share_shapes(tokens, width):
    dp_count, ctx_count = lax.axis_size("dp"), lax.axis_size(CONTEXT)
    if (width // (dp_count * ctx_count)) % LANES:
        return []
    return [shaped((tokens, 2 * width // ctx_count), BF16)] * (ctx_count // 2)


def write_shares(here, source_ref, share_refs, by_core=False):
    width = source_ref.shape[1]
    dp_count, ctx_count = lax.axis_size("dp"), lax.axis_size(CONTEXT)
    piece = width // (dp_count * ctx_count)
    for m, share_ref in enumerate(share_refs):
        for side in range(2):
            for d in range(dp_count):
                owner = ((here ^ (2 * m)) // 2) * 2 + side if by_core else here ^ (2 * m + side)
                start = pl.multiple_of((d * ctx_count + owner) * piece, LANES)
                to = (side * dp_count + d) * piece
                share_ref[:, to : to + piece] = source_ref[:, pl.ds(start, piece)]


def shares_of(value, written, by_core=False):
    if written:
        return list(written)
    dp_count, ctx_count = lax.axis_size("dp"), lax.axis_size(CONTEXT)
    here = lax.axis_index(CONTEXT)
    tokens, width = value.shape
    blocks = value.reshape(tokens, dp_count, ctx_count, width // (dp_count * ctx_count))
    cuts = [
        lax.dynamic_index_in_dim(
            blocks, (here ^ k) // 2 * 2 + k % 2 if by_core else here ^ k, 2, keepdims=False
        ).reshape(tokens, -1)
        for k in range(ctx_count)
    ]
    return [
        jnp.concatenate(cuts[2 * m : 2 * m + 2], axis=1) for m in range(ctx_count // 2)
    ]


def pick_kernel(here_ref, value_ref, *share_refs):
    write_shares(here_ref[0], value_ref, share_refs)


def pick_shares(chain, here, value, after=()):
    shapes = share_shapes(*value.shape)
    if not shapes:
        return shares_of(value, ())
    return chain(
        pick_kernel,
        shapes,
        here,
        value,
        in_specs=[whole(value.shape)],
        out_specs=[whole(s.shape) for s in shapes],
        scalars=1,
        after=after,
    )


def pick_block(size, largest):
    for block in range(largest, 0, -LANES):
        if size % block == 0:
            return block
    return size


def rows_kernel(count, *refs):
    narrow_refs, wide_refs = refs[:count], refs[count : 2 * count]
    own_ref, other_ref, turned_ref = refs[2 * count :]

    @pl.when(pl.program_id(0) == 0)
    def _():
        for k in range(count):
            turned_ref[k] = narrow_refs[k][...].T

    total = dot_nn(turned_ref[0], wide_refs[0][...])
    for k in range(1, count):
        total += dot_nn(turned_ref[k], wide_refs[k][...])
    half = total.shape[0] // 2
    own_ref[...] = total[:half].astype(BF16)
    other_ref[...] = total[half:].astype(BF16)


def row_products(chain, narrow, wide, after=()):
    dp_count = lax.axis_size("dp")
    count = len(narrow)
    tokens, rows = narrow[0].shape
    columns = wide[0].shape[1]
    block = pick_block(columns, 512)
    out = shaped((rows // 2, columns), BF16)
    own, other = chain(
        partial(rows_kernel, count),
        [out] * 2,
        *narrow,
        *wide,
        grid=(columns // block,),
        in_specs=[whole((tokens, rows))] * count
        + [pl.BlockSpec((tokens, block), lambda j: (0, j))] * count,
        us=5.0,
        out_specs=[pl.BlockSpec((rows // 2, block), lambda j: (0, j))] * 2,
        scratch=[pltpu.VMEM((count, rows, tokens), BF16)],
        after=after,
    )
    shape = (dp_count, rows // (2 * dp_count), columns)
    return own.reshape(shape), swap(other.reshape(shape), CONTEXT, 1)


def scattered_kernel(count, *refs):
    narrow_refs, wide_refs = refs[:count], refs[count : 2 * count]
    out_ref, turned_ref = refs[2 * count :]

    @pl.when(pl.program_id(0) == 0)
    def _():
        for k in range(count):
            turned_ref[k] = narrow_refs[k][...].T

    total = dot_nn(turned_ref[0], wide_refs[0][...])
    for k in range(1, count):
        total += dot_nn(turned_ref[k], wide_refs[k][...])
    total = total.astype(BF16)
    dp_count, cores, piece = out_ref.shape[:3]
    for side in range(cores):
        for d in range(dp_count):
            start = (side * dp_count + d) * piece
            out_ref[d, side] = total[start : start + piece]


def row_scatter(chain, narrow, wide, after=()):
    dp_count = lax.axis_size("dp")
    count = len(narrow)
    tokens, rows = narrow[0].shape
    columns = wide[0].shape[1]
    block = pick_block(columns, 512)
    piece = rows // (2 * dp_count)
    product = chain(
        partial(scattered_kernel, count),
        shaped((dp_count, 2, piece, columns), BF16),
        *narrow,
        *wide,
        grid=(columns // block,),
        in_specs=[whole((tokens, rows))] * count
        + [pl.BlockSpec((tokens, block), lambda j: (0, j))] * count,
        us=5.0,
        out_specs=pl.BlockSpec((dp_count, 2, piece, block), lambda j: (0, 0, 0, j)),
        scratch=[pltpu.VMEM((count, rows, tokens), BF16)],
        after=after,
    )
    return lax.psum_scatter(
        product.reshape(rows, columns), ("dp", "core"), scatter_dimension=0, tiled=True
    )


def dealt_kernel(block, *refs):
    parts, outs = refs[:-2], refs[-2:]
    at = 0
    for ref in parts:
        for j in range(0, ref.shape[1], 2 * block):
            for side, out_ref in enumerate(outs):
                start = j + side * block
                out_ref[:, at : at + block] = ref[:, start : start + block].astype(F32)
            at += block


def columns_kernel(count, *refs):
    narrow_refs, wide_refs = refs[:count], refs[count : 2 * count]
    own_ref, other_ref = refs[2 * count :]
    total = dot_tn(wide_refs[0][...], narrow_refs[0][...])
    for k in range(1, count):
        total += dot_tn(wide_refs[k][...], narrow_refs[k][...])
    total = total.astype(BF16)
    piece = own_ref.shape[2]
    for side, out_ref in enumerate((own_ref, other_ref)):
        for d in range(out_ref.shape[0]):
            start = (side * out_ref.shape[0] + d) * piece
            out_ref[d] = total[:, start : start + piece]


def column_products(chain, wide, narrow, after=()):
    dp_count = lax.axis_size("dp")
    count = len(narrow)
    tokens, columns = narrow[0].shape
    rows = wide[0].shape[1]
    block = pick_block(rows, 512)
    piece = columns // (2 * dp_count)
    own, other = chain(
        partial(columns_kernel, count),
        [shaped((dp_count, rows, piece), BF16)] * 2,
        *narrow,
        *wide,
        grid=(rows // block,),
        in_specs=[whole((tokens, columns))] * count
        + [pl.BlockSpec((tokens, block), lambda j: (0, j))] * count,
        us=3.0,
        out_specs=[pl.BlockSpec((dp_count, block, piece), lambda j: (0, j, 0))] * 2,
        after=after,
    )
    return own, swap(other, CONTEXT, 1)


def ring_kernel(inputs, block, index_ref, *refs):
    total = refs[0][0].astype(F32)
    for ref in refs[1:inputs]:
        total += ref[0].astype(F32)
    outs = refs[inputs:]
    if len(outs) == 1:
        outs[0][0] = total.astype(outs[0].dtype)
        return
    for j in range(total.shape[1] // block):
        at = j // len(outs) * block
        outs[j % len(outs)][0, :, at : at + block] = total[:, j * block : (j + 1) * block]


class Ring:
    def __init__(self, chain, own, other, block=0):
        self.chain, self.products, self.block = chain, (own, other), block
        self.count = lax.axis_size("dp")
        self.done, self.arrived, self.result = 0, None, None

    def step(self):
        self.done += 1
        last = self.done == self.count
        index = (lax.axis_index("dp") - self.done) % self.count
        shape = (1,) + self.products[0].shape[1:]
        chunk = pl.BlockSpec(shape, lambda i, index_ref: (index_ref[0], 0, 0))
        arrived = [] if self.arrived is None else [self.arrived]
        outs = [shaped(shape, F32 if last else BF16)]
        if last and self.block:
            outs = [shaped(shape[:2] + (shape[2] // 2,), F32)] * 2
        total = self.chain(
            partial(ring_kernel, 2 + len(arrived), self.block),
            outs,
            index.astype(jnp.int32).reshape(1),
            *self.products,
            *arrived,
            in_specs=[chunk] * 2 + [whole(shape)] * len(arrived),
            out_specs=[whole(o.shape) for o in outs],
            scalars=1,
        )
        if last:
            self.result = [t[0] for t in (total if self.block else [total])]
        else:
            ring = [(i, (i + 1) % self.count) for i in range(self.count)]
            self.arrived = lax.ppermute(total, "dp", ring)

    @property
    def open(self):
        return self.result is None


def turns(rings):
    for ring in rings:
        if ring.open:
            ring.step()


def finish(rings):
    while any(ring.open for ring in rings):
        turns(rings)


def rotary_tables(tokens):
    frequencies = jnp.exp(
        jnp.arange(HALF, dtype=F32) * (-2.0 * math.log(ROPE_BASE) / HEAD_WIDTH)
    )
    positions = lax.axis_index(CONTEXT) * tokens + jnp.arange(tokens, dtype=jnp.int32)
    angles = positions.astype(F32)[:, None] * frequencies[None, :]
    cosine, sine = jnp.cos(angles), jnp.sin(angles)
    copies = LANES // HEAD_WIDTH
    return (
        jnp.concatenate([cosine, cosine] * copies, axis=1),
        jnp.concatenate([-sine, sine] * copies, axis=1),
    )


def rotate(values, cosine, sine):
    turned = []
    lane = lax.broadcasted_iota(jnp.int32, cosine.shape, 1)
    first = lane % HEAD_WIDTH < HALF
    for start in range(0, values.shape[1], LANES):
        part = values[:, start : start + LANES]
        partner = jnp.where(
            first, pltpu.roll(part, LANES - HALF, 1), pltpu.roll(part, HALF, 1)
        )
        turned.append(part * cosine + partner * sine)
    return turned[0] if len(turned) == 1 else jnp.concatenate(turned, axis=1)


def rms_of(values):
    return lax.rsqrt(jnp.mean(values * values, axis=-1, keepdims=True) + EPS)


def first_norm_kernel(
    x_ref, gain_ref, key_ref, value_ref, cos_ref, sin_ref, normed_ref, kv_ref
):
    x = x_ref[...].astype(F32)
    normed_ref[...] = (x * rms_of(x) * gain_ref[...]).astype(BF16)
    normed = normed_ref[...]
    kv_width = key_ref.shape[1]
    keys = rotate(dot_nn(normed, key_ref[...]), cos_ref[...], sin_ref[...])
    kv_ref[:, :kv_width] = keys.astype(BF16)
    kv_ref[:, kv_width:] = dot_nn(normed, value_ref[...]).astype(BF16)


def query_kernel(normed_ref, weight_ref, cos_ref, sin_ref, out_ref):
    queries = rotate(dot_nn(normed_ref[...], weight_ref[...]), cos_ref[...], sin_ref[...])
    out_ref[...] = (queries.astype(BF16).astype(F32) * (HEAD_WIDTH**-0.5)).astype(BF16)


def write_bias(here, bias_ref, count):
    tokens = bias_ref.shape[1]
    key = lax.broadcasted_iota(jnp.int32, (tokens, tokens), 0)
    query = lax.broadcasted_iota(jnp.int32, (tokens, tokens), 1)
    for k in range(count):
        allowed = (here ^ k) * tokens + key <= here * tokens + query
        bias_ref[k * tokens : (k + 1) * tokens, :] = jnp.where(allowed, 0.0, NEG_FILL)


def attend_kernel(count, kv_heads, group_blocks, here_ref, *refs):
    q_ref, kv_refs, weight_ref = refs[0], refs[1 : 1 + count], refs[1 + count]
    attn_ref, lse_ref, proj_ref, key_ref, turned_ref, bias_ref, total_ref = refs[2 + count :]
    tokens = q_ref.shape[0]
    step = pl.program_id(0)

    @pl.when(step == 0)
    def _():
        write_bias(here_ref[0], bias_ref, count)
        for k in range(count):
            rows = slice(k * tokens, (k + 1) * tokens)
            values_t = kv_refs[k][:, kv_heads * HEAD_WIDTH :].T
            for g in range(kv_heads):
                cut = slice(g * HEAD_WIDTH, (g + 1) * HEAD_WIDTH)
                key_ref[g, rows, :] = kv_refs[k][:, cut]
                turned_ref[g, :, rows] = values_t[cut, :]

    group = step // group_blocks
    keys, values_t = key_ref[group], turned_ref[group]
    heads = q_ref.shape[1] // HEAD_WIDTH
    outs = []
    for h in range(heads):
        query = q_ref[:, h * HEAD_WIDTH : (h + 1) * HEAD_WIDTH]
        scores = dot_nt(keys, query) + bias_ref[...]
        top = jnp.max(scores, axis=0, keepdims=True)
        expo = jnp.exp(scores - top)
        total = jnp.sum(expo, axis=0, keepdims=True)
        outs.append(dot_nn(values_t, expo.astype(BF16)) / total)
        lse_ref[0, h : h + 1, :] = top + jnp.log(total)
    attn_ref[...] = jnp.concatenate(outs, axis=0).T.astype(BF16)
    term = dot_nn(attn_ref[...], weight_ref[...])

    @pl.when(step == 0)
    def _():
        total_ref[...] = term

    @pl.when(step > 0)
    def _():
        total_ref[...] += term

    @pl.when(step == pl.num_programs(0) - 1)
    def _():
        proj_ref[...] = total_ref[...].astype(BF16)


def attend(chain, here, queries, kv_pieces, output_matrix):
    tokens, q_width = queries.shape
    count = len(kv_pieces)
    kv_heads = kv_pieces[0].shape[1] // (2 * HEAD_WIDTH)
    width = output_matrix.shape[1]
    block = 256
    blocks = q_width // block
    return chain(
        partial(attend_kernel, count, kv_heads, blocks // kv_heads),
        [
            shaped((tokens, q_width), BF16),
            shaped((blocks, block // HEAD_WIDTH, tokens), F32),
            shaped((tokens, width), BF16),
        ],
        here, queries, *kv_pieces, output_matrix,
        grid=(blocks,),
        in_specs=[pl.BlockSpec((tokens, block), lambda j, *_: (0, j))]
        + [whole(p.shape) for p in kv_pieces]
        + [pl.BlockSpec((block, width), lambda j, *_: (j, 0))],
        us=14.0,
        out_specs=[
            pl.BlockSpec((tokens, block), lambda j, *_: (0, j)),
            pl.BlockSpec((1, block // HEAD_WIDTH, tokens), lambda j, *_: (j, 0, 0)),
            whole((tokens, width)),
        ],
        scratch=[
            pltpu.VMEM((kv_heads, count * tokens, HEAD_WIDTH), BF16),
            pltpu.VMEM((kv_heads, HEAD_WIDTH, count * tokens), BF16),
            pltpu.VMEM((count * tokens, tokens), F32),
            pltpu.VMEM((tokens, width), F32),
        ],
        scalars=1,
    )


def attend_back_kernel(count, kv_heads, group_blocks, here_ref, *refs):
    q_ref, attn_ref, lse_ref, grad_ref, weight_ref, cos_ref, sin_ref = refs[:7]
    kv_refs, dq_ref = refs[7 : 7 + count], refs[7 + count]
    dkv_refs = refs[8 + count : 8 + 2 * count]
    key_ref, value_ref, turned_ref, bias_ref, dkey_ref, dvalue_ref = refs[8 + 2 * count :]
    tokens = q_ref.shape[0]
    step = pl.program_id(0)

    @pl.when(step == 0)
    def _():
        write_bias(here_ref[0], bias_ref, count)
        dkey_ref[...] = jnp.zeros_like(dkey_ref)
        dvalue_ref[...] = jnp.zeros_like(dvalue_ref)
        for k in range(count):
            rows = slice(k * tokens, (k + 1) * tokens)
            keys_t = kv_refs[k][:, : kv_heads * HEAD_WIDTH].T
            for g in range(kv_heads):
                cut = slice(g * HEAD_WIDTH, (g + 1) * HEAD_WIDTH)
                value_cut = slice((kv_heads + g) * HEAD_WIDTH, (kv_heads + g + 1) * HEAD_WIDTH)
                key_ref[g, rows, :] = kv_refs[k][:, cut]
                value_ref[g, rows, :] = kv_refs[k][:, value_cut]
                turned_ref[g, :, rows] = keys_t[cut, :]

    group = step // group_blocks
    keys, values, keys_t = key_ref[group], value_ref[group], turned_ref[group]
    d_attn = dot_nt(grad_ref[...], weight_ref[...])
    d_attn_b = d_attn.astype(BF16)
    products = (d_attn * attn_ref[...].astype(F32)).T
    heads = q_ref.shape[1] // HEAD_WIDTH
    d_queries, d_key, d_value = [], None, None
    for h in range(heads):
        cut = slice(h * HEAD_WIDTH, (h + 1) * HEAD_WIDTH)
        query, d_out = q_ref[:, cut], d_attn_b[:, cut]
        delta = jnp.sum(products[cut, :], axis=0, keepdims=True)
        probs = jnp.exp(dot_nt(keys, query) + bias_ref[...] - lse_ref[0, h : h + 1, :])
        d_scores = (probs * (dot_nt(values, d_out) - delta)).astype(BF16)
        value_term = dot_nn(probs.astype(BF16), d_out)
        key_term = dot_nn(d_scores, query)
        d_value = value_term if h == 0 else d_value + value_term
        d_key = key_term if h == 0 else d_key + key_term
        d_queries.append(dot_nn(keys_t, d_scores))
    dkey_ref[group] += d_key
    dvalue_ref[group] += d_value
    d_query = jnp.concatenate(d_queries, axis=0).T * (HEAD_WIDTH**-0.5)
    dq_ref[...] = rotate(d_query, cos_ref[...], -sin_ref[...]).astype(BF16)

    @pl.when(step == pl.num_programs(0) - 1)
    def _():
        for k in range(count):
            rows = slice(k * tokens, (k + 1) * tokens)
            for g in range(kv_heads):
                cut = slice(g * HEAD_WIDTH, (g + 1) * HEAD_WIDTH)
                value_cut = slice((kv_heads + g) * HEAD_WIDTH, (kv_heads + g + 1) * HEAD_WIDTH)
                dkv_refs[k][:, cut] = dkey_ref[g, rows, :].astype(BF16)
                dkv_refs[k][:, value_cut] = dvalue_ref[g, rows, :].astype(BF16)


def attend_back(chain, here, queries, attn_b, lse, grad, output_matrix, tables, kv_pieces):
    tokens, q_width = queries.shape
    count = len(kv_pieces)
    kv_heads = kv_pieces[0].shape[1] // (2 * HEAD_WIDTH)
    width = output_matrix.shape[1]
    block = 256
    blocks = q_width // block
    column = pl.BlockSpec((tokens, block), lambda j, *_: (0, j))
    outs = chain(
        partial(attend_back_kernel, count, kv_heads, blocks // kv_heads),
        [shaped((tokens, q_width), BF16)] + [shaped(p.shape, BF16) for p in kv_pieces],
        here, queries, attn_b, lse, grad, output_matrix, *tables, *kv_pieces,
        grid=(blocks,),
        in_specs=[
            column,
            column,
            pl.BlockSpec((1, block // HEAD_WIDTH, tokens), lambda j, *_: (j, 0, 0)),
            whole((tokens, width)),
            pl.BlockSpec((block, width), lambda j, *_: (j, 0)),
            whole(tables[0].shape),
            whole(tables[1].shape),
        ]
        + [whole(p.shape) for p in kv_pieces],
        us=16.0,
        out_specs=[column] + [whole(p.shape) for p in kv_pieces],
        scratch=[
            pltpu.VMEM((kv_heads, count * tokens, HEAD_WIDTH), BF16),
            pltpu.VMEM((kv_heads, count * tokens, HEAD_WIDTH), BF16),
            pltpu.VMEM((kv_heads, HEAD_WIDTH, count * tokens), BF16),
            pltpu.VMEM((count * tokens, tokens), F32),
            pltpu.VMEM((kv_heads, count * tokens, HEAD_WIDTH), F32),
            pltpu.VMEM((kv_heads, count * tokens, HEAD_WIDTH), F32),
        ],
        scalars=1,
    )
    return outs[0], outs[1:]


def kv_total_kernel(count, *refs):
    cos_ref, sin_ref, out_ref = refs[count:]
    total = refs[0][...].astype(F32)
    for k in range(1, count):
        total += refs[k][...].astype(F32)
    half = total.shape[1] // 2
    out_ref[:, :half] = rotate(total[:, :half], cos_ref[...], -sin_ref[...]).astype(BF16)
    out_ref[:, half:] = total[:, half:].astype(BF16)


def second_norm_kernel(
    here_ref, x_ref, own_ref, other_ref, gain_ref, resid_ref, normed_ref, *share_refs
):
    resid = x_ref[...].astype(F32) + (own_ref[...].astype(F32) + other_ref[...].astype(F32))
    resid_ref[...] = resid
    normed_ref[...] = (resid * rms_of(resid) * gain_ref[...]).astype(BF16)
    write_shares(here_ref[0], normed_ref, share_refs, by_core=True)


def feed_kernel(
    normed_ref, cot_ref, gate_ref, up_ref, down_ref, hidden_ref, d_both_ref
):
    gate = dot_nn(normed_ref[...], gate_ref[...])
    up = dot_nn(normed_ref[...], up_ref[...])
    d_hidden = dot_nt(cot_ref[...], down_ref[...])
    sigmoid = jax.nn.sigmoid(gate)
    active = gate * sigmoid
    hidden_ref[...] = (active * up).astype(BF16)
    d_gate = d_hidden * up * (sigmoid * (1.0 + gate * (1.0 - sigmoid)))
    block = hidden_ref.shape[1]
    d_both_ref[:, :block] = d_gate.astype(BF16)
    d_both_ref[:, block:] = (d_hidden * active).astype(BF16)


def feed_part(chain, normed, cotangent, gate_weight, up_weight, down_weight, first, blocks, block, after=()):
    tokens, width = normed.shape
    column = pl.BlockSpec((width, block), lambda j: (0, first + j))
    return chain(
        feed_kernel,
        [shaped((tokens, blocks * block), BF16), shaped((tokens, 2 * blocks * block), BF16)],
        normed, cotangent, gate_weight, up_weight, down_weight,
        grid=(blocks,),
        in_specs=[
            whole((tokens, width)),
            whole((tokens, width)),
            column,
            column,
            pl.BlockSpec((block, width), lambda j: (first + j, 0)),
        ],
        us=10.0,
        out_specs=[
            pl.BlockSpec((tokens, block), lambda j: (0, j)),
            pl.BlockSpec((tokens, 2 * block), lambda j: (0, j)),
        ],
        after=after,
    )


def part_column(refs, block, visit):
    step, first = pl.program_id(0), 0
    for ref in refs:
        blocks = ref.shape[1] // block
        here = (step >= first) & (step < first + blocks)
        offset = pl.multiple_of((step - first) * block, LANES)
        pl.when(here)(partial(visit, ref, pl.ds(offset, block)))
        first += blocks


def feed_back_kernel(started, block, *refs):
    both_ref, gate_ref, up_ref = refs[:3]
    out_ref, total_ref = refs[-2:]

    @pl.when(pl.program_id(0) == 0)
    def _():
        total_ref[...] = refs[3][...] if started else jnp.zeros_like(total_ref)

    both = both_ref[...]
    total_ref[...] += dot_nt(both[:, :block], gate_ref[...]) + dot_nt(both[:, block:], up_ref[...])

    @pl.when(pl.program_id(0) == pl.num_programs(0) - 1)
    def _():
        out_ref[...] = total_ref[...].astype(out_ref.dtype)


def feed_back(chain, d_both, gate_weight, up_weight, first, block, started, dtype, us, **options):
    tokens, width = d_both.shape[0], gate_weight.shape[0]
    column = pl.BlockSpec((width, block), lambda j: (0, first + j))
    return chain(
        partial(feed_back_kernel, len(started), block),
        shaped((tokens, width), dtype),
        d_both,
        gate_weight,
        up_weight,
        *started,
        grid=(d_both.shape[1] // (2 * block),),
        in_specs=[pl.BlockSpec((tokens, 2 * block), lambda j: (0, j)), column, column]
        + [whole((tokens, width))] * len(started),
        us=us,
        out_specs=whole((tokens, width)),
        scratch=[pltpu.VMEM((tokens, width), F32)],
        **options,
    )


def mixed_kernel(parts, block, *refs):
    hidden_refs = refs[:parts]
    weight_ref, out_ref, total_ref = refs[parts:]

    @pl.when(pl.program_id(0) == 0)
    def _():
        total_ref[...] = jnp.zeros_like(total_ref)

    def visit(ref, columns):
        total_ref[...] += dot_nn(ref[:, columns], weight_ref[...])

    part_column(hidden_refs, block, visit)

    @pl.when(pl.program_id(0) == pl.num_programs(0) - 1)
    def _():
        out_ref[...] = total_ref[...].astype(BF16)


def mix(chain, hidden, down_weight, block):
    tokens, width = hidden[0].shape[0], down_weight.shape[1]
    return chain(
        partial(mixed_kernel, len(hidden), block),
        shaped((tokens, width), BF16),
        *hidden, down_weight,
        grid=(down_weight.shape[0] // block,),
        in_specs=[whole(p.shape) for p in hidden]
        + [pl.BlockSpec((block, width), lambda j: (j, 0))],
        us=8.0,
        out_specs=whole((tokens, width)),
        scratch=[pltpu.VMEM((tokens, width), F32)],
    )


def norm_back(d_normed, inputs, gain):
    scale = rms_of(inputs)
    scaled = d_normed * gain
    back = scale * scaled - inputs * (scale * scale * scale) * jnp.mean(
        scaled * inputs, axis=-1, keepdims=True
    )
    return back, jnp.sum(d_normed * inputs * scale, axis=0, keepdims=True)


def second_back_kernel(
    here_ref,
    cot_ref,
    own_ref,
    other_ref,
    resid_ref,
    gain_ref,
    d_resid_ref,
    rounded_ref,
    gain_grad_ref,
    *share_refs,
):
    d_normed = own_ref[...].astype(F32) + other_ref[...].astype(F32)
    back, gain_grad_ref[...] = norm_back(d_normed, resid_ref[...], gain_ref[...])
    d_resid = cot_ref[...].astype(F32) + back
    d_resid_ref[...] = d_resid
    rounded_ref[...] = d_resid.astype(BF16)
    write_shares(here_ref[0], rounded_ref, share_refs)


def first_back_kernel(dq_ref, dkv_ref, query_ref, key_ref, value_ref, out_ref):
    half = key_ref.shape[1]
    out_ref[...] = (
        dot_nt(dq_ref[...], query_ref[...])
        + dot_nt(dkv_ref[:, :half], key_ref[...])
        + dot_nt(dkv_ref[:, half:], value_ref[...])
    ).astype(BF16)


def output_kernel(resid_ref, own_ref, other_ref, out_ref):
    mixed = own_ref[...].astype(F32) + other_ref[...].astype(F32)
    out_ref[...] = (resid_ref[...] + mixed).astype(BF16)


def last_kernel(own_ref, other_ref, x_ref, gain_ref, d_resid_ref, out_ref, gain_grad_ref):
    d_normed = own_ref[...].astype(F32) + other_ref[...].astype(F32)
    back, gain_grad_ref[...] = norm_back(d_normed, x_ref[...].astype(F32), gain_ref[...])
    out_ref[...] = (d_resid_ref[...] + back).astype(BF16)


def on_device(
    layer_input,
    cotangent,
    attn_gain,
    query_weight,
    key_matrix,
    value_matrix,
    output_matrix,
    feed_gain,
    gate_weight,
    up_weight,
    down_weight,
):
    block_shape = layer_input.shape
    tokens = block_shape[0] * block_shape[1]
    width = block_shape[2]
    x = layer_input.reshape(tokens, width)
    cot = cotangent.reshape(tokens, width)
    q_width, kv_width = query_weight.shape[1], key_matrix.shape[1]
    feed_width = gate_weight.shape[1]
    here = lax.axis_index(CONTEXT).astype(jnp.int32).reshape(1)
    attn_gain, feed_gain = attn_gain.reshape(1, width), feed_gain.reshape(1, width)
    tables = rotary_tables(tokens)
    flat, gain = (tokens, width), (1, width)
    shares = share_shapes(tokens, width)
    share_specs = [whole(s.shape) for s in shares]
    table = whole(tables[0].shape)

    chain = Chain()
    first_normed, kv_own = chain(
        first_norm_kernel,
        [shaped(flat, BF16), shaped((tokens, 2 * kv_width), BF16)],
        x,
        attn_gain,
        key_matrix,
        value_matrix,
        *tables,
        in_specs=[
            whole(flat),
            whole(gain),
            whole(key_matrix.shape),
            whole(value_matrix.shape),
            table,
            table,
        ],
        us=1.5,
        out_specs=[whole(flat), whole((tokens, 2 * kv_width))],
    )
    kv_pieces = exchange_context([kv_own] * lax.axis_size(CONTEXT))
    queries = chain(
        query_kernel,
        shaped((tokens, q_width), BF16),
        first_normed,
        query_weight,
        *tables,
        grid=(q_width // 256,),
        in_specs=[whole(flat), pl.BlockSpec((width, 256), lambda j: (0, j)), table, table],
        us=3.0,
        out_specs=pl.BlockSpec((tokens, 256), lambda j: (0, j)),
    )
    cot_cols = exchange_chips(pick_shares(chain, here, cot))
    attn_b, lse, attn_proj = attend(chain, here, queries, kv_pieces, output_matrix)
    attn_other = swap(attn_proj, "tensor", 1)
    attn_pieces = gather_chips(attn_b)
    first_shares = pick_shares(chain, here, first_normed, after=cot_cols)

    resid, normed_two, *two_shares = chain(
        second_norm_kernel,
        [shaped(flat, F32), shaped(flat, BF16)] + shares,
        here,
        x,
        attn_proj,
        attn_other,
        feed_gain,
        in_specs=[whole(flat)] * 3 + [whole(gain)],
        us=2.0,
        out_specs=[whole(flat)] * 2 + share_specs,
        scalars=1,
        after=attn_pieces,
    )
    two_cols = exchange_chips(shares_of(normed_two, two_shares, by_core=True))

    block = pick_block(feed_width, 256)
    blocks = feed_width // block
    cut = blocks * 5 // 11
    weights = (gate_weight, up_weight)
    feed = partial(feed_part, chain, normed_two, cot, *weights, down_weight)
    hidden_one, both_one = feed(0, cut, block)
    hidden_one_pieces, both_one_pieces = gather_chips(hidden_one), gather_chips(both_one)
    hidden_two, both_two = feed(cut, blocks - cut, block, after=two_cols)
    down_one = Ring(chain, *column_products(chain, hidden_one_pieces, cot_cols))
    d_two, hidden_two, both_two = feed_back(
        chain,
        both_one,
        *weights,
        0,
        block,
        [],
        F32,
        7.0,
        carry=[hidden_two, both_two],
    )
    hidden_two_pieces = gather_chips(hidden_two)
    down_one.step()
    d_two, both_two = feed_back(
        chain, both_two, *weights, cut, block, [d_two], BF16, 8.0, carry=[both_two]
    )
    both_two_pieces = gather_chips(both_two)
    d_two_other = swap(d_two, "tensor", 1)
    down_one.step()
    both_one_share = row_scatter(chain, two_cols, both_one_pieces)
    down_one.step()
    d_resid, d_resid_b, feed_gain_sum, *resid_shares = chain(
        second_back_kernel,
        [shaped(flat, F32), shaped(flat, BF16), shaped(gain, F32)] + shares,
        here,
        cot,
        d_two,
        d_two_other,
        resid,
        feed_gain,
        in_specs=[whole(flat)] * 4 + [whole(gain)],
        us=4.0,
        out_specs=[whole(flat)] * 2 + [whole(gain)] + share_specs,
        scalars=1,
    )
    down_one.step()
    down_two = Ring(chain, *column_products(chain, hidden_two_pieces, cot_cols))
    d_query, d_kv_parts = attend_back(
        chain, here, queries, attn_b, lse, d_resid_b, output_matrix, tables, kv_pieces
    )
    resid_cols = exchange_chips(shares_of(d_resid_b, resid_shares))
    d_kv_pieces = exchange_context(d_kv_parts)
    query_pieces = gather_chips(d_query)
    down_two.step()
    mixed = mix(chain, [hidden_one, hidden_two], down_weight, block)
    down_two.step()
    both_two_share = row_scatter(chain, two_cols, both_two_pieces)
    d_kv = chain(
        partial(kv_total_kernel, len(d_kv_pieces)),
        shaped((tokens, 2 * kv_width), BF16),
        *d_kv_pieces,
        *tables,
        in_specs=[whole((tokens, 2 * kv_width))] * len(d_kv_pieces) + [table] * 2,
        out_specs=whole((tokens, 2 * kv_width)),
    )
    row_block = pick_block(width, 512)
    d_one = chain(
        first_back_kernel,
        shaped(flat, BF16),
        d_query,
        d_kv,
        query_weight,
        key_matrix,
        value_matrix,
        grid=(width // row_block,),
        in_specs=[
            whole((tokens, q_width)),
            whole((tokens, 2 * kv_width)),
            pl.BlockSpec((row_block, q_width), lambda j: (j, 0)),
            pl.BlockSpec((row_block, kv_width), lambda j: (j, 0)),
            pl.BlockSpec((row_block, kv_width), lambda j: (j, 0)),
        ],
        us=2.5,
        out_specs=pl.BlockSpec((tokens, row_block), lambda j: (0, j)),
    )
    d_one_other = swap(d_one, "tensor", 1)
    kv_grad_pieces = gather_chips(d_kv)
    first_cols = exchange_chips(first_shares)
    down_two.step()
    out_ring = Ring(chain, *column_products(chain, attn_pieces, resid_cols))
    down_two.step()
    out_ring.step()
    query_ring = Ring(chain, *row_products(chain, first_cols, query_pieces))
    out_ring.step()
    query_ring.step()
    kv_ring = Ring(chain, *row_products(chain, first_cols, kv_grad_pieces))
    input_grad, attn_gain_sum = chain(
        last_kernel,
        [shaped(flat, BF16), shaped(gain, F32)],
        d_one,
        d_one_other,
        x,
        attn_gain,
        d_resid,
        in_specs=[whole(flat)] * 3 + [whole(gain), whole(flat)],
        us=3.0,
        out_specs=[whole(flat), whole(gain)],
    )
    mixed_other = swap(mixed, "tensor", 1)
    gains = scatter_gains(jnp.concatenate([attn_gain_sum, feed_gain_sum], axis=0))
    kv_ring.step()
    out_ring.step()
    query_ring.step()
    kv_ring.step()
    out_ring.step()
    query_ring.step()
    kv_ring.step()
    layer_output = chain(
        output_kernel,
        shaped(flat, BF16),
        resid,
        mixed,
        mixed_other,
        in_specs=[whole(flat)] * 3,
        us=2.0,
        out_specs=whole(flat),
    )
    finish([down_one, down_two, out_ring, query_ring, kv_ring])
    both = [both_one_share, both_two_share]
    share = both[0].shape[0]
    gate_share, up_share = chain(
        partial(dealt_kernel, block),
        [shaped((share, feed_width), F32)] * 2,
        *both,
        in_specs=[whole(b.shape) for b in both],
        out_specs=[whole((share, feed_width))] * 2,
    )

    return (
        layer_output.reshape(block_shape),
        input_grad.reshape(block_shape),
        gains[0],
        query_ring.result[0],
        kv_ring.result[0][:, :kv_width],
        kv_ring.result[0][:, kv_width:],
        out_ring.result[0],
        gains[1],
        gate_share,
        up_share,
        jnp.concatenate([down_one.result[0], down_two.result[0]], axis=0),
    )


def solution(mesh):
    tensor, dp, context = (mesh.shape[a] for a in ("tensor", "dp", "context"))
    axes = ("tensor", "dp") + CONTEXT
    split = jax.sharding.Mesh(mesh.devices.reshape(tensor, dp, context // 2, 2), axes)
    activation = P(CONTEXT, "dp", None)
    rows, columns = P(None, "tensor"), P("tensor", None)
    vector_share, row_share = P(("dp",) + CONTEXT), P(("dp",) + CONTEXT, "tensor")
    column_share = P("tensor", ("dp",) + CONTEXT)
    in_specs = (activation, activation, P(), rows, rows, rows, columns, P(), rows, rows, columns)
    out_specs = (
        activation,
        activation,
        vector_share,
        row_share,
        row_share,
        row_share,
        column_share,
        vector_share,
        row_share,
        row_share,
        column_share,
    )
    return jax.shard_map(
        on_device, mesh=split, in_specs=in_specs, out_specs=out_specs, check_vma=False
    )
```

```python
import math
from functools import partial

import jax
import jax.numpy as jnp
from jax import lax
from jax.experimental import pallas as pl
from jax.experimental.pallas import tpu as pltpu
from jax.sharding import PartitionSpec as P

CONTEXT = ("row", "core")
HEAD_WIDTH = 64
HALF = HEAD_WIDTH // 2
LANES = 128
EPS = 1e-05
ROPE_BASE = 10000.0
NEG_FILL = -1e30
F32 = jnp.float32
BF16 = jnp.bfloat16
MIB = 1024 * 1024
WEIGHT = 3.0
ORDER = (
    "feed_one", "feed_two", "down_one", "feed_back_one", "D1", "feed_back_two", "D1", "both_one",
    "D1", "middle", "D1", "down_two", "heads_back", "D2", "both_two", "mixing", "D2", "kv_total",
    "first_back", "D2", "out_product", "D2", "O", "query_product", "O", "Q", "kv_product", "last",
    "K", "O", "Q", "K", "O", "Q", "K", "output", "deal", "K", "Q",
)
RINGS = ("D1", "D2", "O", "Q", "K")
HELD = {"h2": ("feed_back_one",), "g2": ("feed_back_one", "feed_back_two")}


def dot_nn(a, b):
    return lax.dot_general(a, b, (((1,), (0,)), ((), ())), preferred_element_type=F32)


def dot_nt(a, b):
    return lax.dot_general(a, b, (((1,), (1,)), ((), ())), preferred_element_type=F32)


def dot_tn(a, b):
    return lax.dot_general(a, b, (((0,), (0,)), ((), ())), preferred_element_type=F32)


def whole(shape):
    return pl.BlockSpec(shape, lambda *index: (0,) * len(shape))


def shaped(shape, dtype):
    return jax.ShapeDtypeStruct(shape, dtype)


class Chain:
    def __init__(self):
        self.last = []

    def __call__(
        self,
        body,
        out_shape,
        *operands,
        in_specs,
        out_specs,
        grid=(1,),
        scratch=(),
        scalars=0,
        after=(),
        carry=(),
        vmem=32,
        us=1.0,
    ):
        waits = list(carry) + self.last + list(after)
        inputs = scalars + len(in_specs)
        out_shape = list(out_shape) if isinstance(out_shape, (list, tuple)) else [out_shape]
        out_specs = list(out_specs) if isinstance(out_specs, (list, tuple)) else [out_specs]
        outputs, unread = len(out_shape), pl.BlockSpec(memory_space=pl.ANY)

        def stripped(*refs):
            rest = refs[inputs + len(waits) :]
            body(*refs[:inputs], *rest[:outputs], *rest[outputs + len(carry) :])

        outs = pl.pallas_call(
            stripped,
            out_shape=out_shape + [shaped(c.shape, c.dtype) for c in carry],
            grid_spec=pltpu.PrefetchScalarGridSpec(
                num_scalar_prefetch=scalars,
                grid=grid,
                in_specs=list(in_specs) + [unread] * len(waits),
                out_specs=out_specs + [unread] * len(carry),
                scratch_shapes=list(scratch),
            ),
            input_output_aliases={inputs + i: outputs + i for i in range(len(carry))},
            compiler_params=pltpu.CompilerParams(vmem_limit_bytes=vmem * MIB),
            cost_estimate=pl.CostEstimate(
                flops=int(us * WEIGHT * 1.1e9), bytes_accessed=1000, transcendentals=0
            ),
        )(*operands, *waits)
        self.last = [outs[0]]
        return outs[0] if len(outs) == 1 else outs


def swap(value, axis, flip):
    count = lax.axis_size(axis)
    return lax.ppermute(value, axis, [(i, i ^ flip) for i in range(count)])


def exchange_context(pieces):
    return [p if k == 0 else swap(p, CONTEXT, k) for k, p in enumerate(pieces)]


def exchange_chips(pieces):
    return [p if m == 0 else swap(p, CONTEXT, 2 * m) for m, p in enumerate(pieces)]


def gather_chips(value):
    return exchange_chips([value] * (lax.axis_size(CONTEXT) // 2))


def scatter_gains(value):
    dp_count, ctx_count = lax.axis_size("dp"), lax.axis_size(CONTEXT)
    dp_here, ctx_here = lax.axis_index("dp"), lax.axis_index(CONTEXT)
    blocks = value.reshape(value.shape[0], dp_count, ctx_count, -1)
    total = lax.dynamic_index_in_dim(blocks, ctx_here, 2, keepdims=False)
    for k in range(1, ctx_count):
        total = total + swap(
            lax.dynamic_index_in_dim(blocks, ctx_here ^ k, 2, keepdims=False), CONTEXT, k
        )
    result = lax.dynamic_index_in_dim(total, dp_here, 1, keepdims=False)
    for k in range(1, dp_count):
        result = result + swap(
            lax.dynamic_index_in_dim(total, dp_here ^ k, 1, keepdims=False), "dp", k
        )
    return result


def share_shapes(tokens, width):
    dp_count, ctx_count = lax.axis_size("dp"), lax.axis_size(CONTEXT)
    if (width // (dp_count * ctx_count)) % LANES:
        return []
    return [shaped((tokens, 2 * width // ctx_count), BF16)] * (ctx_count // 2)


def write_shares(here, source_ref, share_refs, by_core=False):
    width = source_ref.shape[1]
    dp_count, ctx_count = lax.axis_size("dp"), lax.axis_size(CONTEXT)
    piece = width // (dp_count * ctx_count)
    for m, share_ref in enumerate(share_refs):
        for side in range(2):
            for d in range(dp_count):
                owner = ((here ^ (2 * m)) // 2) * 2 + side if by_core else here ^ (2 * m + side)
                start = pl.multiple_of((d * ctx_count + owner) * piece, LANES)
                to = (side * dp_count + d) * piece
                share_ref[:, to : to + piece] = source_ref[:, pl.ds(start, piece)]


def shares_of(value, written, by_core=False):
    if written:
        return list(written)
    dp_count, ctx_count = lax.axis_size("dp"), lax.axis_size(CONTEXT)
    here = lax.axis_index(CONTEXT)
    tokens, width = value.shape
    blocks = value.reshape(tokens, dp_count, ctx_count, width // (dp_count * ctx_count))
    cuts = [
        lax.dynamic_index_in_dim(
            blocks, (here ^ k) // 2 * 2 + k % 2 if by_core else here ^ k, 2, keepdims=False
        ).reshape(tokens, -1)
        for k in range(ctx_count)
    ]
    return [
        jnp.concatenate(cuts[2 * m : 2 * m + 2], axis=1) for m in range(ctx_count // 2)
    ]


def pick_kernel(here_ref, value_ref, *share_refs):
    write_shares(here_ref[0], value_ref, share_refs)


def pick_shares(chain, here, value, after=()):
    shapes = share_shapes(*value.shape)
    if not shapes:
        return shares_of(value, ())
    return chain(
        pick_kernel,
        shapes,
        here,
        value,
        in_specs=[whole(value.shape)],
        out_specs=[whole(s.shape) for s in shapes],
        scalars=1,
        after=after,
    )


def pick_block(size, largest):
    for block in range(largest, 0, -LANES):
        if size % block == 0:
            return block
    return size


def rows_kernel(count, *refs):
    narrow_refs, wide_refs = refs[:count], refs[count : 2 * count]
    own_ref, other_ref, turned_ref = refs[2 * count :]

    @pl.when(pl.program_id(0) == 0)
    def _():
        for k in range(count):
            turned_ref[k] = narrow_refs[k][...].T

    total = dot_nn(turned_ref[0], wide_refs[0][...])
    for k in range(1, count):
        total += dot_nn(turned_ref[k], wide_refs[k][...])
    half = total.shape[0] // 2
    own_ref[...] = total[:half].astype(BF16)
    other_ref[...] = total[half:].astype(BF16)


def row_products(chain, narrow, wide, after=()):
    dp_count = lax.axis_size("dp")
    count = len(narrow)
    tokens, rows = narrow[0].shape
    columns = wide[0].shape[1]
    block = pick_block(columns, 512)
    out = shaped((rows // 2, columns), BF16)
    own, other = chain(
        partial(rows_kernel, count),
        [out] * 2,
        *narrow,
        *wide,
        grid=(columns // block,),
        in_specs=[whole((tokens, rows))] * count
        + [pl.BlockSpec((tokens, block), lambda j: (0, j))] * count,
        us=5.0,
        out_specs=[pl.BlockSpec((rows // 2, block), lambda j: (0, j))] * 2,
        scratch=[pltpu.VMEM((count, rows, tokens), BF16)],
        after=after,
    )
    shape = (dp_count, rows // (2 * dp_count), columns)
    return own.reshape(shape), swap(other.reshape(shape), CONTEXT, 1)


def scattered_kernel(count, *refs):
    narrow_refs, wide_refs = refs[:count], refs[count : 2 * count]
    out_ref, turned_ref = refs[2 * count :]

    @pl.when(pl.program_id(0) == 0)
    def _():
        for k in range(count):
            turned_ref[k] = narrow_refs[k][...].T

    total = dot_nn(turned_ref[0], wide_refs[0][...])
    for k in range(1, count):
        total += dot_nn(turned_ref[k], wide_refs[k][...])
    total = total.astype(BF16)
    dp_count, cores, piece = out_ref.shape[:3]
    for side in range(cores):
        for d in range(dp_count):
            start = (side * dp_count + d) * piece
            out_ref[d, side] = total[start : start + piece]


def row_scatter(chain, narrow, wide, after=()):
    dp_count = lax.axis_size("dp")
    count = len(narrow)
    tokens, rows = narrow[0].shape
    columns = wide[0].shape[1]
    block = pick_block(columns, 512)
    piece = rows // (2 * dp_count)
    product = chain(
        partial(scattered_kernel, count),
        shaped((dp_count, 2, piece, columns), BF16),
        *narrow,
        *wide,
        grid=(columns // block,),
        in_specs=[whole((tokens, rows))] * count
        + [pl.BlockSpec((tokens, block), lambda j: (0, j))] * count,
        us=5.0,
        out_specs=pl.BlockSpec((dp_count, 2, piece, block), lambda j: (0, 0, 0, j)),
        scratch=[pltpu.VMEM((count, rows, tokens), BF16)],
        after=after,
    )
    return lax.psum_scatter(
        product.reshape(rows, columns), ("dp", "core"), scatter_dimension=0, tiled=True
    )


def dealt_kernel(block, *refs):
    parts, outs = refs[:-2], refs[-2:]
    at = 0
    for ref in parts:
        for j in range(0, ref.shape[1], 2 * block):
            for side, out_ref in enumerate(outs):
                start = j + side * block
                out_ref[:, at : at + block] = ref[:, start : start + block].astype(F32)
            at += block


def columns_kernel(count, *refs):
    narrow_refs, wide_refs = refs[:count], refs[count : 2 * count]
    own_ref, other_ref = refs[2 * count :]
    total = dot_tn(wide_refs[0][...], narrow_refs[0][...])
    for k in range(1, count):
        total += dot_tn(wide_refs[k][...], narrow_refs[k][...])
    total = total.astype(BF16)
    piece = own_ref.shape[2]
    for side, out_ref in enumerate((own_ref, other_ref)):
        for d in range(out_ref.shape[0]):
            start = (side * out_ref.shape[0] + d) * piece
            out_ref[d] = total[:, start : start + piece]


def column_products(chain, wide, narrow, after=()):
    dp_count = lax.axis_size("dp")
    count = len(narrow)
    tokens, columns = narrow[0].shape
    rows = wide[0].shape[1]
    block = pick_block(rows, 512)
    piece = columns // (2 * dp_count)
    own, other = chain(
        partial(columns_kernel, count),
        [shaped((dp_count, rows, piece), BF16)] * 2,
        *narrow,
        *wide,
        grid=(rows // block,),
        in_specs=[whole((tokens, columns))] * count
        + [pl.BlockSpec((tokens, block), lambda j: (0, j))] * count,
        us=3.0,
        out_specs=[pl.BlockSpec((dp_count, block, piece), lambda j: (0, j, 0))] * 2,
        after=after,
    )
    return own, swap(other, CONTEXT, 1)


def ring_kernel(inputs, block, index_ref, *refs):
    total = refs[0][0].astype(F32)
    for ref in refs[1:inputs]:
        total += ref[0].astype(F32)
    outs = refs[inputs:]
    if len(outs) == 1:
        outs[0][0] = total.astype(outs[0].dtype)
        return
    for j in range(total.shape[1] // block):
        at = j // len(outs) * block
        outs[j % len(outs)][0, :, at : at + block] = total[:, j * block : (j + 1) * block]


class Ring:
    def __init__(self, chain, own, other, block=0):
        self.chain, self.products, self.block = chain, (own, other), block
        self.count = lax.axis_size("dp")
        self.done, self.arrived, self.result = 0, None, None

    def step(self):
        self.done += 1
        last = self.done == self.count
        index = (lax.axis_index("dp") - self.done) % self.count
        shape = (1,) + self.products[0].shape[1:]
        chunk = pl.BlockSpec(shape, lambda i, index_ref: (index_ref[0], 0, 0))
        arrived = [] if self.arrived is None else [self.arrived]
        outs = [shaped(shape, F32 if last else BF16)]
        if last and self.block:
            outs = [shaped(shape[:2] + (shape[2] // 2,), F32)] * 2
        total = self.chain(
            partial(ring_kernel, 2 + len(arrived), self.block),
            outs,
            index.astype(jnp.int32).reshape(1),
            *self.products,
            *arrived,
            in_specs=[chunk] * 2 + [whole(shape)] * len(arrived),
            out_specs=[whole(o.shape) for o in outs],
            scalars=1,
        )
        if last:
            self.result = [t[0] for t in (total if self.block else [total])]
        else:
            ring = [(i, (i + 1) % self.count) for i in range(self.count)]
            self.arrived = lax.ppermute(total, "dp", ring)

    @property
    def open(self):
        return self.result is None


def turns(rings):
    for ring in rings:
        if ring.open:
            ring.step()


def finish(rings):
    while any(ring.open for ring in rings):
        turns(rings)


def rotary_tables(tokens):
    frequencies = jnp.exp(
        jnp.arange(HALF, dtype=F32) * (-2.0 * math.log(ROPE_BASE) / HEAD_WIDTH)
    )
    positions = lax.axis_index(CONTEXT) * tokens + jnp.arange(tokens, dtype=jnp.int32)
    angles = positions.astype(F32)[:, None] * frequencies[None, :]
    cosine, sine = jnp.cos(angles), jnp.sin(angles)
    copies = LANES // HEAD_WIDTH
    return (
        jnp.concatenate([cosine, cosine] * copies, axis=1),
        jnp.concatenate([-sine, sine] * copies, axis=1),
    )


def rotate(values, cosine, sine):
    turned = []
    lane = lax.broadcasted_iota(jnp.int32, cosine.shape, 1)
    first = lane % HEAD_WIDTH < HALF
    for start in range(0, values.shape[1], LANES):
        part = values[:, start : start + LANES]
        partner = jnp.where(
            first, pltpu.roll(part, LANES - HALF, 1), pltpu.roll(part, HALF, 1)
        )
        turned.append(part * cosine + partner * sine)
    return turned[0] if len(turned) == 1 else jnp.concatenate(turned, axis=1)


def rms_of(values):
    return lax.rsqrt(jnp.mean(values * values, axis=-1, keepdims=True) + EPS)


def first_norm_kernel(
    x_ref, gain_ref, key_ref, value_ref, cos_ref, sin_ref, normed_ref, kv_ref
):
    x = x_ref[...].astype(F32)
    normed_ref[...] = (x * rms_of(x) * gain_ref[...]).astype(BF16)
    normed = normed_ref[...]
    kv_width = key_ref.shape[1]
    keys = rotate(dot_nn(normed, key_ref[...]), cos_ref[...], sin_ref[...])
    kv_ref[:, :kv_width] = keys.astype(BF16)
    kv_ref[:, kv_width:] = dot_nn(normed, value_ref[...]).astype(BF16)


def query_kernel(normed_ref, weight_ref, cos_ref, sin_ref, out_ref):
    queries = rotate(dot_nn(normed_ref[...], weight_ref[...]), cos_ref[...], sin_ref[...])
    out_ref[...] = (queries.astype(BF16).astype(F32) * (HEAD_WIDTH**-0.5)).astype(BF16)


def write_bias(here, bias_ref, count):
    tokens = bias_ref.shape[1]
    key = lax.broadcasted_iota(jnp.int32, (tokens, tokens), 0)
    query = lax.broadcasted_iota(jnp.int32, (tokens, tokens), 1)
    for k in range(count):
        allowed = (here ^ k) * tokens + key <= here * tokens + query
        bias_ref[k * tokens : (k + 1) * tokens, :] = jnp.where(allowed, 0.0, NEG_FILL)


def attend_kernel(count, kv_heads, group_blocks, here_ref, *refs):
    q_ref, kv_refs, weight_ref = refs[0], refs[1 : 1 + count], refs[1 + count]
    attn_ref, lse_ref, proj_ref, key_ref, turned_ref, bias_ref, total_ref = refs[2 + count :]
    tokens = q_ref.shape[0]
    step = pl.program_id(0)

    @pl.when(step == 0)
    def _():
        write_bias(here_ref[0], bias_ref, count)
        for k in range(count):
            rows = slice(k * tokens, (k + 1) * tokens)
            values_t = kv_refs[k][:, kv_heads * HEAD_WIDTH :].T
            for g in range(kv_heads):
                cut = slice(g * HEAD_WIDTH, (g + 1) * HEAD_WIDTH)
                key_ref[g, rows, :] = kv_refs[k][:, cut]
                turned_ref[g, :, rows] = values_t[cut, :]

    group = step // group_blocks
    keys, values_t = key_ref[group], turned_ref[group]
    heads = q_ref.shape[1] // HEAD_WIDTH
    outs = []
    for h in range(heads):
        query = q_ref[:, h * HEAD_WIDTH : (h + 1) * HEAD_WIDTH]
        scores = dot_nt(keys, query) + bias_ref[...]
        top = jnp.max(scores, axis=0, keepdims=True)
        expo = jnp.exp(scores - top)
        total = jnp.sum(expo, axis=0, keepdims=True)
        outs.append(dot_nn(values_t, expo.astype(BF16)) / total)
        lse_ref[0, h : h + 1, :] = top + jnp.log(total)
    attn_ref[...] = jnp.concatenate(outs, axis=0).T.astype(BF16)
    term = dot_nn(attn_ref[...], weight_ref[...])

    @pl.when(step == 0)
    def _():
        total_ref[...] = term

    @pl.when(step > 0)
    def _():
        total_ref[...] += term

    @pl.when(step == pl.num_programs(0) - 1)
    def _():
        proj_ref[...] = total_ref[...].astype(BF16)


def attend(chain, here, queries, kv_pieces, output_matrix):
    tokens, q_width = queries.shape
    count = len(kv_pieces)
    kv_heads = kv_pieces[0].shape[1] // (2 * HEAD_WIDTH)
    width = output_matrix.shape[1]
    block = 256
    blocks = q_width // block
    return chain(
        partial(attend_kernel, count, kv_heads, blocks // kv_heads),
        [
            shaped((tokens, q_width), BF16),
            shaped((blocks, block // HEAD_WIDTH, tokens), F32),
            shaped((tokens, width), BF16),
        ],
        here, queries, *kv_pieces, output_matrix,
        grid=(blocks,),
        in_specs=[pl.BlockSpec((tokens, block), lambda j, *_: (0, j))]
        + [whole(p.shape) for p in kv_pieces]
        + [pl.BlockSpec((block, width), lambda j, *_: (j, 0))],
        us=14.0,
        out_specs=[
            pl.BlockSpec((tokens, block), lambda j, *_: (0, j)),
            pl.BlockSpec((1, block // HEAD_WIDTH, tokens), lambda j, *_: (j, 0, 0)),
            whole((tokens, width)),
        ],
        scratch=[
            pltpu.VMEM((kv_heads, count * tokens, HEAD_WIDTH), BF16),
            pltpu.VMEM((kv_heads, HEAD_WIDTH, count * tokens), BF16),
            pltpu.VMEM((count * tokens, tokens), F32),
            pltpu.VMEM((tokens, width), F32),
        ],
        scalars=1,
    )


def attend_back_kernel(count, kv_heads, group_blocks, here_ref, *refs):
    q_ref, attn_ref, lse_ref, grad_ref, weight_ref, cos_ref, sin_ref = refs[:7]
    kv_refs, dq_ref = refs[7 : 7 + count], refs[7 + count]
    dkv_refs = refs[8 + count : 8 + 2 * count]
    key_ref, value_ref, turned_ref, bias_ref, dkey_ref, dvalue_ref = refs[8 + 2 * count :]
    tokens = q_ref.shape[0]
    step = pl.program_id(0)

    @pl.when(step == 0)
    def _():
        write_bias(here_ref[0], bias_ref, count)
        dkey_ref[...] = jnp.zeros_like(dkey_ref)
        dvalue_ref[...] = jnp.zeros_like(dvalue_ref)
        for k in range(count):
            rows = slice(k * tokens, (k + 1) * tokens)
            keys_t = kv_refs[k][:, : kv_heads * HEAD_WIDTH].T
            for g in range(kv_heads):
                cut = slice(g * HEAD_WIDTH, (g + 1) * HEAD_WIDTH)
                value_cut = slice((kv_heads + g) * HEAD_WIDTH, (kv_heads + g + 1) * HEAD_WIDTH)
                key_ref[g, rows, :] = kv_refs[k][:, cut]
                value_ref[g, rows, :] = kv_refs[k][:, value_cut]
                turned_ref[g, :, rows] = keys_t[cut, :]

    group = step // group_blocks
    keys, values, keys_t = key_ref[group], value_ref[group], turned_ref[group]
    d_attn = dot_nt(grad_ref[...], weight_ref[...])
    d_attn_b = d_attn.astype(BF16)
    products = (d_attn * attn_ref[...].astype(F32)).T
    heads = q_ref.shape[1] // HEAD_WIDTH
    d_queries, d_key, d_value = [], None, None
    for h in range(heads):
        cut = slice(h * HEAD_WIDTH, (h + 1) * HEAD_WIDTH)
        query, d_out = q_ref[:, cut], d_attn_b[:, cut]
        delta = jnp.sum(products[cut, :], axis=0, keepdims=True)
        probs = jnp.exp(dot_nt(keys, query) + bias_ref[...] - lse_ref[0, h : h + 1, :])
        d_scores = (probs * (dot_nt(values, d_out) - delta)).astype(BF16)
        value_term = dot_nn(probs.astype(BF16), d_out)
        key_term = dot_nn(d_scores, query)
        d_value = value_term if h == 0 else d_value + value_term
        d_key = key_term if h == 0 else d_key + key_term
        d_queries.append(dot_nn(keys_t, d_scores))
    dkey_ref[group] += d_key
    dvalue_ref[group] += d_value
    d_query = jnp.concatenate(d_queries, axis=0).T * (HEAD_WIDTH**-0.5)
    dq_ref[...] = rotate(d_query, cos_ref[...], -sin_ref[...]).astype(BF16)

    @pl.when(step == pl.num_programs(0) - 1)
    def _():
        for k in range(count):
            rows = slice(k * tokens, (k + 1) * tokens)
            for g in range(kv_heads):
                cut = slice(g * HEAD_WIDTH, (g + 1) * HEAD_WIDTH)
                value_cut = slice((kv_heads + g) * HEAD_WIDTH, (kv_heads + g + 1) * HEAD_WIDTH)
                dkv_refs[k][:, cut] = dkey_ref[g, rows, :].astype(BF16)
                dkv_refs[k][:, value_cut] = dvalue_ref[g, rows, :].astype(BF16)


def attend_back(chain, here, queries, attn_b, lse, grad, output_matrix, tables, kv_pieces):
    tokens, q_width = queries.shape
    count = len(kv_pieces)
    kv_heads = kv_pieces[0].shape[1] // (2 * HEAD_WIDTH)
    width = output_matrix.shape[1]
    block = 256
    blocks = q_width // block
    column = pl.BlockSpec((tokens, block), lambda j, *_: (0, j))
    outs = chain(
        partial(attend_back_kernel, count, kv_heads, blocks // kv_heads),
        [shaped((tokens, q_width), BF16)] + [shaped(p.shape, BF16) for p in kv_pieces],
        here, queries, attn_b, lse, grad, output_matrix, *tables, *kv_pieces,
        grid=(blocks,),
        in_specs=[
            column,
            column,
            pl.BlockSpec((1, block // HEAD_WIDTH, tokens), lambda j, *_: (j, 0, 0)),
            whole((tokens, width)),
            pl.BlockSpec((block, width), lambda j, *_: (j, 0)),
            whole(tables[0].shape),
            whole(tables[1].shape),
        ]
        + [whole(p.shape) for p in kv_pieces],
        us=16.0,
        out_specs=[column] + [whole(p.shape) for p in kv_pieces],
        scratch=[
            pltpu.VMEM((kv_heads, count * tokens, HEAD_WIDTH), BF16),
            pltpu.VMEM((kv_heads, count * tokens, HEAD_WIDTH), BF16),
            pltpu.VMEM((kv_heads, HEAD_WIDTH, count * tokens), BF16),
            pltpu.VMEM((count * tokens, tokens), F32),
            pltpu.VMEM((kv_heads, count * tokens, HEAD_WIDTH), F32),
            pltpu.VMEM((kv_heads, count * tokens, HEAD_WIDTH), F32),
        ],
        scalars=1,
    )
    return outs[0], outs[1:]


def kv_total_kernel(count, *refs):
    cos_ref, sin_ref, out_ref = refs[count:]
    total = refs[0][...].astype(F32)
    for k in range(1, count):
        total += refs[k][...].astype(F32)
    half = total.shape[1] // 2
    out_ref[:, :half] = rotate(total[:, :half], cos_ref[...], -sin_ref[...]).astype(BF16)
    out_ref[:, half:] = total[:, half:].astype(BF16)


def second_norm_kernel(
    here_ref, x_ref, own_ref, other_ref, gain_ref, resid_ref, normed_ref, *share_refs
):
    resid = x_ref[...].astype(F32) + (own_ref[...].astype(F32) + other_ref[...].astype(F32))
    resid_ref[...] = resid
    normed_ref[...] = (resid * rms_of(resid) * gain_ref[...]).astype(BF16)
    write_shares(here_ref[0], normed_ref, share_refs, by_core=True)


def feed_kernel(
    normed_ref, cot_ref, gate_ref, up_ref, down_ref, hidden_ref, d_both_ref
):
    gate = dot_nn(normed_ref[...], gate_ref[...])
    up = dot_nn(normed_ref[...], up_ref[...])
    d_hidden = dot_nt(cot_ref[...], down_ref[...])
    sigmoid = jax.nn.sigmoid(gate)
    active = gate * sigmoid
    hidden_ref[...] = (active * up).astype(BF16)
    d_gate = d_hidden * up * (sigmoid * (1.0 + gate * (1.0 - sigmoid)))
    block = hidden_ref.shape[1]
    d_both_ref[:, :block] = d_gate.astype(BF16)
    d_both_ref[:, block:] = (d_hidden * active).astype(BF16)


def feed_part(chain, normed, cotangent, gate_weight, up_weight, down_weight, first, blocks, block, after=()):
    tokens, width = normed.shape
    column = pl.BlockSpec((width, block), lambda j: (0, first + j))
    return chain(
        feed_kernel,
        [shaped((tokens, blocks * block), BF16), shaped((tokens, 2 * blocks * block), BF16)],
        normed, cotangent, gate_weight, up_weight, down_weight,
        grid=(blocks,),
        in_specs=[
            whole((tokens, width)),
            whole((tokens, width)),
            column,
            column,
            pl.BlockSpec((block, width), lambda j: (first + j, 0)),
        ],
        us=10.0,
        out_specs=[
            pl.BlockSpec((tokens, block), lambda j: (0, j)),
            pl.BlockSpec((tokens, 2 * block), lambda j: (0, j)),
        ],
        after=after,
    )


def part_column(refs, block, visit):
    step, first = pl.program_id(0), 0
    for ref in refs:
        blocks = ref.shape[1] // block
        here = (step >= first) & (step < first + blocks)
        offset = pl.multiple_of((step - first) * block, LANES)
        pl.when(here)(partial(visit, ref, pl.ds(offset, block)))
        first += blocks


def feed_back_kernel(started, block, *refs):
    both_ref, gate_ref, up_ref = refs[:3]
    out_ref, total_ref = refs[-2:]

    @pl.when(pl.program_id(0) == 0)
    def _():
        total_ref[...] = refs[3][...] if started else jnp.zeros_like(total_ref)

    both = both_ref[...]
    total_ref[...] += dot_nt(both[:, :block], gate_ref[...]) + dot_nt(both[:, block:], up_ref[...])

    @pl.when(pl.program_id(0) == pl.num_programs(0) - 1)
    def _():
        out_ref[...] = total_ref[...].astype(out_ref.dtype)


def feed_back(chain, d_both, gate_weight, up_weight, first, block, started, dtype, us, **options):
    tokens, width = d_both.shape[0], gate_weight.shape[0]
    column = pl.BlockSpec((width, block), lambda j: (0, first + j))
    return chain(
        partial(feed_back_kernel, len(started), block),
        shaped((tokens, width), dtype),
        d_both,
        gate_weight,
        up_weight,
        *started,
        grid=(d_both.shape[1] // (2 * block),),
        in_specs=[pl.BlockSpec((tokens, 2 * block), lambda j: (0, j)), column, column]
        + [whole((tokens, width))] * len(started),
        us=us,
        out_specs=whole((tokens, width)),
        scratch=[pltpu.VMEM((tokens, width), F32)],
        **options,
    )


def mixed_kernel(parts, block, *refs):
    hidden_refs = refs[:parts]
    weight_ref, out_ref, total_ref = refs[parts:]

    @pl.when(pl.program_id(0) == 0)
    def _():
        total_ref[...] = jnp.zeros_like(total_ref)

    def visit(ref, columns):
        total_ref[...] += dot_nn(ref[:, columns], weight_ref[...])

    part_column(hidden_refs, block, visit)

    @pl.when(pl.program_id(0) == pl.num_programs(0) - 1)
    def _():
        out_ref[...] = total_ref[...].astype(BF16)


def mix(chain, hidden, down_weight, block):
    tokens, width = hidden[0].shape[0], down_weight.shape[1]
    return chain(
        partial(mixed_kernel, len(hidden), block),
        shaped((tokens, width), BF16),
        *hidden, down_weight,
        grid=(down_weight.shape[0] // block,),
        in_specs=[whole(p.shape) for p in hidden]
        + [pl.BlockSpec((block, width), lambda j: (j, 0))],
        us=8.0,
        out_specs=whole((tokens, width)),
        scratch=[pltpu.VMEM((tokens, width), F32)],
    )


def norm_back(d_normed, inputs, gain):
    scale = rms_of(inputs)
    scaled = d_normed * gain
    back = scale * scaled - inputs * (scale * scale * scale) * jnp.mean(
        scaled * inputs, axis=-1, keepdims=True
    )
    return back, jnp.sum(d_normed * inputs * scale, axis=0, keepdims=True)


def second_back_kernel(
    here_ref,
    cot_ref,
    own_ref,
    other_ref,
    resid_ref,
    gain_ref,
    d_resid_ref,
    rounded_ref,
    gain_grad_ref,
    *share_refs,
):
    d_normed = own_ref[...].astype(F32) + other_ref[...].astype(F32)
    back, gain_grad_ref[...] = norm_back(d_normed, resid_ref[...], gain_ref[...])
    d_resid = cot_ref[...].astype(F32) + back
    d_resid_ref[...] = d_resid
    rounded_ref[...] = d_resid.astype(BF16)
    write_shares(here_ref[0], rounded_ref, share_refs)


def first_back_kernel(dq_ref, dkv_ref, query_ref, key_ref, value_ref, out_ref):
    half = key_ref.shape[1]
    out_ref[...] = (
        dot_nt(dq_ref[...], query_ref[...])
        + dot_nt(dkv_ref[:, :half], key_ref[...])
        + dot_nt(dkv_ref[:, half:], value_ref[...])
    ).astype(BF16)


def output_kernel(resid_ref, own_ref, other_ref, out_ref):
    mixed = own_ref[...].astype(F32) + other_ref[...].astype(F32)
    out_ref[...] = (resid_ref[...] + mixed).astype(BF16)


def last_kernel(own_ref, other_ref, x_ref, gain_ref, d_resid_ref, out_ref, gain_grad_ref):
    d_normed = own_ref[...].astype(F32) + other_ref[...].astype(F32)
    back, gain_grad_ref[...] = norm_back(d_normed, x_ref[...].astype(F32), gain_ref[...])
    out_ref[...] = (d_resid_ref[...] + back).astype(BF16)


def on_device(
    layer_input,
    cotangent,
    attn_gain,
    query_weight,
    key_matrix,
    value_matrix,
    output_matrix,
    feed_gain,
    gate_weight,
    up_weight,
    down_weight,
):
    block_shape = layer_input.shape
    tokens = block_shape[0] * block_shape[1]
    width = block_shape[2]
    x = layer_input.reshape(tokens, width)
    cot = cotangent.reshape(tokens, width)
    q_width, kv_width = query_weight.shape[1], key_matrix.shape[1]
    feed_width = gate_weight.shape[1]
    here = lax.axis_index(CONTEXT).astype(jnp.int32).reshape(1)
    attn_gain, feed_gain = attn_gain.reshape(1, width), feed_gain.reshape(1, width)
    tables = rotary_tables(tokens)
    flat, gain = (tokens, width), (1, width)
    shares = share_shapes(tokens, width)
    share_specs = [whole(s.shape) for s in shares]
    table = whole(tables[0].shape)

    chain = Chain()
    first_normed, kv_own = chain(
        first_norm_kernel,
        [shaped(flat, BF16), shaped((tokens, 2 * kv_width), BF16)],
        x,
        attn_gain,
        key_matrix,
        value_matrix,
        *tables,
        in_specs=[
            whole(flat),
            whole(gain),
            whole(key_matrix.shape),
            whole(value_matrix.shape),
            table,
            table,
        ],
        us=1.5,
        out_specs=[whole(flat), whole((tokens, 2 * kv_width))],
    )
    kv_pieces = exchange_context([kv_own] * lax.axis_size(CONTEXT))
    queries = chain(
        query_kernel,
        shaped((tokens, q_width), BF16),
        first_normed,
        query_weight,
        *tables,
        grid=(q_width // 256,),
        in_specs=[whole(flat), pl.BlockSpec((width, 256), lambda j: (0, j)), table, table],
        us=3.0,
        out_specs=pl.BlockSpec((tokens, 256), lambda j: (0, j)),
    )
    cot_cols = exchange_chips(pick_shares(chain, here, cot))
    attn_b, lse, attn_proj = attend(chain, here, queries, kv_pieces, output_matrix)
    attn_other = swap(attn_proj, "tensor", 1)
    attn_pieces = gather_chips(attn_b)
    first_shares = pick_shares(chain, here, first_normed, after=cot_cols)

    resid, normed_two, *two_shares = chain(
        second_norm_kernel,
        [shaped(flat, F32), shaped(flat, BF16)] + shares,
        here,
        x,
        attn_proj,
        attn_other,
        feed_gain,
        in_specs=[whole(flat)] * 3 + [whole(gain)],
        us=2.0,
        out_specs=[whole(flat)] * 2 + share_specs,
        scalars=1,
    )
    two_cols = exchange_chips(shares_of(normed_two, two_shares, by_core=True))

    block = pick_block(feed_width, 256)
    blocks = feed_width // block
    cut = blocks * 5 // 11
    weights = (gate_weight, up_weight)
    feed = partial(feed_part, chain, normed_two, cot, *weights, down_weight)
    v = {"h1": None}

    def held(name, kernel):
        return [v[name]] if name in v and kernel in HELD[name] else []

    def feed_one():
        v["h1"], v["g1"] = feed(0, cut, block)
        v["h1s"], v["g1s"] = gather_chips(v["h1"]), gather_chips(v["g1"])

    def feed_two():
        v["h2"], v["g2"] = feed(cut, blocks - cut, block, after=two_cols + attn_pieces)

    def feed_back_one():
        outs = feed_back(
            chain,
            v["g1"],
            *weights,
            0,
            block,
            [],
            F32,
            7.0,
            carry=held("h2", "feed_back_one") + held("g2", "feed_back_one"),
        )
        release(outs, "feed_back_one")

    def feed_back_two():
        outs = feed_back(
            chain,
            v["g2"],
            *weights,
            cut,
            block,
            [v["d_two"]],
            BF16,
            8.0,
            carry=held("h2", "feed_back_two") + held("g2", "feed_back_two"),
        )
        release(outs, "feed_back_two")
        v["d_two_other"] = swap(v["d_two"], "tensor", 1)

    def release(outs, kernel):
        outs = list(outs) if isinstance(outs, (list, tuple)) else [outs]
        v["d_two"] = outs.pop(0)
        for name in ("h2", "g2"):
            if held(name, kernel):
                v[name] = outs.pop(0)

    def pieces(name):
        if name + "s" not in v:
            v[name + "s"] = gather_chips(v[name])
        return v[name + "s"]

    def down_one():
        v["D1"] = Ring(chain, *column_products(chain, pieces("h1"), cot_cols))

    def down_two():
        v["D2"] = Ring(chain, *column_products(chain, pieces("h2"), cot_cols))

    def both_one():
        v["both_one"] = row_scatter(chain, two_cols, pieces("g1"))

    def both_two():
        v["both_two"] = row_scatter(chain, two_cols, pieces("g2"))

    def middle():
        v["d_resid"], v["d_resid_b"], v["feed_gain_sum"], *resid_shares = chain(
            second_back_kernel,
            [shaped(flat, F32), shaped(flat, BF16), shaped(gain, F32)] + shares,
            here,
            cot,
            v["d_two"],
            v["d_two_other"],
            resid,
            feed_gain,
            in_specs=[whole(flat)] * 4 + [whole(gain)],
            us=4.0,
            out_specs=[whole(flat)] * 2 + [whole(gain)] + share_specs,
            scalars=1,
        )
        v["resid_cols"] = exchange_chips(shares_of(v["d_resid_b"], resid_shares))

    def heads_back():
        v["d_query"], d_kv_parts = attend_back(
            chain, here, queries, attn_b, lse, v["d_resid_b"], output_matrix, tables, kv_pieces
        )
        v["d_kv_pieces"] = exchange_context(d_kv_parts)
        v["d_querys"] = gather_chips(v["d_query"])

    def kv_total():
        received = v["d_kv_pieces"]
        v["d_kv"] = chain(
            partial(kv_total_kernel, len(received)),
            shaped((tokens, 2 * kv_width), BF16),
            *received,
            *tables,
            in_specs=[whole((tokens, 2 * kv_width))] * len(received) + [table] * 2,
            out_specs=whole((tokens, 2 * kv_width)),
        )
        v["d_kvs"] = gather_chips(v["d_kv"])

    def first_back():
        row_block = pick_block(width, 512)
        v["d_one"] = chain(
            first_back_kernel,
            shaped(flat, BF16),
            v["d_query"],
            v["d_kv"],
            query_weight,
            key_matrix,
            value_matrix,
            grid=(width // row_block,),
            in_specs=[
                whole((tokens, q_width)),
                whole((tokens, 2 * kv_width)),
                pl.BlockSpec((row_block, q_width), lambda j: (j, 0)),
                pl.BlockSpec((row_block, kv_width), lambda j: (j, 0)),
                pl.BlockSpec((row_block, kv_width), lambda j: (j, 0)),
            ],
            us=2.5,
            out_specs=pl.BlockSpec((tokens, row_block), lambda j: (0, j)),
        )
        v["d_one_other"] = swap(v["d_one"], "tensor", 1)

    def first_columns():
        if "first_cols" not in v:
            v["first_cols"] = exchange_chips(first_shares)
        return v["first_cols"]

    def out_product():
        v["O"] = Ring(chain, *column_products(chain, attn_pieces, v["resid_cols"]))

    def query_product():
        v["Q"] = Ring(chain, *row_products(chain, first_columns(), v["d_querys"]))

    def kv_product():
        v["K"] = Ring(chain, *row_products(chain, first_columns(), v["d_kvs"]))

    def mixing():
        v["mixed"] = mix(chain, [v["h1"], v["h2"]], down_weight, block)
        v["mixed_other"] = swap(v["mixed"], "tensor", 1)

    def output():
        v["layer_output"] = chain(
            output_kernel,
            shaped(flat, BF16),
            resid,
            v["mixed"],
            v["mixed_other"],
            in_specs=[whole(flat)] * 3,
            us=2.0,
            out_specs=whole(flat),
        )

    def last():
        v["input_grad"], attn_gain_sum = chain(
            last_kernel,
            [shaped(flat, BF16), shaped(gain, F32)],
            v["d_one"],
            v["d_one_other"],
            x,
            attn_gain,
            v["d_resid"],
            in_specs=[whole(flat)] * 3 + [whole(gain), whole(flat)],
            us=3.0,
            out_specs=[whole(flat), whole(gain)],
        )
        gain_sums = jnp.concatenate([attn_gain_sum, v["feed_gain_sum"]], axis=0)
        v["gains"] = scatter_gains(gain_sums)

    def deal():
        both = [v["both_one"], v["both_two"]]
        share = both[0].shape[0]
        v["gate_share"], v["up_share"] = chain(
            partial(dealt_kernel, block),
            [shaped((share, feed_width), F32)] * 2,
            *both,
            in_specs=[whole(b.shape) for b in both],
            out_specs=[whole((share, feed_width))] * 2,
        )

    tasks = (
        feed_one,
        feed_two,
        feed_back_one,
        feed_back_two,
        down_one,
        down_two,
        both_one,
        both_two,
        middle,
        heads_back,
        kv_total,
        first_back,
        out_product,
        query_product,
        kv_product,
        mixing,
        output,
        last,
        deal,
    )
    by_name = {task.__name__: task for task in tasks}
    for name in ORDER:
        if name in by_name:
            by_name[name]()
        elif v[name].open:
            v[name].step()
    for name in RINGS:
        while v[name].open:
            v[name].step()
    layer_output, input_grad, gains = v["layer_output"], v["input_grad"], v["gains"]
    out_ring, query_ring, kv_ring = v["O"], v["Q"], v["K"]
    gate_share, up_share = v["gate_share"], v["up_share"]
    down_one, down_two = v["D1"], v["D2"]

    return (
        layer_output.reshape(block_shape),
        input_grad.reshape(block_shape),
        gains[0],
        query_ring.result[0],
        kv_ring.result[0][:, :kv_width],
        kv_ring.result[0][:, kv_width:],
        out_ring.result[0],
        gains[1],
        gate_share,
        up_share,
        jnp.concatenate([down_one.result[0], down_two.result[0]], axis=0),
    )


def solution(mesh):
    tensor, dp, context = (mesh.shape[a] for a in ("tensor", "dp", "context"))
    axes = ("tensor", "dp") + CONTEXT
    split = jax.sharding.Mesh(mesh.devices.reshape(tensor, dp, context // 2, 2), axes)
    activation = P(CONTEXT, "dp", None)
    rows, columns = P(None, "tensor"), P("tensor", None)
    vector_share, row_share = P(("dp",) + CONTEXT), P(("dp",) + CONTEXT, "tensor")
    column_share = P("tensor", ("dp",) + CONTEXT)
    in_specs = (activation, activation, P(), rows, rows, rows, columns, P(), rows, rows, columns)
    out_specs = (
        activation,
        activation,
        vector_share,
        row_share,
        row_share,
        row_share,
        column_share,
        vector_share,
        row_share,
        row_share,
        column_share,
    )
    return jax.shard_map(
        on_device, mesh=split, in_specs=in_specs, out_specs=out_specs, check_vma=False
    )
```

```python
import math
from functools import partial

import jax
import jax.numpy as jnp
from jax import lax
from jax.experimental import pallas as pl
from jax.experimental.pallas import tpu as pltpu
from jax.sharding import PartitionSpec as P

CONTEXT = ("row", "core")
HEAD_WIDTH = 64
HALF = HEAD_WIDTH // 2
LANES = 128
EPS = 1e-05
ROPE_BASE = 10000.0
NEG_FILL = -1e30
F32 = jnp.float32
BF16 = jnp.bfloat16
MIB = 1024 * 1024
WEIGHT = 3.0
ORDER = (
    "feed_one", "feed_two", "down_one", "feed_back_one", "D1", "feed_back_two", "D1", "both_one",
    "D1", "middle", "D1", "down_two", "heads_back", "D2", "both_two", "mixing", "D2", "kv_total",
    "first_back", "D2", "out_product", "D2", "O", "query_product", "O", "Q", "kv_product", "last",
    "K", "O", "Q", "K", "O", "Q", "K", "output", "deal", "K", "Q",
)
RINGS = ("D1", "D2", "O", "Q", "K")
HELD = {"h2": ("feed_back_one",), "g2": ("feed_back_one", "feed_back_two")}


def dot_nn(a, b):
    return lax.dot_general(a, b, (((1,), (0,)), ((), ())), preferred_element_type=F32)


def dot_nt(a, b):
    return lax.dot_general(a, b, (((1,), (1,)), ((), ())), preferred_element_type=F32)


def dot_tn(a, b):
    return lax.dot_general(a, b, (((0,), (0,)), ((), ())), preferred_element_type=F32)


def whole(shape):
    return pl.BlockSpec(shape, lambda *index: (0,) * len(shape))


def shaped(shape, dtype):
    return jax.ShapeDtypeStruct(shape, dtype)


class Chain:
    def __init__(self):
        self.last = []

    def __call__(
        self,
        body,
        out_shape,
        *operands,
        in_specs,
        out_specs,
        grid=(1,),
        scratch=(),
        scalars=0,
        after=(),
        carry=(),
        vmem=32,
        us=1.0,
    ):
        waits = list(carry) + self.last + list(after)
        inputs = scalars + len(in_specs)
        out_shape = list(out_shape) if isinstance(out_shape, (list, tuple)) else [out_shape]
        out_specs = list(out_specs) if isinstance(out_specs, (list, tuple)) else [out_specs]
        outputs, unread = len(out_shape), pl.BlockSpec(memory_space=pl.ANY)

        def stripped(*refs):
            rest = refs[inputs + len(waits) :]
            body(*refs[:inputs], *rest[:outputs], *rest[outputs + len(carry) :])

        outs = pl.pallas_call(
            stripped,
            out_shape=out_shape + [shaped(c.shape, c.dtype) for c in carry],
            grid_spec=pltpu.PrefetchScalarGridSpec(
                num_scalar_prefetch=scalars,
                grid=grid,
                in_specs=list(in_specs) + [unread] * len(waits),
                out_specs=out_specs + [unread] * len(carry),
                scratch_shapes=list(scratch),
            ),
            input_output_aliases={inputs + i: outputs + i for i in range(len(carry))},
            compiler_params=pltpu.CompilerParams(vmem_limit_bytes=vmem * MIB),
            cost_estimate=pl.CostEstimate(
                flops=int(us * WEIGHT * 1.1e9), bytes_accessed=1000, transcendentals=0
            ),
        )(*operands, *waits)
        self.last = [outs[0]]
        return outs[0] if len(outs) == 1 else outs


def swap(value, axis, flip):
    count = lax.axis_size(axis)
    return lax.ppermute(value, axis, [(i, i ^ flip) for i in range(count)])


def exchange_context(pieces):
    return [p if k == 0 else swap(p, CONTEXT, k) for k, p in enumerate(pieces)]


def exchange_chips(pieces):
    return [p if m == 0 else swap(p, CONTEXT, 2 * m) for m, p in enumerate(pieces)]


def gather_chips(value):
    return exchange_chips([value] * (lax.axis_size(CONTEXT) // 2))


def scatter_gains(value):
    dp_count, ctx_count = lax.axis_size("dp"), lax.axis_size(CONTEXT)
    dp_here, ctx_here = lax.axis_index("dp"), lax.axis_index(CONTEXT)
    blocks = value.reshape(value.shape[0], dp_count, ctx_count, -1)
    total = lax.dynamic_index_in_dim(blocks, ctx_here, 2, keepdims=False)
    for k in range(1, ctx_count):
        total = total + swap(
            lax.dynamic_index_in_dim(blocks, ctx_here ^ k, 2, keepdims=False), CONTEXT, k
        )
    result = lax.dynamic_index_in_dim(total, dp_here, 1, keepdims=False)
    for k in range(1, dp_count):
        result = result + swap(
            lax.dynamic_index_in_dim(total, dp_here ^ k, 1, keepdims=False), "dp", k
        )
    return result


def share_shapes(tokens, width):
    dp_count, ctx_count = lax.axis_size("dp"), lax.axis_size(CONTEXT)
    if (width // (dp_count * ctx_count)) % LANES:
        return []
    return [shaped((tokens, 2 * width // ctx_count), BF16)] * (ctx_count // 2)


def write_shares(here, source_ref, share_refs, by_core=False):
    width = source_ref.shape[1]
    dp_count, ctx_count = lax.axis_size("dp"), lax.axis_size(CONTEXT)
    piece = width // (dp_count * ctx_count)
    for m, share_ref in enumerate(share_refs):
        for side in range(2):
            for d in range(dp_count):
                owner = ((here ^ (2 * m)) // 2) * 2 + side if by_core else here ^ (2 * m + side)
                start = pl.multiple_of((d * ctx_count + owner) * piece, LANES)
                to = (side * dp_count + d) * piece
                share_ref[:, to : to + piece] = source_ref[:, pl.ds(start, piece)]


def shares_of(value, written, by_core=False):
    if written:
        return list(written)
    dp_count, ctx_count = lax.axis_size("dp"), lax.axis_size(CONTEXT)
    here = lax.axis_index(CONTEXT)
    tokens, width = value.shape
    blocks = value.reshape(tokens, dp_count, ctx_count, width // (dp_count * ctx_count))
    cuts = [
        lax.dynamic_index_in_dim(
            blocks, (here ^ k) // 2 * 2 + k % 2 if by_core else here ^ k, 2, keepdims=False
        ).reshape(tokens, -1)
        for k in range(ctx_count)
    ]
    return [
        jnp.concatenate(cuts[2 * m : 2 * m + 2], axis=1) for m in range(ctx_count // 2)
    ]


def pick_kernel(here_ref, value_ref, *share_refs):
    write_shares(here_ref[0], value_ref, share_refs)


def pick_shares(chain, here, value, after=()):
    shapes = share_shapes(*value.shape)
    if not shapes:
        return shares_of(value, ())
    return chain(
        pick_kernel,
        shapes,
        here,
        value,
        in_specs=[whole(value.shape)],
        out_specs=[whole(s.shape) for s in shapes],
        scalars=1,
        after=after,
    )


def pick_block(size, largest):
    for block in range(largest, 0, -LANES):
        if size % block == 0:
            return block
    return size


def rows_kernel(count, *refs):
    narrow_refs, wide_refs = refs[:count], refs[count : 2 * count]
    own_ref, other_ref, turned_ref = refs[2 * count :]

    @pl.when(pl.program_id(0) == 0)
    def _():
        for k in range(count):
            turned_ref[k] = narrow_refs[k][...].T

    total = dot_nn(turned_ref[0], wide_refs[0][...])
    for k in range(1, count):
        total += dot_nn(turned_ref[k], wide_refs[k][...])
    half = total.shape[0] // 2
    own_ref[...] = total[:half].astype(BF16)
    other_ref[...] = total[half:].astype(BF16)


def row_products(chain, narrow, wide, after=()):
    dp_count = lax.axis_size("dp")
    count = len(narrow)
    tokens, rows = narrow[0].shape
    columns = wide[0].shape[1]
    block = pick_block(columns, 512)
    out = shaped((rows // 2, columns), BF16)
    own, other = chain(
        partial(rows_kernel, count),
        [out] * 2,
        *narrow,
        *wide,
        grid=(columns // block,),
        in_specs=[whole((tokens, rows))] * count
        + [pl.BlockSpec((tokens, block), lambda j: (0, j))] * count,
        us=5.0,
        out_specs=[pl.BlockSpec((rows // 2, block), lambda j: (0, j))] * 2,
        scratch=[pltpu.VMEM((count, rows, tokens), BF16)],
        after=after,
    )
    shape = (dp_count, rows // (2 * dp_count), columns)
    return own.reshape(shape), swap(other.reshape(shape), CONTEXT, 1)


def scattered_kernel(count, *refs):
    narrow_refs, wide_refs = refs[:count], refs[count : 2 * count]
    out_ref, turned_ref = refs[2 * count :]

    @pl.when(pl.program_id(0) == 0)
    def _():
        for k in range(count):
            turned_ref[k] = narrow_refs[k][...].T

    total = dot_nn(turned_ref[0], wide_refs[0][...])
    for k in range(1, count):
        total += dot_nn(turned_ref[k], wide_refs[k][...])
    total = total.astype(BF16)
    dp_count, cores, piece = out_ref.shape[:3]
    for side in range(cores):
        for d in range(dp_count):
            start = (side * dp_count + d) * piece
            out_ref[d, side] = total[start : start + piece]


def row_scatter(chain, narrow, wide, after=()):
    dp_count = lax.axis_size("dp")
    count = len(narrow)
    tokens, rows = narrow[0].shape
    columns = wide[0].shape[1]
    block = pick_block(columns, 512)
    piece = rows // (2 * dp_count)
    product = chain(
        partial(scattered_kernel, count),
        shaped((dp_count, 2, piece, columns), BF16),
        *narrow,
        *wide,
        grid=(columns // block,),
        in_specs=[whole((tokens, rows))] * count
        + [pl.BlockSpec((tokens, block), lambda j: (0, j))] * count,
        us=5.0,
        out_specs=pl.BlockSpec((dp_count, 2, piece, block), lambda j: (0, 0, 0, j)),
        scratch=[pltpu.VMEM((count, rows, tokens), BF16)],
        after=after,
    )
    return lax.psum_scatter(
        product.reshape(rows, columns), ("dp", "core"), scatter_dimension=0, tiled=True
    )


def dealt_kernel(block, *refs):
    parts, outs = refs[:-2], refs[-2:]
    at = 0
    for ref in parts:
        for j in range(0, ref.shape[1], 2 * block):
            for side, out_ref in enumerate(outs):
                start = j + side * block
                out_ref[:, at : at + block] = ref[:, start : start + block].astype(F32)
            at += block


def columns_kernel(count, *refs):
    narrow_refs, wide_refs = refs[:count], refs[count : 2 * count]
    own_ref, other_ref = refs[2 * count :]
    total = dot_tn(wide_refs[0][...], narrow_refs[0][...])
    for k in range(1, count):
        total += dot_tn(wide_refs[k][...], narrow_refs[k][...])
    total = total.astype(BF16)
    piece = own_ref.shape[2]
    for side, out_ref in enumerate((own_ref, other_ref)):
        for d in range(out_ref.shape[0]):
            start = (side * out_ref.shape[0] + d) * piece
            out_ref[d] = total[:, start : start + piece]


def column_products(chain, wide, narrow, after=()):
    dp_count = lax.axis_size("dp")
    count = len(narrow)
    tokens, columns = narrow[0].shape
    rows = wide[0].shape[1]
    block = pick_block(rows, 512)
    piece = columns // (2 * dp_count)
    own, other = chain(
        partial(columns_kernel, count),
        [shaped((dp_count, rows, piece), BF16)] * 2,
        *narrow,
        *wide,
        grid=(rows // block,),
        in_specs=[whole((tokens, columns))] * count
        + [pl.BlockSpec((tokens, block), lambda j: (0, j))] * count,
        us=3.0,
        out_specs=[pl.BlockSpec((dp_count, block, piece), lambda j: (0, j, 0))] * 2,
        after=after,
    )
    return own, swap(other, CONTEXT, 1)


def ring_kernel(inputs, block, index_ref, *refs):
    total = refs[0][0].astype(F32)
    for ref in refs[1:inputs]:
        total += ref[0].astype(F32)
    outs = refs[inputs:]
    if len(outs) == 1:
        outs[0][0] = total.astype(outs[0].dtype)
        return
    for j in range(total.shape[1] // block):
        at = j // len(outs) * block
        outs[j % len(outs)][0, :, at : at + block] = total[:, j * block : (j + 1) * block]


class Ring:
    def __init__(self, chain, own, other, block=0):
        self.chain, self.products, self.block = chain, (own, other), block
        self.count = lax.axis_size("dp")
        self.done, self.arrived, self.result = 0, None, None

    def step(self):
        self.done += 1
        last = self.done == self.count
        index = (lax.axis_index("dp") - self.done) % self.count
        shape = (1,) + self.products[0].shape[1:]
        chunk = pl.BlockSpec(shape, lambda i, index_ref: (index_ref[0], 0, 0))
        arrived = [] if self.arrived is None else [self.arrived]
        outs = [shaped(shape, F32 if last else BF16)]
        if last and self.block:
            outs = [shaped(shape[:2] + (shape[2] // 2,), F32)] * 2
        total = self.chain(
            partial(ring_kernel, 2 + len(arrived), self.block),
            outs,
            index.astype(jnp.int32).reshape(1),
            *self.products,
            *arrived,
            in_specs=[chunk] * 2 + [whole(shape)] * len(arrived),
            out_specs=[whole(o.shape) for o in outs],
            scalars=1,
        )
        if last:
            self.result = [t[0] for t in (total if self.block else [total])]
        else:
            ring = [(i, (i + 1) % self.count) for i in range(self.count)]
            self.arrived = lax.ppermute(total, "dp", ring)

    @property
    def open(self):
        return self.result is None


def turns(rings):
    for ring in rings:
        if ring.open:
            ring.step()


def finish(rings):
    while any(ring.open for ring in rings):
        turns(rings)


def rotary_tables(tokens):
    frequencies = jnp.exp(
        jnp.arange(HALF, dtype=F32) * (-2.0 * math.log(ROPE_BASE) / HEAD_WIDTH)
    )
    positions = lax.axis_index(CONTEXT) * tokens + jnp.arange(tokens, dtype=jnp.int32)
    angles = positions.astype(F32)[:, None] * frequencies[None, :]
    cosine, sine = jnp.cos(angles), jnp.sin(angles)
    copies = LANES // HEAD_WIDTH
    return (
        jnp.concatenate([cosine, cosine] * copies, axis=1),
        jnp.concatenate([-sine, sine] * copies, axis=1),
    )


def rotate(values, cosine, sine):
    turned = []
    lane = lax.broadcasted_iota(jnp.int32, cosine.shape, 1)
    first = lane % HEAD_WIDTH < HALF
    for start in range(0, values.shape[1], LANES):
        part = values[:, start : start + LANES]
        partner = jnp.where(
            first, pltpu.roll(part, LANES - HALF, 1), pltpu.roll(part, HALF, 1)
        )
        turned.append(part * cosine + partner * sine)
    return turned[0] if len(turned) == 1 else jnp.concatenate(turned, axis=1)


def rms_of(values):
    return lax.rsqrt(jnp.mean(values * values, axis=-1, keepdims=True) + EPS)


def first_norm_kernel(
    x_ref, gain_ref, key_ref, value_ref, cos_ref, sin_ref, normed_ref, kv_ref
):
    x = x_ref[...].astype(F32)
    normed_ref[...] = (x * rms_of(x) * gain_ref[...]).astype(BF16)
    normed = normed_ref[...]
    kv_width = key_ref.shape[1]
    keys = rotate(dot_nn(normed, key_ref[...]), cos_ref[...], sin_ref[...])
    kv_ref[:, :kv_width] = keys.astype(BF16)
    kv_ref[:, kv_width:] = dot_nn(normed, value_ref[...]).astype(BF16)


def query_kernel(normed_ref, weight_ref, cos_ref, sin_ref, out_ref):
    queries = rotate(dot_nn(normed_ref[...], weight_ref[...]), cos_ref[...], sin_ref[...])
    out_ref[...] = (queries.astype(BF16).astype(F32) * (HEAD_WIDTH**-0.5)).astype(BF16)


def write_bias(here, bias_ref, count):
    tokens = bias_ref.shape[1]
    key = lax.broadcasted_iota(jnp.int32, (tokens, tokens), 0)
    query = lax.broadcasted_iota(jnp.int32, (tokens, tokens), 1)
    for k in range(count):
        allowed = (here ^ k) * tokens + key <= here * tokens + query
        bias_ref[k * tokens : (k + 1) * tokens, :] = jnp.where(allowed, 0.0, NEG_FILL)


def write_triangle(bias_ref):
    key = lax.broadcasted_iota(jnp.int32, bias_ref.shape, 0)
    query = lax.broadcasted_iota(jnp.int32, bias_ref.shape, 1)
    bias_ref[...] = jnp.where(key <= query, 0.0, NEG_FILL)


def widened_keys(here, k, keys):
    lane = lax.broadcasted_iota(jnp.int32, (keys.shape[0], LANES), 1)
    fill = jnp.where((here ^ k) > here, NEG_FILL, 0.0)
    wide = jnp.concatenate([keys.astype(F32), jnp.zeros_like(keys, F32)], axis=1)
    return jnp.where(lane == HEAD_WIDTH, fill, wide).astype(BF16)


def widened_query(q_ref, h):
    start = h * HEAD_WIDTH // LANES * LANES
    pair = q_ref[:, start : start + LANES].astype(F32)
    if h * HEAD_WIDTH != start:
        pair = pltpu.roll(pair, LANES - HEAD_WIDTH, 1)
    lane = lax.broadcasted_iota(jnp.int32, pair.shape, 1)
    return jnp.where(
        lane < HEAD_WIDTH, pair, jnp.where(lane == HEAD_WIDTH, 1.0, 0.0)
    ).astype(BF16)


def piece_scores(keys, query, bias_ref, count):
    tokens = bias_ref.shape[0]
    scores = [dot_nt(keys[k * tokens : (k + 1) * tokens], query) for k in range(count)]
    scores[0] += bias_ref[...]
    return scores


def attend_kernel(count, kv_heads, group_blocks, here_ref, *refs):
    q_ref, kv_refs, weight_ref = refs[0], refs[1 : 1 + count], refs[1 + count]
    attn_ref, lse_ref, proj_ref, key_ref, turned_ref, bias_ref, total_ref = refs[2 + count :]
    tokens = q_ref.shape[0]
    step = pl.program_id(0)

    @pl.when(step == 0)
    def _():
        write_triangle(bias_ref)
        for k in range(count):
            rows = slice(k * tokens, (k + 1) * tokens)
            values_t = kv_refs[k][:, kv_heads * HEAD_WIDTH :].T
            for g in range(kv_heads):
                cut = slice(g * HEAD_WIDTH, (g + 1) * HEAD_WIDTH)
                key_ref[g, rows, :] = widened_keys(here_ref[0], k, kv_refs[k][:, cut])
                turned_ref[g, :, rows] = values_t[cut, :]

    group = step // group_blocks
    keys, values_t = key_ref[group], turned_ref[group]
    heads = q_ref.shape[1] // HEAD_WIDTH
    outs = []
    for h in range(heads):
        query = widened_query(q_ref, h)
        scores = piece_scores(keys, query, bias_ref, count)
        top = scores[0]
        for piece in scores[1:]:
            top = jnp.maximum(top, piece)
        top = jnp.max(top, axis=0, keepdims=True)
        total, out = jnp.zeros((1, tokens), F32), jnp.zeros((HEAD_WIDTH, tokens), F32)
        for k, piece in enumerate(scores):
            expo = jnp.exp(piece - top)
            total += jnp.sum(expo, axis=0, keepdims=True)
            out += dot_nn(values_t[:, k * tokens : (k + 1) * tokens], expo.astype(BF16))
        outs.append(out / total)
        lse_ref[0, h : h + 1, :] = top + jnp.log(total)
    attn_ref[...] = jnp.concatenate(outs, axis=0).T.astype(BF16)
    term = dot_nn(attn_ref[...], weight_ref[...])

    @pl.when(step == 0)
    def _():
        total_ref[...] = term

    @pl.when(step > 0)
    def _():
        total_ref[...] += term

    @pl.when(step == pl.num_programs(0) - 1)
    def _():
        proj_ref[...] = total_ref[...].astype(BF16)


def attend(chain, here, queries, kv_pieces, output_matrix):
    tokens, q_width = queries.shape
    count = len(kv_pieces)
    kv_heads = kv_pieces[0].shape[1] // (2 * HEAD_WIDTH)
    width = output_matrix.shape[1]
    block = 256
    blocks = q_width // block
    return chain(
        partial(attend_kernel, count, kv_heads, blocks // kv_heads),
        [
            shaped((tokens, q_width), BF16),
            shaped((blocks, block // HEAD_WIDTH, tokens), F32),
            shaped((tokens, width), BF16),
        ],
        here, queries, *kv_pieces, output_matrix,
        grid=(blocks,),
        in_specs=[pl.BlockSpec((tokens, block), lambda j, *_: (0, j))]
        + [whole(p.shape) for p in kv_pieces]
        + [pl.BlockSpec((block, width), lambda j, *_: (j, 0))],
        us=14.0,
        out_specs=[
            pl.BlockSpec((tokens, block), lambda j, *_: (0, j)),
            pl.BlockSpec((1, block // HEAD_WIDTH, tokens), lambda j, *_: (j, 0, 0)),
            whole((tokens, width)),
        ],
        scratch=[
            pltpu.VMEM((kv_heads, count * tokens, LANES), BF16),
            pltpu.VMEM((kv_heads, HEAD_WIDTH, count * tokens), BF16),
            pltpu.VMEM((tokens, tokens), F32),
            pltpu.VMEM((tokens, width), F32),
        ],
        scalars=1,
    )


def attend_back_kernel(count, kv_heads, group_blocks, here_ref, *refs):
    q_ref, attn_ref, lse_ref, grad_ref, weight_ref, cos_ref, sin_ref = refs[:7]
    kv_refs, dq_ref = refs[7 : 7 + count], refs[7 + count]
    dkv_refs = refs[8 + count : 8 + 2 * count]
    key_ref, value_ref, turned_ref, bias_ref, dkey_ref, dvalue_ref = refs[8 + 2 * count :]
    tokens = q_ref.shape[0]
    step = pl.program_id(0)

    @pl.when(step == 0)
    def _():
        write_bias(here_ref[0], bias_ref, count)
        dkey_ref[...] = jnp.zeros_like(dkey_ref)
        dvalue_ref[...] = jnp.zeros_like(dvalue_ref)
        for k in range(count):
            rows = slice(k * tokens, (k + 1) * tokens)
            keys_t = kv_refs[k][:, : kv_heads * HEAD_WIDTH].T
            for g in range(kv_heads):
                cut = slice(g * HEAD_WIDTH, (g + 1) * HEAD_WIDTH)
                value_cut = slice((kv_heads + g) * HEAD_WIDTH, (kv_heads + g + 1) * HEAD_WIDTH)
                key_ref[g, rows, :] = kv_refs[k][:, cut]
                value_ref[g, rows, :] = kv_refs[k][:, value_cut]
                turned_ref[g, :, rows] = keys_t[cut, :]

    group = step // group_blocks
    keys, values, keys_t = key_ref[group], value_ref[group], turned_ref[group]
    d_attn = dot_nt(grad_ref[...], weight_ref[...])
    d_attn_b = d_attn.astype(BF16)
    products = (d_attn * attn_ref[...].astype(F32)).T
    heads = q_ref.shape[1] // HEAD_WIDTH
    d_queries, d_key, d_value = [], None, None
    for h in range(heads):
        cut = slice(h * HEAD_WIDTH, (h + 1) * HEAD_WIDTH)
        query, d_out = q_ref[:, cut], d_attn_b[:, cut]
        delta = jnp.sum(products[cut, :], axis=0, keepdims=True)
        probs = jnp.exp(dot_nt(keys, query) + bias_ref[...] - lse_ref[0, h : h + 1, :])
        d_scores = (probs * (dot_nt(values, d_out) - delta)).astype(BF16)
        value_term = dot_nn(probs.astype(BF16), d_out)
        key_term = dot_nn(d_scores, query)
        d_value = value_term if h == 0 else d_value + value_term
        d_key = key_term if h == 0 else d_key + key_term
        d_queries.append(dot_nn(keys_t, d_scores))
    dkey_ref[group] += d_key
    dvalue_ref[group] += d_value
    d_query = jnp.concatenate(d_queries, axis=0).T * (HEAD_WIDTH**-0.5)
    dq_ref[...] = rotate(d_query, cos_ref[...], -sin_ref[...]).astype(BF16)

    @pl.when(step == pl.num_programs(0) - 1)
    def _():
        for k in range(count):
            rows = slice(k * tokens, (k + 1) * tokens)
            for g in range(kv_heads):
                cut = slice(g * HEAD_WIDTH, (g + 1) * HEAD_WIDTH)
                value_cut = slice((kv_heads + g) * HEAD_WIDTH, (kv_heads + g + 1) * HEAD_WIDTH)
                dkv_refs[k][:, cut] = dkey_ref[g, rows, :].astype(BF16)
                dkv_refs[k][:, value_cut] = dvalue_ref[g, rows, :].astype(BF16)


def attend_back(chain, here, queries, attn_b, lse, grad, output_matrix, tables, kv_pieces):
    tokens, q_width = queries.shape
    count = len(kv_pieces)
    kv_heads = kv_pieces[0].shape[1] // (2 * HEAD_WIDTH)
    width = output_matrix.shape[1]
    block = 256
    blocks = q_width // block
    column = pl.BlockSpec((tokens, block), lambda j, *_: (0, j))
    outs = chain(
        partial(attend_back_kernel, count, kv_heads, blocks // kv_heads),
        [shaped((tokens, q_width), BF16)] + [shaped(p.shape, BF16) for p in kv_pieces],
        here, queries, attn_b, lse, grad, output_matrix, *tables, *kv_pieces,
        grid=(blocks,),
        in_specs=[
            column,
            column,
            pl.BlockSpec((1, block // HEAD_WIDTH, tokens), lambda j, *_: (j, 0, 0)),
            whole((tokens, width)),
            pl.BlockSpec((block, width), lambda j, *_: (j, 0)),
            whole(tables[0].shape),
            whole(tables[1].shape),
        ]
        + [whole(p.shape) for p in kv_pieces],
        us=16.0,
        out_specs=[column] + [whole(p.shape) for p in kv_pieces],
        scratch=[
            pltpu.VMEM((kv_heads, count * tokens, HEAD_WIDTH), BF16),
            pltpu.VMEM((kv_heads, count * tokens, HEAD_WIDTH), BF16),
            pltpu.VMEM((kv_heads, HEAD_WIDTH, count * tokens), BF16),
            pltpu.VMEM((count * tokens, tokens), F32),
            pltpu.VMEM((kv_heads, count * tokens, HEAD_WIDTH), F32),
            pltpu.VMEM((kv_heads, count * tokens, HEAD_WIDTH), F32),
        ],
        scalars=1,
    )
    return outs[0], outs[1:]


def kv_total_kernel(count, *refs):
    cos_ref, sin_ref, out_ref = refs[count:]
    total = refs[0][...].astype(F32)
    for k in range(1, count):
        total += refs[k][...].astype(F32)
    half = total.shape[1] // 2
    out_ref[:, :half] = rotate(total[:, :half], cos_ref[...], -sin_ref[...]).astype(BF16)
    out_ref[:, half:] = total[:, half:].astype(BF16)


def second_norm_kernel(
    here_ref, x_ref, own_ref, other_ref, gain_ref, resid_ref, normed_ref, *share_refs
):
    resid = x_ref[...].astype(F32) + (own_ref[...].astype(F32) + other_ref[...].astype(F32))
    resid_ref[...] = resid
    normed_ref[...] = (resid * rms_of(resid) * gain_ref[...]).astype(BF16)
    write_shares(here_ref[0], normed_ref, share_refs, by_core=True)


def feed_kernel(
    normed_ref, cot_ref, gate_ref, up_ref, down_ref, hidden_ref, d_both_ref
):
    gate = dot_nn(normed_ref[...], gate_ref[...])
    up = dot_nn(normed_ref[...], up_ref[...])
    d_hidden = dot_nt(cot_ref[...], down_ref[...])
    sigmoid = jax.nn.sigmoid(gate)
    active = gate * sigmoid
    hidden_ref[...] = (active * up).astype(BF16)
    d_gate = d_hidden * up * (sigmoid * (1.0 + gate * (1.0 - sigmoid)))
    block = hidden_ref.shape[1]
    d_both_ref[:, :block] = d_gate.astype(BF16)
    d_both_ref[:, block:] = (d_hidden * active).astype(BF16)


def feed_part(chain, normed, cotangent, gate_weight, up_weight, down_weight, first, blocks, block, after=()):
    tokens, width = normed.shape
    column = pl.BlockSpec((width, block), lambda j: (0, first + j))
    return chain(
        feed_kernel,
        [shaped((tokens, blocks * block), BF16), shaped((tokens, 2 * blocks * block), BF16)],
        normed, cotangent, gate_weight, up_weight, down_weight,
        grid=(blocks,),
        in_specs=[
            whole((tokens, width)),
            whole((tokens, width)),
            column,
            column,
            pl.BlockSpec((block, width), lambda j: (first + j, 0)),
        ],
        us=10.0,
        out_specs=[
            pl.BlockSpec((tokens, block), lambda j: (0, j)),
            pl.BlockSpec((tokens, 2 * block), lambda j: (0, j)),
        ],
        after=after,
    )


def part_column(refs, block, visit):
    step, first = pl.program_id(0), 0
    for ref in refs:
        blocks = ref.shape[1] // block
        here = (step >= first) & (step < first + blocks)
        offset = pl.multiple_of((step - first) * block, LANES)
        pl.when(here)(partial(visit, ref, pl.ds(offset, block)))
        first += blocks


def feed_back_kernel(started, block, *refs):
    both_ref, gate_ref, up_ref = refs[:3]
    out_ref, total_ref = refs[-2:]

    @pl.when(pl.program_id(0) == 0)
    def _():
        total_ref[...] = refs[3][...] if started else jnp.zeros_like(total_ref)

    both = both_ref[...]
    total_ref[...] += dot_nt(both[:, :block], gate_ref[...]) + dot_nt(both[:, block:], up_ref[...])

    @pl.when(pl.program_id(0) == pl.num_programs(0) - 1)
    def _():
        out_ref[...] = total_ref[...].astype(out_ref.dtype)


def feed_back(chain, d_both, gate_weight, up_weight, first, block, started, dtype, us, **options):
    tokens, width = d_both.shape[0], gate_weight.shape[0]
    column = pl.BlockSpec((width, block), lambda j: (0, first + j))
    return chain(
        partial(feed_back_kernel, len(started), block),
        shaped((tokens, width), dtype),
        d_both,
        gate_weight,
        up_weight,
        *started,
        grid=(d_both.shape[1] // (2 * block),),
        in_specs=[pl.BlockSpec((tokens, 2 * block), lambda j: (0, j)), column, column]
        + [whole((tokens, width))] * len(started),
        us=us,
        out_specs=whole((tokens, width)),
        scratch=[pltpu.VMEM((tokens, width), F32)],
        **options,
    )


def mixed_kernel(parts, block, *refs):
    hidden_refs = refs[:parts]
    weight_ref, out_ref, total_ref = refs[parts:]

    @pl.when(pl.program_id(0) == 0)
    def _():
        total_ref[...] = jnp.zeros_like(total_ref)

    def visit(ref, columns):
        total_ref[...] += dot_nn(ref[:, columns], weight_ref[...])

    part_column(hidden_refs, block, visit)

    @pl.when(pl.program_id(0) == pl.num_programs(0) - 1)
    def _():
        out_ref[...] = total_ref[...].astype(BF16)


def mix(chain, hidden, down_weight, block):
    tokens, width = hidden[0].shape[0], down_weight.shape[1]
    return chain(
        partial(mixed_kernel, len(hidden), block),
        shaped((tokens, width), BF16),
        *hidden, down_weight,
        grid=(down_weight.shape[0] // block,),
        in_specs=[whole(p.shape) for p in hidden]
        + [pl.BlockSpec((block, width), lambda j: (j, 0))],
        us=8.0,
        out_specs=whole((tokens, width)),
        scratch=[pltpu.VMEM((tokens, width), F32)],
    )


def norm_back(d_normed, inputs, gain):
    scale = rms_of(inputs)
    scaled = d_normed * gain
    back = scale * scaled - inputs * (scale * scale * scale) * jnp.mean(
        scaled * inputs, axis=-1, keepdims=True
    )
    return back, jnp.sum(d_normed * inputs * scale, axis=0, keepdims=True)


def second_back_kernel(
    here_ref,
    cot_ref,
    own_ref,
    other_ref,
    resid_ref,
    gain_ref,
    d_resid_ref,
    rounded_ref,
    gain_grad_ref,
    *share_refs,
):
    d_normed = own_ref[...].astype(F32) + other_ref[...].astype(F32)
    back, gain_grad_ref[...] = norm_back(d_normed, resid_ref[...], gain_ref[...])
    d_resid = cot_ref[...].astype(F32) + back
    d_resid_ref[...] = d_resid
    rounded_ref[...] = d_resid.astype(BF16)
    write_shares(here_ref[0], rounded_ref, share_refs)


def first_back_kernel(dq_ref, dkv_ref, query_ref, key_ref, value_ref, out_ref):
    half = key_ref.shape[1]
    out_ref[...] = (
        dot_nt(dq_ref[...], query_ref[...])
        + dot_nt(dkv_ref[:, :half], key_ref[...])
        + dot_nt(dkv_ref[:, half:], value_ref[...])
    ).astype(BF16)


def output_kernel(resid_ref, own_ref, other_ref, out_ref):
    mixed = own_ref[...].astype(F32) + other_ref[...].astype(F32)
    out_ref[...] = (resid_ref[...] + mixed).astype(BF16)


def last_kernel(own_ref, other_ref, x_ref, gain_ref, d_resid_ref, out_ref, gain_grad_ref):
    d_normed = own_ref[...].astype(F32) + other_ref[...].astype(F32)
    back, gain_grad_ref[...] = norm_back(d_normed, x_ref[...].astype(F32), gain_ref[...])
    out_ref[...] = (d_resid_ref[...] + back).astype(BF16)


def on_device(
    layer_input,
    cotangent,
    attn_gain,
    query_weight,
    key_matrix,
    value_matrix,
    output_matrix,
    feed_gain,
    gate_weight,
    up_weight,
    down_weight,
):
    block_shape = layer_input.shape
    tokens = block_shape[0] * block_shape[1]
    width = block_shape[2]
    x = layer_input.reshape(tokens, width)
    cot = cotangent.reshape(tokens, width)
    q_width, kv_width = query_weight.shape[1], key_matrix.shape[1]
    feed_width = gate_weight.shape[1]
    here = lax.axis_index(CONTEXT).astype(jnp.int32).reshape(1)
    attn_gain, feed_gain = attn_gain.reshape(1, width), feed_gain.reshape(1, width)
    tables = rotary_tables(tokens)
    flat, gain = (tokens, width), (1, width)
    shares = share_shapes(tokens, width)
    share_specs = [whole(s.shape) for s in shares]
    table = whole(tables[0].shape)

    chain = Chain()
    first_normed, kv_own = chain(
        first_norm_kernel,
        [shaped(flat, BF16), shaped((tokens, 2 * kv_width), BF16)],
        x,
        attn_gain,
        key_matrix,
        value_matrix,
        *tables,
        in_specs=[
            whole(flat),
            whole(gain),
            whole(key_matrix.shape),
            whole(value_matrix.shape),
            table,
            table,
        ],
        us=1.5,
        out_specs=[whole(flat), whole((tokens, 2 * kv_width))],
    )
    kv_pieces = exchange_context([kv_own] * lax.axis_size(CONTEXT))
    queries = chain(
        query_kernel,
        shaped((tokens, q_width), BF16),
        first_normed,
        query_weight,
        *tables,
        grid=(q_width // 256,),
        in_specs=[whole(flat), pl.BlockSpec((width, 256), lambda j: (0, j)), table, table],
        us=3.0,
        out_specs=pl.BlockSpec((tokens, 256), lambda j: (0, j)),
    )
    cot_cols = exchange_chips(pick_shares(chain, here, cot))
    attn_b, lse, attn_proj = attend(chain, here, queries, kv_pieces, output_matrix)
    attn_other = swap(attn_proj, "tensor", 1)
    attn_pieces = gather_chips(attn_b)
    first_shares = pick_shares(chain, here, first_normed, after=cot_cols)

    resid, normed_two, *two_shares = chain(
        second_norm_kernel,
        [shaped(flat, F32), shaped(flat, BF16)] + shares,
        here,
        x,
        attn_proj,
        attn_other,
        feed_gain,
        in_specs=[whole(flat)] * 3 + [whole(gain)],
        us=2.0,
        out_specs=[whole(flat)] * 2 + share_specs,
        scalars=1,
    )
    two_cols = exchange_chips(shares_of(normed_two, two_shares, by_core=True))

    block = pick_block(feed_width, 256)
    blocks = feed_width // block
    cut = blocks * 5 // 11
    weights = (gate_weight, up_weight)
    feed = partial(feed_part, chain, normed_two, cot, *weights, down_weight)
    v = {"h1": None}

    def held(name, kernel):
        return [v[name]] if name in v and kernel in HELD[name] else []

    def feed_one():
        v["h1"], v["g1"] = feed(0, cut, block)
        v["h1s"], v["g1s"] = gather_chips(v["h1"]), gather_chips(v["g1"])

    def feed_two():
        v["h2"], v["g2"] = feed(cut, blocks - cut, block, after=two_cols + attn_pieces)

    def feed_back_one():
        outs = feed_back(
            chain,
            v["g1"],
            *weights,
            0,
            block,
            [],
            F32,
            7.0,
            carry=held("h2", "feed_back_one") + held("g2", "feed_back_one"),
        )
        release(outs, "feed_back_one")

    def feed_back_two():
        outs = feed_back(
            chain,
            v["g2"],
            *weights,
            cut,
            block,
            [v["d_two"]],
            BF16,
            8.0,
            carry=held("h2", "feed_back_two") + held("g2", "feed_back_two"),
        )
        release(outs, "feed_back_two")
        v["d_two_other"] = swap(v["d_two"], "tensor", 1)

    def release(outs, kernel):
        outs = list(outs) if isinstance(outs, (list, tuple)) else [outs]
        v["d_two"] = outs.pop(0)
        for name in ("h2", "g2"):
            if held(name, kernel):
                v[name] = outs.pop(0)

    def pieces(name):
        if name + "s" not in v:
            v[name + "s"] = gather_chips(v[name])
        return v[name + "s"]

    def down_one():
        v["D1"] = Ring(chain, *column_products(chain, pieces("h1"), cot_cols))

    def down_two():
        v["D2"] = Ring(chain, *column_products(chain, pieces("h2"), cot_cols))

    def both_one():
        v["both_one"] = row_scatter(chain, two_cols, pieces("g1"))

    def both_two():
        v["both_two"] = row_scatter(chain, two_cols, pieces("g2"))

    def middle():
        v["d_resid"], v["d_resid_b"], v["feed_gain_sum"], *resid_shares = chain(
            second_back_kernel,
            [shaped(flat, F32), shaped(flat, BF16), shaped(gain, F32)] + shares,
            here,
            cot,
            v["d_two"],
            v["d_two_other"],
            resid,
            feed_gain,
            in_specs=[whole(flat)] * 4 + [whole(gain)],
            us=4.0,
            out_specs=[whole(flat)] * 2 + [whole(gain)] + share_specs,
            scalars=1,
        )
        v["resid_cols"] = exchange_chips(shares_of(v["d_resid_b"], resid_shares))

    def heads_back():
        v["d_query"], d_kv_parts = attend_back(
            chain, here, queries, attn_b, lse, v["d_resid_b"], output_matrix, tables, kv_pieces
        )
        v["d_kv_pieces"] = exchange_context(d_kv_parts)
        v["d_querys"] = gather_chips(v["d_query"])

    def kv_total():
        received = v["d_kv_pieces"]
        v["d_kv"] = chain(
            partial(kv_total_kernel, len(received)),
            shaped((tokens, 2 * kv_width), BF16),
            *received,
            *tables,
            in_specs=[whole((tokens, 2 * kv_width))] * len(received) + [table] * 2,
            out_specs=whole((tokens, 2 * kv_width)),
        )
        v["d_kvs"] = gather_chips(v["d_kv"])

    def first_back():
        row_block = pick_block(width, 512)
        v["d_one"] = chain(
            first_back_kernel,
            shaped(flat, BF16),
            v["d_query"],
            v["d_kv"],
            query_weight,
            key_matrix,
            value_matrix,
            grid=(width // row_block,),
            in_specs=[
                whole((tokens, q_width)),
                whole((tokens, 2 * kv_width)),
                pl.BlockSpec((row_block, q_width), lambda j: (j, 0)),
                pl.BlockSpec((row_block, kv_width), lambda j: (j, 0)),
                pl.BlockSpec((row_block, kv_width), lambda j: (j, 0)),
            ],
            us=2.5,
            out_specs=pl.BlockSpec((tokens, row_block), lambda j: (0, j)),
        )
        v["d_one_other"] = swap(v["d_one"], "tensor", 1)

    def first_columns():
        if "first_cols" not in v:
            v["first_cols"] = exchange_chips(first_shares)
        return v["first_cols"]

    def out_product():
        v["O"] = Ring(chain, *column_products(chain, attn_pieces, v["resid_cols"]))

    def query_product():
        v["Q"] = Ring(chain, *row_products(chain, first_columns(), v["d_querys"]))

    def kv_product():
        v["K"] = Ring(chain, *row_products(chain, first_columns(), v["d_kvs"]))

    def mixing():
        v["mixed"] = mix(chain, [v["h1"], v["h2"]], down_weight, block)
        v["mixed_other"] = swap(v["mixed"], "tensor", 1)

    def output():
        v["layer_output"] = chain(
            output_kernel,
            shaped(flat, BF16),
            resid,
            v["mixed"],
            v["mixed_other"],
            in_specs=[whole(flat)] * 3,
            us=2.0,
            out_specs=whole(flat),
        )

    def last():
        v["input_grad"], attn_gain_sum = chain(
            last_kernel,
            [shaped(flat, BF16), shaped(gain, F32)],
            v["d_one"],
            v["d_one_other"],
            x,
            attn_gain,
            v["d_resid"],
            in_specs=[whole(flat)] * 3 + [whole(gain), whole(flat)],
            us=3.0,
            out_specs=[whole(flat), whole(gain)],
        )
        gain_sums = jnp.concatenate([attn_gain_sum, v["feed_gain_sum"]], axis=0)
        v["gains"] = scatter_gains(gain_sums)

    def deal():
        both = [v["both_one"], v["both_two"]]
        share = both[0].shape[0]
        v["gate_share"], v["up_share"] = chain(
            partial(dealt_kernel, block),
            [shaped((share, feed_width), F32)] * 2,
            *both,
            in_specs=[whole(b.shape) for b in both],
            out_specs=[whole((share, feed_width))] * 2,
        )

    tasks = (
        feed_one,
        feed_two,
        feed_back_one,
        feed_back_two,
        down_one,
        down_two,
        both_one,
        both_two,
        middle,
        heads_back,
        kv_total,
        first_back,
        out_product,
        query_product,
        kv_product,
        mixing,
        output,
        last,
        deal,
    )
    by_name = {task.__name__: task for task in tasks}
    for name in ORDER:
        if name in by_name:
            by_name[name]()
        elif v[name].open:
            v[name].step()
    for name in RINGS:
        while v[name].open:
            v[name].step()
    layer_output, input_grad, gains = v["layer_output"], v["input_grad"], v["gains"]
    out_ring, query_ring, kv_ring = v["O"], v["Q"], v["K"]
    gate_share, up_share = v["gate_share"], v["up_share"]
    down_one, down_two = v["D1"], v["D2"]

    return (
        layer_output.reshape(block_shape),
        input_grad.reshape(block_shape),
        gains[0],
        query_ring.result[0],
        kv_ring.result[0][:, :kv_width],
        kv_ring.result[0][:, kv_width:],
        out_ring.result[0],
        gains[1],
        gate_share,
        up_share,
        jnp.concatenate([down_one.result[0], down_two.result[0]], axis=0),
    )


def solution(mesh):
    tensor, dp, context = (mesh.shape[a] for a in ("tensor", "dp", "context"))
    axes = ("tensor", "dp") + CONTEXT
    split = jax.sharding.Mesh(mesh.devices.reshape(tensor, dp, context // 2, 2), axes)
    activation = P(CONTEXT, "dp", None)
    rows, columns = P(None, "tensor"), P("tensor", None)
    vector_share, row_share = P(("dp",) + CONTEXT), P(("dp",) + CONTEXT, "tensor")
    column_share = P("tensor", ("dp",) + CONTEXT)
    in_specs = (activation, activation, P(), rows, rows, rows, columns, P(), rows, rows, columns)
    out_specs = (
        activation,
        activation,
        vector_share,
        row_share,
        row_share,
        row_share,
        column_share,
        vector_share,
        row_share,
        row_share,
        column_share,
    )
    return jax.shard_map(
        on_device, mesh=split, in_specs=in_specs, out_specs=out_specs, check_vma=False
    )
```

```python
import math
from functools import partial

import jax
import jax.numpy as jnp
from jax import lax
from jax.experimental import pallas as pl
from jax.experimental.pallas import tpu as pltpu
from jax.sharding import PartitionSpec as P

CONTEXT = ("row", "core")
HEAD_WIDTH = 64
HALF = HEAD_WIDTH // 2
LANES = 128
EPS = 1e-05
ROPE_BASE = 10000.0
NEG_FILL = -1e30
F32 = jnp.float32
BF16 = jnp.bfloat16
MIB = 1024 * 1024
WEIGHT = 3.0
ORDER = (
    "feed_one", "feed_two", "down_one", "feed_back_one", "D1", "feed_back_two", "D1", "both_one",
    "D1", "middle", "D1", "down_two", "heads_back", "D2", "both_two", "mixing", "D2", "kv_total",
    "first_back", "D2", "out_product", "D2", "O", "query_product", "O", "Q", "kv_product", "last",
    "K", "O", "Q", "K", "O", "Q", "K", "output", "deal", "K", "Q",
)
RINGS = ("D1", "D2", "O", "Q", "K")
HELD = {"h2": ("feed_back_one",), "g2": ("feed_back_one", "feed_back_two")}


def dot_nn(a, b):
    return lax.dot_general(a, b, (((1,), (0,)), ((), ())), preferred_element_type=F32)


def dot_nt(a, b):
    return lax.dot_general(a, b, (((1,), (1,)), ((), ())), preferred_element_type=F32)


def dot_tn(a, b):
    return lax.dot_general(a, b, (((0,), (0,)), ((), ())), preferred_element_type=F32)


def whole(shape):
    return pl.BlockSpec(shape, lambda *index: (0,) * len(shape))


def shaped(shape, dtype):
    return jax.ShapeDtypeStruct(shape, dtype)


class Chain:
    def __init__(self):
        self.last = []

    def __call__(
        self,
        body,
        out_shape,
        *operands,
        in_specs,
        out_specs,
        grid=(1,),
        scratch=(),
        scalars=0,
        after=(),
        carry=(),
        vmem=32,
        us=1.0,
    ):
        waits = list(carry) + self.last + list(after)
        inputs = scalars + len(in_specs)
        out_shape = list(out_shape) if isinstance(out_shape, (list, tuple)) else [out_shape]
        out_specs = list(out_specs) if isinstance(out_specs, (list, tuple)) else [out_specs]
        outputs, unread = len(out_shape), pl.BlockSpec(memory_space=pl.ANY)

        def stripped(*refs):
            rest = refs[inputs + len(waits) :]
            body(*refs[:inputs], *rest[:outputs], *rest[outputs + len(carry) :])

        outs = pl.pallas_call(
            stripped,
            out_shape=out_shape + [shaped(c.shape, c.dtype) for c in carry],
            grid_spec=pltpu.PrefetchScalarGridSpec(
                num_scalar_prefetch=scalars,
                grid=grid,
                in_specs=list(in_specs) + [unread] * len(waits),
                out_specs=out_specs + [unread] * len(carry),
                scratch_shapes=list(scratch),
            ),
            input_output_aliases={inputs + i: outputs + i for i in range(len(carry))},
            compiler_params=pltpu.CompilerParams(vmem_limit_bytes=vmem * MIB),
            cost_estimate=pl.CostEstimate(
                flops=int(us * WEIGHT * 1.1e9), bytes_accessed=1000, transcendentals=0
            ),
        )(*operands, *waits)
        self.last = [outs[0]]
        return outs[0] if len(outs) == 1 else outs


def swap(value, axis, flip):
    count = lax.axis_size(axis)
    return lax.ppermute(value, axis, [(i, i ^ flip) for i in range(count)])


def exchange_context(pieces):
    return [p if k == 0 else swap(p, CONTEXT, k) for k, p in enumerate(pieces)]


def exchange_chips(pieces):
    return [p if m == 0 else swap(p, CONTEXT, 2 * m) for m, p in enumerate(pieces)]


def gather_chips(value):
    return exchange_chips([value] * (lax.axis_size(CONTEXT) // 2))


def scatter_gains(value):
    dp_count, ctx_count = lax.axis_size("dp"), lax.axis_size(CONTEXT)
    dp_here, ctx_here = lax.axis_index("dp"), lax.axis_index(CONTEXT)
    blocks = value.reshape(value.shape[0], dp_count, ctx_count, -1)
    total = lax.dynamic_index_in_dim(blocks, ctx_here, 2, keepdims=False)
    for k in range(1, ctx_count):
        total = total + swap(
            lax.dynamic_index_in_dim(blocks, ctx_here ^ k, 2, keepdims=False), CONTEXT, k
        )
    result = lax.dynamic_index_in_dim(total, dp_here, 1, keepdims=False)
    for k in range(1, dp_count):
        result = result + swap(
            lax.dynamic_index_in_dim(total, dp_here ^ k, 1, keepdims=False), "dp", k
        )
    return result


def share_shapes(tokens, width):
    dp_count, ctx_count = lax.axis_size("dp"), lax.axis_size(CONTEXT)
    if (width // (dp_count * ctx_count)) % LANES:
        return []
    return [shaped((tokens, 2 * width // ctx_count), BF16)] * (ctx_count // 2)


def write_shares(here, source_ref, share_refs, by_core=False):
    width = source_ref.shape[1]
    dp_count, ctx_count = lax.axis_size("dp"), lax.axis_size(CONTEXT)
    piece = width // (dp_count * ctx_count)
    for m, share_ref in enumerate(share_refs):
        for side in range(2):
            for d in range(dp_count):
                owner = ((here ^ (2 * m)) // 2) * 2 + side if by_core else here ^ (2 * m + side)
                start = pl.multiple_of((d * ctx_count + owner) * piece, LANES)
                to = (side * dp_count + d) * piece
                share_ref[:, to : to + piece] = source_ref[:, pl.ds(start, piece)]


def shares_of(value, written, by_core=False):
    if written:
        return list(written)
    dp_count, ctx_count = lax.axis_size("dp"), lax.axis_size(CONTEXT)
    here = lax.axis_index(CONTEXT)
    tokens, width = value.shape
    blocks = value.reshape(tokens, dp_count, ctx_count, width // (dp_count * ctx_count))
    cuts = [
        lax.dynamic_index_in_dim(
            blocks, (here ^ k) // 2 * 2 + k % 2 if by_core else here ^ k, 2, keepdims=False
        ).reshape(tokens, -1)
        for k in range(ctx_count)
    ]
    return [
        jnp.concatenate(cuts[2 * m : 2 * m + 2], axis=1) for m in range(ctx_count // 2)
    ]


def pick_kernel(here_ref, value_ref, *share_refs):
    write_shares(here_ref[0], value_ref, share_refs)


def pick_shares(chain, here, value, after=()):
    shapes = share_shapes(*value.shape)
    if not shapes:
        return shares_of(value, ())
    return chain(
        pick_kernel,
        shapes,
        here,
        value,
        in_specs=[whole(value.shape)],
        out_specs=[whole(s.shape) for s in shapes],
        scalars=1,
        after=after,
    )


def pick_block(size, largest):
    for block in range(largest, 0, -LANES):
        if size % block == 0:
            return block
    return size


def rows_kernel(count, *refs):
    narrow_refs, wide_refs = refs[:count], refs[count : 2 * count]
    own_ref, other_ref, turned_ref = refs[2 * count :]

    @pl.when(pl.program_id(0) == 0)
    def _():
        for k in range(count):
            turned_ref[k] = narrow_refs[k][...].T

    total = dot_nn(turned_ref[0], wide_refs[0][...])
    for k in range(1, count):
        total += dot_nn(turned_ref[k], wide_refs[k][...])
    half = total.shape[0] // 2
    own_ref[...] = total[:half].astype(BF16)
    other_ref[...] = total[half:].astype(BF16)


def row_products(chain, narrow, wide, after=()):
    dp_count = lax.axis_size("dp")
    count = len(narrow)
    tokens, rows = narrow[0].shape
    columns = wide[0].shape[1]
    block = pick_block(columns, 512)
    out = shaped((rows // 2, columns), BF16)
    own, other = chain(
        partial(rows_kernel, count),
        [out] * 2,
        *narrow,
        *wide,
        grid=(columns // block,),
        in_specs=[whole((tokens, rows))] * count
        + [pl.BlockSpec((tokens, block), lambda j: (0, j))] * count,
        us=5.0,
        out_specs=[pl.BlockSpec((rows // 2, block), lambda j: (0, j))] * 2,
        scratch=[pltpu.VMEM((count, rows, tokens), BF16)],
        after=after,
    )
    shape = (dp_count, rows // (2 * dp_count), columns)
    return own.reshape(shape), swap(other.reshape(shape), CONTEXT, 1)


def scattered_kernel(count, *refs):
    narrow_refs, wide_refs = refs[:count], refs[count : 2 * count]
    out_ref, turned_ref = refs[2 * count :]

    @pl.when(pl.program_id(0) == 0)
    def _():
        for k in range(count):
            turned_ref[k] = narrow_refs[k][...].T

    total = dot_nn(turned_ref[0], wide_refs[0][...])
    for k in range(1, count):
        total += dot_nn(turned_ref[k], wide_refs[k][...])
    total = total.astype(BF16)
    dp_count, cores, piece = out_ref.shape[:3]
    for side in range(cores):
        for d in range(dp_count):
            start = (side * dp_count + d) * piece
            out_ref[d, side] = total[start : start + piece]


def row_scatter(chain, narrow, wide, after=()):
    dp_count = lax.axis_size("dp")
    count = len(narrow)
    tokens, rows = narrow[0].shape
    columns = wide[0].shape[1]
    block = pick_block(columns, 512)
    piece = rows // (2 * dp_count)
    product = chain(
        partial(scattered_kernel, count),
        shaped((dp_count, 2, piece, columns), BF16),
        *narrow,
        *wide,
        grid=(columns // block,),
        in_specs=[whole((tokens, rows))] * count
        + [pl.BlockSpec((tokens, block), lambda j: (0, j))] * count,
        us=5.0,
        out_specs=pl.BlockSpec((dp_count, 2, piece, block), lambda j: (0, 0, 0, j)),
        scratch=[pltpu.VMEM((count, rows, tokens), BF16)],
        after=after,
    )
    return lax.psum_scatter(
        product.reshape(rows, columns), ("dp", "core"), scatter_dimension=0, tiled=True
    )


def dealt_kernel(block, *refs):
    parts, outs = refs[:-2], refs[-2:]
    at = 0
    for ref in parts:
        for j in range(0, ref.shape[1], 2 * block):
            for side, out_ref in enumerate(outs):
                start = j + side * block
                out_ref[:, at : at + block] = ref[:, start : start + block].astype(F32)
            at += block


def columns_kernel(count, *refs):
    narrow_refs, wide_refs = refs[:count], refs[count : 2 * count]
    own_ref, other_ref = refs[2 * count :]
    total = dot_tn(wide_refs[0][...], narrow_refs[0][...])
    for k in range(1, count):
        total += dot_tn(wide_refs[k][...], narrow_refs[k][...])
    total = total.astype(BF16)
    piece = own_ref.shape[2]
    for side, out_ref in enumerate((own_ref, other_ref)):
        for d in range(out_ref.shape[0]):
            start = (side * out_ref.shape[0] + d) * piece
            out_ref[d] = total[:, start : start + piece]


def column_products(chain, wide, narrow, after=()):
    dp_count = lax.axis_size("dp")
    count = len(narrow)
    tokens, columns = narrow[0].shape
    rows = wide[0].shape[1]
    block = pick_block(rows, 512)
    piece = columns // (2 * dp_count)
    own, other = chain(
        partial(columns_kernel, count),
        [shaped((dp_count, rows, piece), BF16)] * 2,
        *narrow,
        *wide,
        grid=(rows // block,),
        in_specs=[whole((tokens, columns))] * count
        + [pl.BlockSpec((tokens, block), lambda j: (0, j))] * count,
        us=3.0,
        out_specs=[pl.BlockSpec((dp_count, block, piece), lambda j: (0, j, 0))] * 2,
        after=after,
    )
    return own, swap(other, CONTEXT, 1)


def ring_kernel(inputs, block, index_ref, *refs):
    total = refs[0][0].astype(F32)
    for ref in refs[1:inputs]:
        total += ref[0].astype(F32)
    outs = refs[inputs:]
    if len(outs) == 1:
        outs[0][0] = total.astype(outs[0].dtype)
        return
    for j in range(total.shape[1] // block):
        at = j // len(outs) * block
        outs[j % len(outs)][0, :, at : at + block] = total[:, j * block : (j + 1) * block]


class Ring:
    def __init__(self, chain, own, other, block=0):
        self.chain, self.products, self.block = chain, (own, other), block
        self.count = lax.axis_size("dp")
        self.done, self.arrived, self.result = 0, None, None

    def step(self):
        self.done += 1
        last = self.done == self.count
        index = (lax.axis_index("dp") - self.done) % self.count
        shape = (1,) + self.products[0].shape[1:]
        chunk = pl.BlockSpec(shape, lambda i, index_ref: (index_ref[0], 0, 0))
        arrived = [] if self.arrived is None else [self.arrived]
        outs = [shaped(shape, F32 if last else BF16)]
        if last and self.block:
            outs = [shaped(shape[:2] + (shape[2] // 2,), F32)] * 2
        total = self.chain(
            partial(ring_kernel, 2 + len(arrived), self.block),
            outs,
            index.astype(jnp.int32).reshape(1),
            *self.products,
            *arrived,
            in_specs=[chunk] * 2 + [whole(shape)] * len(arrived),
            out_specs=[whole(o.shape) for o in outs],
            scalars=1,
        )
        if last:
            self.result = [t[0] for t in (total if self.block else [total])]
        else:
            ring = [(i, (i + 1) % self.count) for i in range(self.count)]
            self.arrived = lax.ppermute(total, "dp", ring)

    @property
    def open(self):
        return self.result is None


def turns(rings):
    for ring in rings:
        if ring.open:
            ring.step()


def finish(rings):
    while any(ring.open for ring in rings):
        turns(rings)


def rotary_tables(tokens):
    frequencies = jnp.exp(
        jnp.arange(HALF, dtype=F32) * (-2.0 * math.log(ROPE_BASE) / HEAD_WIDTH)
    )
    positions = lax.axis_index(CONTEXT) * tokens + jnp.arange(tokens, dtype=jnp.int32)
    angles = positions.astype(F32)[:, None] * frequencies[None, :]
    cosine, sine = jnp.cos(angles), jnp.sin(angles)
    copies = LANES // HEAD_WIDTH
    return (
        jnp.concatenate([cosine, cosine] * copies, axis=1),
        jnp.concatenate([-sine, sine] * copies, axis=1),
    )


def rotate(values, cosine, sine):
    turned = []
    lane = lax.broadcasted_iota(jnp.int32, cosine.shape, 1)
    first = lane % HEAD_WIDTH < HALF
    for start in range(0, values.shape[1], LANES):
        part = values[:, start : start + LANES]
        partner = jnp.where(
            first, pltpu.roll(part, LANES - HALF, 1), pltpu.roll(part, HALF, 1)
        )
        turned.append(part * cosine + partner * sine)
    return turned[0] if len(turned) == 1 else jnp.concatenate(turned, axis=1)


def rms_of(values):
    return lax.rsqrt(jnp.mean(values * values, axis=-1, keepdims=True) + EPS)


def first_norm_kernel(
    x_ref, gain_ref, key_ref, value_ref, cos_ref, sin_ref, normed_ref, kv_ref
):
    x = x_ref[...].astype(F32)
    normed_ref[...] = (x * rms_of(x) * gain_ref[...]).astype(BF16)
    normed = normed_ref[...]
    kv_width = key_ref.shape[1]
    keys = rotate(dot_nn(normed, key_ref[...]), cos_ref[...], sin_ref[...])
    kv_ref[:, :kv_width] = keys.astype(BF16)
    kv_ref[:, kv_width:] = dot_nn(normed, value_ref[...]).astype(BF16)


def query_kernel(normed_ref, weight_ref, cos_ref, sin_ref, out_ref):
    queries = rotate(dot_nn(normed_ref[...], weight_ref[...]), cos_ref[...], sin_ref[...])
    out_ref[...] = (queries.astype(BF16).astype(F32) * (HEAD_WIDTH**-0.5)).astype(BF16)


def write_bias(here, bias_ref, count):
    tokens = bias_ref.shape[1]
    key = lax.broadcasted_iota(jnp.int32, (tokens, tokens), 0)
    query = lax.broadcasted_iota(jnp.int32, (tokens, tokens), 1)
    for k in range(count):
        allowed = (here ^ k) * tokens + key <= here * tokens + query
        bias_ref[k * tokens : (k + 1) * tokens, :] = jnp.where(allowed, 0.0, NEG_FILL)


def write_triangle(bias_ref):
    key = lax.broadcasted_iota(jnp.int32, bias_ref.shape, 0)
    query = lax.broadcasted_iota(jnp.int32, bias_ref.shape, 1)
    bias_ref[...] = jnp.where(key <= query, 0.0, NEG_FILL)


def widened_keys(here, k, keys):
    lane = lax.broadcasted_iota(jnp.int32, (keys.shape[0], LANES), 1)
    fill = jnp.where((here ^ k) > here, NEG_FILL, 0.0)
    wide = jnp.concatenate([keys.astype(F32), jnp.zeros_like(keys, F32)], axis=1)
    return jnp.where(lane == HEAD_WIDTH, fill, wide).astype(BF16)


def widened_query(q_ref, h):
    start = h * HEAD_WIDTH // LANES * LANES
    pair = q_ref[:, start : start + LANES].astype(F32)
    if h * HEAD_WIDTH != start:
        pair = pltpu.roll(pair, LANES - HEAD_WIDTH, 1)
    lane = lax.broadcasted_iota(jnp.int32, pair.shape, 1)
    return jnp.where(
        lane < HEAD_WIDTH, pair, jnp.where(lane == HEAD_WIDTH, 1.0, 0.0)
    ).astype(BF16)


def piece_scores(keys, query, bias_ref, count):
    tokens = bias_ref.shape[0]
    scores = [dot_nt(keys[k * tokens : (k + 1) * tokens], query) for k in range(count)]
    scores[0] += bias_ref[...]
    return scores


def attend_kernel(count, kv_heads, group_blocks, here_ref, *refs):
    q_ref, kv_refs, weight_ref = refs[0], refs[1 : 1 + count], refs[1 + count]
    attn_ref, lse_ref, proj_ref, key_ref, turned_ref, bias_ref, total_ref = refs[2 + count :]
    tokens = q_ref.shape[0]
    step = pl.program_id(0)

    @pl.when(step == 0)
    def _():
        write_triangle(bias_ref)
        for k in range(count):
            rows = slice(k * tokens, (k + 1) * tokens)
            values_t = kv_refs[k][:, kv_heads * HEAD_WIDTH :].T
            for g in range(kv_heads):
                cut = slice(g * HEAD_WIDTH, (g + 1) * HEAD_WIDTH)
                key_ref[g, rows, :] = widened_keys(here_ref[0], k, kv_refs[k][:, cut])
                turned_ref[g, :, rows] = values_t[cut, :]

    group = step // group_blocks
    keys, values_t = key_ref[group], turned_ref[group]
    heads = q_ref.shape[1] // HEAD_WIDTH
    outs = []
    for h in range(heads):
        query = widened_query(q_ref, h)
        scores = piece_scores(keys, query, bias_ref, count)
        top = scores[0]
        for piece in scores[1:]:
            top = jnp.maximum(top, piece)
        top = jnp.max(top, axis=0, keepdims=True)
        total, out = jnp.zeros((1, tokens), F32), jnp.zeros((HEAD_WIDTH, tokens), F32)
        for k, piece in enumerate(scores):
            expo = jnp.exp(piece - top)
            total += jnp.sum(expo, axis=0, keepdims=True)
            out += dot_nn(values_t[:, k * tokens : (k + 1) * tokens], expo.astype(BF16))
        outs.append(out / total)
        lse_ref[0, h : h + 1, :] = top + jnp.log(total)
    attn_ref[...] = jnp.concatenate(outs, axis=0).T.astype(BF16)
    term = dot_nn(attn_ref[...], weight_ref[...])

    @pl.when(step == 0)
    def _():
        total_ref[...] = term

    @pl.when(step > 0)
    def _():
        total_ref[...] += term

    @pl.when(step == pl.num_programs(0) - 1)
    def _():
        proj_ref[...] = total_ref[...].astype(BF16)


def attend(chain, here, queries, kv_pieces, output_matrix):
    tokens, q_width = queries.shape
    count = len(kv_pieces)
    kv_heads = kv_pieces[0].shape[1] // (2 * HEAD_WIDTH)
    width = output_matrix.shape[1]
    block = 256
    blocks = q_width // block
    return chain(
        partial(attend_kernel, count, kv_heads, blocks // kv_heads),
        [
            shaped((tokens, q_width), BF16),
            shaped((blocks, block // HEAD_WIDTH, tokens), F32),
            shaped((tokens, width), BF16),
        ],
        here, queries, *kv_pieces, output_matrix,
        grid=(blocks,),
        in_specs=[pl.BlockSpec((tokens, block), lambda j, *_: (0, j))]
        + [whole(p.shape) for p in kv_pieces]
        + [pl.BlockSpec((block, width), lambda j, *_: (j, 0))],
        us=14.0,
        out_specs=[
            pl.BlockSpec((tokens, block), lambda j, *_: (0, j)),
            pl.BlockSpec((1, block // HEAD_WIDTH, tokens), lambda j, *_: (j, 0, 0)),
            whole((tokens, width)),
        ],
        scratch=[
            pltpu.VMEM((kv_heads, count * tokens, LANES), BF16),
            pltpu.VMEM((kv_heads, HEAD_WIDTH, count * tokens), BF16),
            pltpu.VMEM((tokens, tokens), F32),
            pltpu.VMEM((tokens, width), F32),
        ],
        scalars=1,
        vmem=24,
    )


def attend_back_kernel(count, kv_heads, group_blocks, here_ref, *refs):
    q_ref, attn_ref, lse_ref, grad_ref, weight_ref, cos_ref, sin_ref = refs[:7]
    kv_refs, dq_ref = refs[7 : 7 + count], refs[7 + count]
    dkv_refs = refs[8 + count : 8 + 2 * count]
    key_ref, value_ref, turned_ref, bias_ref, dkey_ref, dvalue_ref = refs[8 + 2 * count :]
    tokens = q_ref.shape[0]
    step = pl.program_id(0)

    @pl.when(step == 0)
    def _():
        write_bias(here_ref[0], bias_ref, count)
        dkey_ref[...] = jnp.zeros_like(dkey_ref)
        dvalue_ref[...] = jnp.zeros_like(dvalue_ref)
        for k in range(count):
            rows = slice(k * tokens, (k + 1) * tokens)
            keys_t = kv_refs[k][:, : kv_heads * HEAD_WIDTH].T
            for g in range(kv_heads):
                cut = slice(g * HEAD_WIDTH, (g + 1) * HEAD_WIDTH)
                value_cut = slice((kv_heads + g) * HEAD_WIDTH, (kv_heads + g + 1) * HEAD_WIDTH)
                key_ref[g, rows, :] = kv_refs[k][:, cut]
                value_ref[g, rows, :] = kv_refs[k][:, value_cut]
                turned_ref[g, :, rows] = keys_t[cut, :]

    group = step // group_blocks
    keys, values, keys_t = key_ref[group], value_ref[group], turned_ref[group]
    d_attn = dot_nt(grad_ref[...], weight_ref[...])
    d_attn_b = d_attn.astype(BF16)
    products = (d_attn * attn_ref[...].astype(F32)).T
    heads = q_ref.shape[1] // HEAD_WIDTH
    d_queries, d_key, d_value = [], None, None
    for h in range(heads):
        cut = slice(h * HEAD_WIDTH, (h + 1) * HEAD_WIDTH)
        query, d_out = q_ref[:, cut], d_attn_b[:, cut]
        delta = jnp.sum(products[cut, :], axis=0, keepdims=True)
        probs = jnp.exp(dot_nt(keys, query) + bias_ref[...] - lse_ref[0, h : h + 1, :])
        d_scores = (probs * (dot_nt(values, d_out) - delta)).astype(BF16)
        value_term = dot_nn(probs.astype(BF16), d_out)
        key_term = dot_nn(d_scores, query)
        d_value = value_term if h == 0 else d_value + value_term
        d_key = key_term if h == 0 else d_key + key_term
        d_queries.append(dot_nn(keys_t, d_scores))
    dkey_ref[group] += d_key
    dvalue_ref[group] += d_value
    d_query = jnp.concatenate(d_queries, axis=0).T * (HEAD_WIDTH**-0.5)
    dq_ref[...] = rotate(d_query, cos_ref[...], -sin_ref[...]).astype(BF16)

    @pl.when(step == pl.num_programs(0) - 1)
    def _():
        for k in range(count):
            rows = slice(k * tokens, (k + 1) * tokens)
            for g in range(kv_heads):
                cut = slice(g * HEAD_WIDTH, (g + 1) * HEAD_WIDTH)
                value_cut = slice((kv_heads + g) * HEAD_WIDTH, (kv_heads + g + 1) * HEAD_WIDTH)
                dkv_refs[k][:, cut] = dkey_ref[g, rows, :].astype(BF16)
                dkv_refs[k][:, value_cut] = dvalue_ref[g, rows, :].astype(BF16)


def attend_back(chain, here, queries, attn_b, lse, grad, output_matrix, tables, kv_pieces):
    tokens, q_width = queries.shape
    count = len(kv_pieces)
    kv_heads = kv_pieces[0].shape[1] // (2 * HEAD_WIDTH)
    width = output_matrix.shape[1]
    block = 256
    blocks = q_width // block
    column = pl.BlockSpec((tokens, block), lambda j, *_: (0, j))
    outs = chain(
        partial(attend_back_kernel, count, kv_heads, blocks // kv_heads),
        [shaped((tokens, q_width), BF16)] + [shaped(p.shape, BF16) for p in kv_pieces],
        here, queries, attn_b, lse, grad, output_matrix, *tables, *kv_pieces,
        grid=(blocks,),
        in_specs=[
            column,
            column,
            pl.BlockSpec((1, block // HEAD_WIDTH, tokens), lambda j, *_: (j, 0, 0)),
            whole((tokens, width)),
            pl.BlockSpec((block, width), lambda j, *_: (j, 0)),
            whole(tables[0].shape),
            whole(tables[1].shape),
        ]
        + [whole(p.shape) for p in kv_pieces],
        us=16.0,
        out_specs=[column] + [whole(p.shape) for p in kv_pieces],
        scratch=[
            pltpu.VMEM((kv_heads, count * tokens, HEAD_WIDTH), BF16),
            pltpu.VMEM((kv_heads, count * tokens, HEAD_WIDTH), BF16),
            pltpu.VMEM((kv_heads, HEAD_WIDTH, count * tokens), BF16),
            pltpu.VMEM((count * tokens, tokens), F32),
            pltpu.VMEM((kv_heads, count * tokens, HEAD_WIDTH), F32),
            pltpu.VMEM((kv_heads, count * tokens, HEAD_WIDTH), F32),
        ],
        scalars=1,
    )
    return outs[0], outs[1:]


def kv_total_kernel(count, *refs):
    cos_ref, sin_ref, out_ref = refs[count:]
    total = refs[0][...].astype(F32)
    for k in range(1, count):
        total += refs[k][...].astype(F32)
    half = total.shape[1] // 2
    out_ref[:, :half] = rotate(total[:, :half], cos_ref[...], -sin_ref[...]).astype(BF16)
    out_ref[:, half:] = total[:, half:].astype(BF16)


def second_norm_kernel(
    here_ref, x_ref, own_ref, other_ref, gain_ref, resid_ref, normed_ref, *share_refs
):
    resid = x_ref[...].astype(F32) + (own_ref[...].astype(F32) + other_ref[...].astype(F32))
    resid_ref[...] = resid
    normed_ref[...] = (resid * rms_of(resid) * gain_ref[...]).astype(BF16)
    write_shares(here_ref[0], normed_ref, share_refs, by_core=True)


def feed_kernel(
    normed_ref, cot_ref, gate_ref, up_ref, down_ref, hidden_ref, d_both_ref
):
    gate = dot_nn(normed_ref[...], gate_ref[...])
    up = dot_nn(normed_ref[...], up_ref[...])
    d_hidden = dot_nt(cot_ref[...], down_ref[...])
    sigmoid = jax.nn.sigmoid(gate)
    active = gate * sigmoid
    hidden_ref[...] = (active * up).astype(BF16)
    d_gate = d_hidden * up * (sigmoid * (1.0 + gate * (1.0 - sigmoid)))
    block = hidden_ref.shape[1]
    d_both_ref[:, :block] = d_gate.astype(BF16)
    d_both_ref[:, block:] = (d_hidden * active).astype(BF16)


def feed_part(chain, normed, cotangent, gate_weight, up_weight, down_weight, first, blocks, block, after=()):
    tokens, width = normed.shape
    column = pl.BlockSpec((width, block), lambda j: (0, first + j))
    return chain(
        feed_kernel,
        [shaped((tokens, blocks * block), BF16), shaped((tokens, 2 * blocks * block), BF16)],
        normed, cotangent, gate_weight, up_weight, down_weight,
        grid=(blocks,),
        in_specs=[
            whole((tokens, width)),
            whole((tokens, width)),
            column,
            column,
            pl.BlockSpec((block, width), lambda j: (first + j, 0)),
        ],
        us=10.0,
        out_specs=[
            pl.BlockSpec((tokens, block), lambda j: (0, j)),
            pl.BlockSpec((tokens, 2 * block), lambda j: (0, j)),
        ],
        after=after,
    )


def part_column(refs, block, visit):
    step, first = pl.program_id(0), 0
    for ref in refs:
        blocks = ref.shape[1] // block
        here = (step >= first) & (step < first + blocks)
        offset = pl.multiple_of((step - first) * block, LANES)
        pl.when(here)(partial(visit, ref, pl.ds(offset, block)))
        first += blocks


def feed_back_kernel(started, block, *refs):
    both_ref, gate_ref, up_ref = refs[:3]
    out_ref, total_ref = refs[-2:]

    @pl.when(pl.program_id(0) == 0)
    def _():
        total_ref[...] = refs[3][...] if started else jnp.zeros_like(total_ref)

    both = both_ref[...]
    total_ref[...] += dot_nt(both[:, :block], gate_ref[...]) + dot_nt(both[:, block:], up_ref[...])

    @pl.when(pl.program_id(0) == pl.num_programs(0) - 1)
    def _():
        out_ref[...] = total_ref[...].astype(out_ref.dtype)


def feed_back(chain, d_both, gate_weight, up_weight, first, block, started, dtype, us, **options):
    tokens, width = d_both.shape[0], gate_weight.shape[0]
    column = pl.BlockSpec((width, block), lambda j: (0, first + j))
    return chain(
        partial(feed_back_kernel, len(started), block),
        shaped((tokens, width), dtype),
        d_both,
        gate_weight,
        up_weight,
        *started,
        grid=(d_both.shape[1] // (2 * block),),
        in_specs=[pl.BlockSpec((tokens, 2 * block), lambda j: (0, j)), column, column]
        + [whole((tokens, width))] * len(started),
        us=us,
        out_specs=whole((tokens, width)),
        scratch=[pltpu.VMEM((tokens, width), F32)],
        **options,
    )


def mixed_kernel(parts, block, *refs):
    hidden_refs = refs[:parts]
    weight_ref, out_ref, total_ref = refs[parts:]

    @pl.when(pl.program_id(0) == 0)
    def _():
        total_ref[...] = jnp.zeros_like(total_ref)

    def visit(ref, columns):
        total_ref[...] += dot_nn(ref[:, columns], weight_ref[...])

    part_column(hidden_refs, block, visit)

    @pl.when(pl.program_id(0) == pl.num_programs(0) - 1)
    def _():
        out_ref[...] = total_ref[...].astype(BF16)


def mix(chain, hidden, down_weight, block):
    tokens, width = hidden[0].shape[0], down_weight.shape[1]
    return chain(
        partial(mixed_kernel, len(hidden), block),
        shaped((tokens, width), BF16),
        *hidden, down_weight,
        grid=(down_weight.shape[0] // block,),
        in_specs=[whole(p.shape) for p in hidden]
        + [pl.BlockSpec((block, width), lambda j: (j, 0))],
        us=8.0,
        out_specs=whole((tokens, width)),
        scratch=[pltpu.VMEM((tokens, width), F32)],
    )


def norm_back(d_normed, inputs, gain):
    scale = rms_of(inputs)
    scaled = d_normed * gain
    back = scale * scaled - inputs * (scale * scale * scale) * jnp.mean(
        scaled * inputs, axis=-1, keepdims=True
    )
    return back, jnp.sum(d_normed * inputs * scale, axis=0, keepdims=True)


def second_back_kernel(
    here_ref,
    cot_ref,
    own_ref,
    other_ref,
    resid_ref,
    gain_ref,
    d_resid_ref,
    rounded_ref,
    gain_grad_ref,
    *share_refs,
):
    d_normed = own_ref[...].astype(F32) + other_ref[...].astype(F32)
    back, gain_grad_ref[...] = norm_back(d_normed, resid_ref[...], gain_ref[...])
    d_resid = cot_ref[...].astype(F32) + back
    d_resid_ref[...] = d_resid
    rounded_ref[...] = d_resid.astype(BF16)
    write_shares(here_ref[0], rounded_ref, share_refs)


def first_back_kernel(dq_ref, dkv_ref, query_ref, key_ref, value_ref, out_ref):
    half = key_ref.shape[1]
    out_ref[...] = (
        dot_nt(dq_ref[...], query_ref[...])
        + dot_nt(dkv_ref[:, :half], key_ref[...])
        + dot_nt(dkv_ref[:, half:], value_ref[...])
    ).astype(BF16)


def output_kernel(resid_ref, own_ref, other_ref, out_ref):
    mixed = own_ref[...].astype(F32) + other_ref[...].astype(F32)
    out_ref[...] = (resid_ref[...] + mixed).astype(BF16)


def last_kernel(own_ref, other_ref, x_ref, gain_ref, d_resid_ref, out_ref, gain_grad_ref):
    d_normed = own_ref[...].astype(F32) + other_ref[...].astype(F32)
    back, gain_grad_ref[...] = norm_back(d_normed, x_ref[...].astype(F32), gain_ref[...])
    out_ref[...] = (d_resid_ref[...] + back).astype(BF16)


def on_device(
    layer_input,
    cotangent,
    attn_gain,
    query_weight,
    key_matrix,
    value_matrix,
    output_matrix,
    feed_gain,
    gate_weight,
    up_weight,
    down_weight,
):
    block_shape = layer_input.shape
    tokens = block_shape[0] * block_shape[1]
    width = block_shape[2]
    x = layer_input.reshape(tokens, width)
    cot = cotangent.reshape(tokens, width)
    q_width, kv_width = query_weight.shape[1], key_matrix.shape[1]
    feed_width = gate_weight.shape[1]
    here = lax.axis_index(CONTEXT).astype(jnp.int32).reshape(1)
    attn_gain, feed_gain = attn_gain.reshape(1, width), feed_gain.reshape(1, width)
    tables = rotary_tables(tokens)
    flat, gain = (tokens, width), (1, width)
    shares = share_shapes(tokens, width)
    share_specs = [whole(s.shape) for s in shares]
    table = whole(tables[0].shape)

    chain = Chain()
    first_normed, kv_own = chain(
        first_norm_kernel,
        [shaped(flat, BF16), shaped((tokens, 2 * kv_width), BF16)],
        x,
        attn_gain,
        key_matrix,
        value_matrix,
        *tables,
        in_specs=[
            whole(flat),
            whole(gain),
            whole(key_matrix.shape),
            whole(value_matrix.shape),
            table,
            table,
        ],
        us=1.5,
        out_specs=[whole(flat), whole((tokens, 2 * kv_width))],
    )
    kv_pieces = exchange_context([kv_own] * lax.axis_size(CONTEXT))
    queries = chain(
        query_kernel,
        shaped((tokens, q_width), BF16),
        first_normed,
        query_weight,
        *tables,
        grid=(q_width // 256,),
        in_specs=[whole(flat), pl.BlockSpec((width, 256), lambda j: (0, j)), table, table],
        us=3.0,
        out_specs=pl.BlockSpec((tokens, 256), lambda j: (0, j)),
    )
    cot_cols = exchange_chips(pick_shares(chain, here, cot))
    attn_b, lse, attn_proj = attend(chain, here, queries, kv_pieces, output_matrix)
    attn_other = swap(attn_proj, "tensor", 1)
    attn_pieces = gather_chips(attn_b)
    first_shares = pick_shares(chain, here, first_normed, after=cot_cols)

    resid, normed_two, *two_shares = chain(
        second_norm_kernel,
        [shaped(flat, F32), shaped(flat, BF16)] + shares,
        here,
        x,
        attn_proj,
        attn_other,
        feed_gain,
        in_specs=[whole(flat)] * 3 + [whole(gain)],
        us=2.0,
        out_specs=[whole(flat)] * 2 + share_specs,
        scalars=1,
    )
    two_cols = exchange_chips(shares_of(normed_two, two_shares, by_core=True))

    block = pick_block(feed_width, 256)
    blocks = feed_width // block
    cut = blocks * 5 // 11
    weights = (gate_weight, up_weight)
    feed = partial(feed_part, chain, normed_two, cot, *weights, down_weight)
    v = {"h1": None}

    def held(name, kernel):
        return [v[name]] if name in v and kernel in HELD[name] else []

    def feed_one():
        v["h1"], v["g1"] = feed(0, cut, block)
        v["h1s"], v["g1s"] = gather_chips(v["h1"]), gather_chips(v["g1"])

    def feed_two():
        v["h2"], v["g2"] = feed(cut, blocks - cut, block, after=two_cols + attn_pieces)

    def feed_back_one():
        outs = feed_back(
            chain,
            v["g1"],
            *weights,
            0,
            block,
            [],
            F32,
            7.0,
            carry=held("h2", "feed_back_one") + held("g2", "feed_back_one"),
        )
        release(outs, "feed_back_one")

    def feed_back_two():
        outs = feed_back(
            chain,
            v["g2"],
            *weights,
            cut,
            block,
            [v["d_two"]],
            BF16,
            8.0,
            carry=held("h2", "feed_back_two") + held("g2", "feed_back_two"),
        )
        release(outs, "feed_back_two")
        v["d_two_other"] = swap(v["d_two"], "tensor", 1)

    def release(outs, kernel):
        outs = list(outs) if isinstance(outs, (list, tuple)) else [outs]
        v["d_two"] = outs.pop(0)
        for name in ("h2", "g2"):
            if held(name, kernel):
                v[name] = outs.pop(0)

    def pieces(name):
        if name + "s" not in v:
            v[name + "s"] = gather_chips(v[name])
        return v[name + "s"]

    def down_one():
        v["D1"] = Ring(chain, *column_products(chain, pieces("h1"), cot_cols))

    def down_two():
        v["D2"] = Ring(chain, *column_products(chain, pieces("h2"), cot_cols))

    def both_one():
        v["both_one"] = row_scatter(chain, two_cols, pieces("g1"))

    def both_two():
        v["both_two"] = row_scatter(chain, two_cols, pieces("g2"))

    def middle():
        v["d_resid"], v["d_resid_b"], v["feed_gain_sum"], *resid_shares = chain(
            second_back_kernel,
            [shaped(flat, F32), shaped(flat, BF16), shaped(gain, F32)] + shares,
            here,
            cot,
            v["d_two"],
            v["d_two_other"],
            resid,
            feed_gain,
            in_specs=[whole(flat)] * 4 + [whole(gain)],
            us=4.0,
            out_specs=[whole(flat)] * 2 + [whole(gain)] + share_specs,
            scalars=1,
        )
        v["resid_cols"] = exchange_chips(shares_of(v["d_resid_b"], resid_shares))

    def heads_back():
        v["d_query"], d_kv_parts = attend_back(
            chain, here, queries, attn_b, lse, v["d_resid_b"], output_matrix, tables, kv_pieces
        )
        v["d_kv_pieces"] = exchange_context(d_kv_parts)
        v["d_querys"] = gather_chips(v["d_query"])

    def kv_total():
        received = v["d_kv_pieces"]
        v["d_kv"] = chain(
            partial(kv_total_kernel, len(received)),
            shaped((tokens, 2 * kv_width), BF16),
            *received,
            *tables,
            in_specs=[whole((tokens, 2 * kv_width))] * len(received) + [table] * 2,
            out_specs=whole((tokens, 2 * kv_width)),
        )
        v["d_kvs"] = gather_chips(v["d_kv"])

    def first_back():
        row_block = pick_block(width, 512)
        v["d_one"] = chain(
            first_back_kernel,
            shaped(flat, BF16),
            v["d_query"],
            v["d_kv"],
            query_weight,
            key_matrix,
            value_matrix,
            grid=(width // row_block,),
            in_specs=[
                whole((tokens, q_width)),
                whole((tokens, 2 * kv_width)),
                pl.BlockSpec((row_block, q_width), lambda j: (j, 0)),
                pl.BlockSpec((row_block, kv_width), lambda j: (j, 0)),
                pl.BlockSpec((row_block, kv_width), lambda j: (j, 0)),
            ],
            us=2.5,
            out_specs=pl.BlockSpec((tokens, row_block), lambda j: (0, j)),
        )
        v["d_one_other"] = swap(v["d_one"], "tensor", 1)

    def first_columns():
        if "first_cols" not in v:
            v["first_cols"] = exchange_chips(first_shares)
        return v["first_cols"]

    def out_product():
        v["O"] = Ring(chain, *column_products(chain, attn_pieces, v["resid_cols"]))

    def query_product():
        v["Q"] = Ring(chain, *row_products(chain, first_columns(), v["d_querys"]))

    def kv_product():
        v["K"] = Ring(chain, *row_products(chain, first_columns(), v["d_kvs"]))

    def mixing():
        v["mixed"] = mix(chain, [v["h1"], v["h2"]], down_weight, block)
        v["mixed_other"] = swap(v["mixed"], "tensor", 1)

    def output():
        v["layer_output"] = chain(
            output_kernel,
            shaped(flat, BF16),
            resid,
            v["mixed"],
            v["mixed_other"],
            in_specs=[whole(flat)] * 3,
            us=2.0,
            out_specs=whole(flat),
        )

    def last():
        v["input_grad"], attn_gain_sum = chain(
            last_kernel,
            [shaped(flat, BF16), shaped(gain, F32)],
            v["d_one"],
            v["d_one_other"],
            x,
            attn_gain,
            v["d_resid"],
            in_specs=[whole(flat)] * 3 + [whole(gain), whole(flat)],
            us=3.0,
            out_specs=[whole(flat), whole(gain)],
        )
        gain_sums = jnp.concatenate([attn_gain_sum, v["feed_gain_sum"]], axis=0)
        v["gains"] = scatter_gains(gain_sums)

    def deal():
        both = [v["both_one"], v["both_two"]]
        share = both[0].shape[0]
        v["gate_share"], v["up_share"] = chain(
            partial(dealt_kernel, block),
            [shaped((share, feed_width), F32)] * 2,
            *both,
            in_specs=[whole(b.shape) for b in both],
            out_specs=[whole((share, feed_width))] * 2,
        )

    tasks = (
        feed_one,
        feed_two,
        feed_back_one,
        feed_back_two,
        down_one,
        down_two,
        both_one,
        both_two,
        middle,
        heads_back,
        kv_total,
        first_back,
        out_product,
        query_product,
        kv_product,
        mixing,
        output,
        last,
        deal,
    )
    by_name = {task.__name__: task for task in tasks}
    for name in ORDER:
        if name in by_name:
            by_name[name]()
        elif v[name].open:
            v[name].step()
    for name in RINGS:
        while v[name].open:
            v[name].step()
    layer_output, input_grad, gains = v["layer_output"], v["input_grad"], v["gains"]
    out_ring, query_ring, kv_ring = v["O"], v["Q"], v["K"]
    gate_share, up_share = v["gate_share"], v["up_share"]
    down_one, down_two = v["D1"], v["D2"]

    return (
        layer_output.reshape(block_shape),
        input_grad.reshape(block_shape),
        gains[0],
        query_ring.result[0],
        kv_ring.result[0][:, :kv_width],
        kv_ring.result[0][:, kv_width:],
        out_ring.result[0],
        gains[1],
        gate_share,
        up_share,
        jnp.concatenate([down_one.result[0], down_two.result[0]], axis=0),
    )


def solution(mesh):
    tensor, dp, context = (mesh.shape[a] for a in ("tensor", "dp", "context"))
    axes = ("tensor", "dp") + CONTEXT
    split = jax.sharding.Mesh(mesh.devices.reshape(tensor, dp, context // 2, 2), axes)
    activation = P(CONTEXT, "dp", None)
    rows, columns = P(None, "tensor"), P("tensor", None)
    vector_share, row_share = P(("dp",) + CONTEXT), P(("dp",) + CONTEXT, "tensor")
    column_share = P("tensor", ("dp",) + CONTEXT)
    in_specs = (activation, activation, P(), rows, rows, rows, columns, P(), rows, rows, columns)
    out_specs = (
        activation,
        activation,
        vector_share,
        row_share,
        row_share,
        row_share,
        column_share,
        vector_share,
        row_share,
        row_share,
        column_share,
    )
    return jax.shard_map(
        on_device, mesh=split, in_specs=in_specs, out_specs=out_specs, check_vma=False
    )
```
